32 devices in a mesh: groups: 2 (over y), seq: 16 (over z, x, core).
Axes of the slice: x: 2, y: 2, z: 4, core: 2. Of those that a mesh axis runs over, the one named last changes fastest.
Arguments:
- queries: bfloat16 [4096, 1536], P(('groups', 'seq')), parts along dimension 0, may hold values from -6 to 6
- keys: bfloat16 [4096, 1536], P(('groups', 'seq')), parts along dimension 0, may hold values from -6 to 6
- values: bfloat16 [4096, 1536], P(('groups', 'seq')), parts along dimension 0, may hold values from -6 to 6
- w_out: bfloat16 [1536, 3072], replicated, may hold values from -0.15625 to 0.15625
- shift_mod: float32 [6144], P('groups'), parts along dimension 0, may hold values from -5 to 5
- scale_mod: float32 [6144], P('groups'), parts along dimension 0, may hold values from -3 to 3
- w_final: bfloat16 [3072, 64], replicated, may hold values from -0.109375 to 0.109375
- conv_weight: bfloat16 [432, 512], replicated, may hold values from -0.3125 to 0.3125
- conv_bias: float32 [512], replicated, may hold values from -3 to 3
Outputs:
- decoded: bfloat16 [8, 32, 64, 512], P('groups', 'seq'), parts along dimension 0
The draws below stay inside these ranges and needn't reach their ends.
There are 2 independent parts, one for each index of `groups`. The reference program is written for one: setup_inputs(seed, part) draws one part's arguments, and reference() takes and returns one part's arrays. A program takes and returns all parts, laid end to end along the dimension named above; an argument that names none is the same for every part. Nothing has to cross between parts.
All inputs are finite; a program needn't handle non-finite values.
Results may differ from the reference program's by a relative error of at most 0.018.
Values may be sent and summed in bfloat16 or wider, within the bound.
No kernel may reach another device: no remote copies, remote signals or barrier semaphores. Data moves between devices by JAX's collectives and lax.ppermute only.
A program may use at most 192 MiB of HBM per device.

```python
import math
import jax
import jax.numpy as jnp
from jax import lax

D = 3072
HEADS = 12
HEAD_DIM = 128
LATENT_CH = 16
CONV_CH = 512
FRAMES = 4
ROWS = 32
TOKENS = 2048


def draw_queries(key, part):
    base = jnp.clip(jax.random.normal(jax.random.fold_in(key, 1), (TOKENS, HEADS * HEAD_DIM), jnp.float32), -6.0, 6.0)
    return base.astype(jnp.bfloat16)


def draw_keys(key, part):
    base = jnp.clip(jax.random.normal(jax.random.fold_in(key, 2), (TOKENS, HEADS * HEAD_DIM), jnp.float32), -6.0, 6.0)
    return base.astype(jnp.bfloat16)


def shard_levels(stream_key, dims, shards, smallest, high):
    factor_of, own = 1.0, jax.random.fold_in(stream_key, 6)
    for dim, blocks in shards:
        steps = jnp.exp(jax.random.uniform(jax.random.fold_in(own, dim), (blocks,), jnp.float32, smallest / len(shards), high / len(shards)))
        factor_of = factor_of * jnp.repeat(steps, dims[dim] // blocks).reshape([-1 if axis == dim else 1 for axis in range(len(dims))])
    return factor_of


def scatter_about(own_key, extent, scale, most, cuts=(), kind=jnp.bfloat16):
    drawn = scale * jax.random.normal(own_key, extent, jnp.float32)
    if cuts:
        drawn = drawn * shard_levels(own_key, extent, cuts, -0.22, 0.18)
    return jnp.clip(drawn, -most, most).astype(kind)


def setup_inputs(seed: int = 0, part: int = 0) -> dict:
    key_of = jax.random.split(jax.random.key(seed), 10)
    part_splits = jax.random.split(jax.random.fold_in(key_of[9], part), 10)
    queries = draw_queries(jax.random.fold_in(jax.random.fold_in(key_of[9], part), 71), part)
    keys = draw_keys(jax.random.fold_in(jax.random.fold_in(key_of[9], part), 71), part)
    values = scatter_about(part_splits[2], (TOKENS, HEADS * HEAD_DIM), 1.0, 6.0, ((0, 16),))
    w_out = scatter_about(key_of[3], (HEADS * HEAD_DIM, D), (HEADS * HEAD_DIM) ** -0.5, 0.15625)
    shift_mod = scatter_about(part_splits[4], (D,), 1.0, 5.0, (), jnp.float32)
    scale_mod = scatter_about(part_splits[5], (D,), 0.5, 3.0, (), jnp.float32)
    w_final = scatter_about(key_of[6], (D, 4 * LATENT_CH), D ** -0.5, 0.109375)
    conv_weight = scatter_about(key_of[7], (27 * LATENT_CH, CONV_CH), (27 * LATENT_CH) ** -0.5, 0.3125)
    conv_bias = scatter_about(key_of[8], (CONV_CH,), 0.5, 3.0, (), jnp.float32)
    return {"queries": queries, "keys": keys, "values": values, "w_out": w_out, "shift_mod": shift_mod, "scale_mod": scale_mod, "w_final": w_final, "conv_weight": conv_weight, "conv_bias": conv_bias}


def convolve(padded, conv_weight, conv_bias, frames, width, height):
    taps = []
    for shift_t in range(3):
        for shift_x in range(3):
            for shift_y in range(3):
                taps.append(padded[shift_t:shift_t + frames, shift_x:shift_x + width, shift_y:shift_y + height, :])
    stacked = jnp.concatenate(taps, axis=3)
    flat = stacked.reshape(frames * width * height, stacked.shape[3])
    output = jnp.dot(flat, conv_weight, preferred_element_type=jnp.float32) + conv_bias
    return output.astype(jnp.bfloat16).reshape(frames, width, height, conv_weight.shape[1])

def reference(queries, keys, values, w_out, shift_mod, scale_mod, w_final, conv_weight, conv_bias):
    tokens = queries.shape[0]
    inv_root = 1.0 / math.sqrt(HEAD_DIM)
    query_heads = queries.astype(jnp.float32).reshape(tokens, HEADS, HEAD_DIM).transpose(1, 0, 2)
    key_heads = keys.astype(jnp.float32).reshape(tokens, HEADS, HEAD_DIM).transpose(1, 0, 2)
    value_heads = values.reshape(tokens, HEADS, HEAD_DIM).transpose(1, 0, 2)
    block_rows = min(2048, tokens)

    def per_head(operands):
        query_h, key_h, value_h = operands

        def per_block(query_b):
            scores = jnp.dot(query_b, key_h.T, precision=lax.Precision.HIGHEST) * inv_root
            peak = lax.optimization_barrier(jnp.max(scores, axis=1, keepdims=True))
            exp_scores = jnp.exp(scores - peak)
            weights = lax.optimization_barrier(exp_scores.astype(jnp.bfloat16))
            summed = jnp.dot(weights, value_h, preferred_element_type=jnp.float32)
            return (summed / lax.optimization_barrier(jnp.sum(exp_scores, axis=1, keepdims=True))).astype(jnp.bfloat16)
        query_blocks = query_h.reshape(tokens // block_rows, block_rows, HEAD_DIM)
        return lax.map(per_block, query_blocks).reshape(tokens, HEAD_DIM)
    attended = lax.map(per_head, (query_heads, key_heads, value_heads))
    attended = attended.transpose(1, 0, 2).reshape(tokens, HEADS * HEAD_DIM)
    projected = jnp.dot(attended, w_out, preferred_element_type=jnp.float32)
    centered = projected - lax.optimization_barrier(jnp.mean(projected, axis=1, keepdims=True))
    variance = lax.optimization_barrier(jnp.mean(centered * centered, axis=1, keepdims=True))
    normed = (centered * lax.rsqrt(variance + 1e-06) * (1.0 + scale_mod) + shift_mod).astype(jnp.bfloat16)
    patches = jnp.dot(normed, w_final, preferred_element_type=jnp.float32).astype(jnp.bfloat16)
    columns = tokens // (FRAMES * ROWS)
    latent = patches.reshape(FRAMES, ROWS, columns, LATENT_CH, 2, 2).transpose(0, 2, 5, 1, 4, 3)
    latent = latent.reshape(FRAMES, 2 * columns, 2 * ROWS, LATENT_CH)
    padded = jnp.pad(latent, ((2, 0), (1, 1), (1, 1), (0, 0)), mode='edge')
    return convolve(padded, conv_weight, conv_bias, FRAMES, 2 * columns, 2 * ROWS)
```

```python
import functools
import math

import jax
import jax.numpy as jnp
from jax import lax
from jax.experimental import pallas as pl
from jax.experimental.pallas import tpu as pltpu
from jax.sharding import Mesh
from jax.sharding import PartitionSpec as P

HEAD_DIM = 128
HEAD_GROUPS = 4
LATENT_CH = 16
FRAMES = 4
ROWS = 32
VMEM_LIMIT = 48 * 1024 * 1024
EXP2_SCALE = math.log2(math.e) / math.sqrt(HEAD_DIM)


def attend_kernel(q_ref, kv_ref, o_ref, *, q_blocks, key_step):
    planes, sources, _, part, _ = kv_ref.shape
    steps = planes // key_step
    keys = key_step * sources * part
    per_block = q_ref.shape[0] // q_blocks
    rows = per_block * part

    def scores_of(query, step):
        key = kv_ref[pl.ds(step * key_step, key_step), :, 0].reshape(keys, HEAD_DIM)
        return lax.dot_general(
            query, key, (((1,), (1,)), ((), ())), preferred_element_type=jnp.float32
        )

    def weighted(weights, step):
        value = kv_ref[pl.ds(step * key_step, key_step), :, 1].reshape(keys, HEAD_DIM)
        return jnp.dot(weights.astype(jnp.bfloat16), value, preferred_element_type=jnp.float32)

    for block in range(q_blocks):
        span = slice(block * per_block, (block + 1) * per_block)
        query = q_ref[span, 0].reshape(rows, HEAD_DIM)
        if steps == 1:
            scores = scores_of(query, 0)
            peak = jnp.max(scores, axis=1, keepdims=True) * EXP2_SCALE
            weights = jnp.exp2(scores * EXP2_SCALE - peak)
            total = jnp.sum(weights, axis=1, keepdims=True)
            summed = weighted(weights, 0)
        else:

            def absorb(step, state):
                peak, total, summed = state
                scores = scores_of(query, step) * EXP2_SCALE
                new_peak = jnp.maximum(peak, jnp.max(scores, axis=1, keepdims=True))
                factor = jnp.exp2(peak - new_peak)
                weights = jnp.exp2(scores - new_peak)
                total = total * factor + jnp.sum(weights, axis=1, keepdims=True)
                return new_peak, total, summed * factor + weighted(weights, step)

            peak, total, summed = lax.fori_loop(
                0,
                steps,
                absorb,
                (
                    jnp.full((rows, 1), -1e30, jnp.float32),
                    jnp.zeros((rows, 1), jnp.float32),
                    jnp.zeros((rows, HEAD_DIM), jnp.float32),
                ),
            )
        out = (summed / total).astype(jnp.bfloat16)
        o_ref[span] = out.reshape(per_block, part, HEAD_DIM)


def attend(queries, keys_values):
    sources, _, part, width = queries.shape
    planes = keys_values.shape[0]
    key_step = math.gcd(planes, 4)
    return pl.pallas_call(
        functools.partial(attend_kernel, q_blocks=2, key_step=key_step),
        grid=(width // HEAD_DIM,),
        in_specs=[
            pl.BlockSpec((sources, 1, part, HEAD_DIM), lambda h: (0, 0, 0, h)),
            pl.BlockSpec((planes, sources, 2, part, HEAD_DIM), lambda h: (0, 0, 0, 0, h)),
        ],
        out_specs=pl.BlockSpec((sources, part, HEAD_DIM), lambda h: (0, 0, h)),
        out_shape=jax.ShapeDtypeStruct((sources, part, width), jnp.bfloat16),
        compiler_params=pltpu.CompilerParams(vmem_limit_bytes=VMEM_LIMIT),
    )(queries, keys_values)


def final_kernel(o_ref, w_ref, scale_ref, shift_ref, w_final_ref, out_ref, projected, *, columns):
    step = pl.program_id(0)
    groups, _, width = o_ref.shape
    tile = w_ref.shape[1]
    acc = None
    for group in range(groups):
        part = jnp.dot(
            o_ref[group],
            w_ref[group * width : (group + 1) * width, :],
            preferred_element_type=jnp.float32,
        )
        acc = part if acc is None else acc + part
    projected[step] = acc

    @pl.when(step == pl.num_programs(0) - 1)
    def _():
        steps = projected.shape[0]
        tokens = projected.shape[1]
        features = steps * tile
        total = projected[0]
        for i in range(1, steps):
            total = total + projected[i]
        mean = jnp.sum(total, axis=1, keepdims=True) * (1.0 / features)
        squares = None
        for i in range(steps):
            centered = projected[i] - mean
            squares = centered * centered if squares is None else squares + centered * centered
        variance = jnp.sum(squares, axis=1, keepdims=True) * (1.0 / features)
        inverse = lax.rsqrt(variance + 1e-06)
        patches = None
        for i in range(steps):
            lanes = slice(i * tile, (i + 1) * tile)
            normed = (projected[i] - mean) * inverse * (1.0 + scale_ref[:, lanes]) + shift_ref[:, lanes]
            part = jnp.dot(
                normed.astype(jnp.bfloat16), w_final_ref[lanes, :], preferred_element_type=jnp.float32
            )
            patches = part if patches is None else patches + part
        half = patches.shape[1] // 2
        own = patches[:, :half]
        edge = patches[:, half:]
        lane = lax.broadcasted_iota(jnp.int32, own.shape, 1)
        column = lax.broadcasted_iota(jnp.int32, own.shape, 0) % columns
        from_left = jnp.where(column == 0, edge, pltpu.roll(own, 1, 0))
        from_right = jnp.where(column == columns - 1, edge, pltpu.roll(own, tokens - 1, 0))
        cells = jnp.where(
            lane < half // 4, from_left, jnp.where(lane >= 3 * (half // 4), from_right, own)
        )
        out_ref[...] = cells.astype(jnp.bfloat16)


def final_layer(attended, w_out, scale_mod, shift_mod, w_final, columns):
    groups, tokens, width = attended.shape
    inner, features = w_out.shape
    tile = 512
    steps = features // tile
    by_cell = w_final.reshape(features, LATENT_CH, 2, 2).transpose(0, 3, 2, 1)
    by_cell = by_cell.reshape(features, 2, 2 * LATENT_CH)
    order = jnp.concatenate([by_cell[:, i] for i in (1, 0, 1, 0, 0, 0, 1, 1)], axis=1)
    lanes = order.shape[1]
    return pl.pallas_call(
        functools.partial(final_kernel, columns=columns),
        grid=(steps,),
        in_specs=[
            pl.BlockSpec((groups, tokens, width), lambda i: (0, 0, 0)),
            pl.BlockSpec((inner, tile), lambda i: (0, i)),
            pl.BlockSpec((1, features), lambda i: (0, 0)),
            pl.BlockSpec((1, features), lambda i: (0, 0)),
            pl.BlockSpec((features, lanes), lambda i: (0, 0)),
        ],
        out_specs=pl.BlockSpec((tokens, lanes // 2), lambda i: (0, 0)),
        out_shape=jax.ShapeDtypeStruct((tokens, lanes // 2), jnp.bfloat16),
        scratch_shapes=[pltpu.VMEM((steps, tokens, tile), jnp.float32)],
        compiler_params=pltpu.CompilerParams(vmem_limit_bytes=VMEM_LIMIT),
    )(attended, w_out, scale_mod[None], shift_mod[None], order)


def convolve_kernel(cells_ref, w_ref, bias_ref, out_ref, latent):
    frames, rows, _ = cells_ref.shape
    cols = latent.shape[1]
    height = 2 * rows
    ch = LATENT_CH
    for f in range(frames):
        cells = cells_ref[f].astype(jnp.float32)
        for x in range(cols):
            for p in range(2):
                lane = (2 * x + p) * ch
                latent[f, x, pl.ds(8 + p, rows, stride=2), :] = cells[:, lane : lane + ch]
            latent[f, x, 7:8, :] = cells[:1, 2 * x * ch : (2 * x + 1) * ch]
            latent[f, x, 8 + height : 9 + height, :] = cells[rows - 1 :, (2 * x + 1) * ch : (2 * x + 2) * ch]
    depth = 9 * ch
    for x in range(cols - 2):
        stacked = []
        for f in range(frames):
            taps = [latent[f, x + b, 7 + e : 7 + e + height, :] for b in range(3) for e in range(3)]
            stacked.append(jnp.concatenate(taps, axis=1).astype(jnp.bfloat16))
        stacked = [stacked[0]] * 2 + stacked
        acc = None
        for a in range(3):
            flat = jnp.concatenate(stacked[a : a + frames], axis=0)
            part = jnp.dot(
                flat, w_ref[a * depth : (a + 1) * depth, :], preferred_element_type=jnp.float32
            )
            acc = part if acc is None else acc + part
        acc = (acc + bias_ref[...]).astype(jnp.bfloat16)
        out_ref[:, x] = acc.reshape(frames, height, acc.shape[1])


def convolve(cells, conv_weight, conv_bias):
    frames, rows, lanes = cells.shape
    cols = lanes // (2 * LATENT_CH)
    channels = conv_weight.shape[1]
    return pl.pallas_call(
        convolve_kernel,
        out_shape=jax.ShapeDtypeStruct((frames, cols - 2, 2 * rows, channels), jnp.bfloat16),
        scratch_shapes=[pltpu.VMEM((frames, cols, 2 * rows + 16, LATENT_CH), jnp.float32)],
        compiler_params=pltpu.CompilerParams(vmem_limit_bytes=VMEM_LIMIT),
    )(cells, conv_weight, conv_bias[None])


def shards(queries, keys, values, w_out, shift_mod, scale_mod, w_final, conv_weight, conv_bias):
    heads = lax.axis_size("heads")
    devices = heads * lax.axis_size("plane")
    tokens, width = queries.shape
    group_width = width // heads
    columns = devices
    pieces = jnp.stack([queries, keys, values]).reshape(3, tokens, heads, group_width)
    pieces = pieces.transpose(2, 0, 1, 3)
    got = lax.all_to_all(pieces, "heads", split_axis=0, concat_axis=0, tiled=True)
    keys_values = lax.all_gather(got[:, 1:], "plane")
    result = attend(got[:, :1], keys_values)
    returned = lax.all_to_all(result, "heads", split_axis=0, concat_axis=0, tiled=True)
    cells = final_layer(returned, w_out, scale_mod, shift_mod, w_final, columns)
    rows_dev = tokens // columns
    laid = cells.reshape(rows_dev, columns, cells.shape[1])
    tile = lax.all_to_all(laid, ("heads", "plane"), split_axis=1, concat_axis=0, tiled=True)
    tile = tile.reshape(FRAMES, ROWS, cells.shape[1])
    return convolve(tile, conv_weight, conv_bias)


def solution(mesh):
    groups, seq = mesh.devices.shape
    split = Mesh(
        mesh.devices.reshape(groups, HEAD_GROUPS, seq // HEAD_GROUPS), ("groups", "heads", "plane")
    )
    by_token = P(("groups", "heads", "plane"), None)
    placed = (by_token, by_token, by_token, P(), P("groups"), P("groups"), P(), P(), P())
    return jax.shard_map(
        shards,
        mesh=split,
        in_specs=placed,
        out_specs=P("groups", ("heads", "plane"), None, None),
        check_vma=False,
    )
```

```python
import functools
import math

import jax
import jax.numpy as jnp
from jax import lax
from jax.experimental import pallas as pl
from jax.experimental.pallas import tpu as pltpu
from jax.sharding import Mesh
from jax.sharding import PartitionSpec as P

HEAD_DIM = 128
HEAD_GROUPS = 4
LATENT_CH = 16
FRAMES = 4
VMEM_LIMIT = 56 * 1024 * 1024
EXP2_SCALE = math.log2(math.e) / math.sqrt(HEAD_DIM)
EARLY, LATE = (1, 0), (2, 3)


def swap(source, axis, distance):
    count = lax.axis_size(axis)
    return lax.ppermute(source, axis, [(i, i ^ distance) for i in range(count)])


def attend_kernel(*refs, sources, parts, targets, rows_step):
    q_refs = refs[:sources]
    kv_refs = refs[sources : sources + parts]
    o_refs = refs[sources + parts :]
    keys = [r[:, :, 0].reshape(-1, HEAD_DIM) for r in kv_refs]
    values = [r[:, :, 1].reshape(-1, HEAD_DIM) for r in kv_refs]
    rows = q_refs[0].shape[1]
    for first in range(0, len(targets), rows_step):
        block = range(first, min(first + rows_step, len(targets)))
        query = jnp.concatenate([q[targets[i]] for i in block for q in q_refs], axis=0)
        scores = [
            lax.dot_general(query, k, (((1,), (1,)), ((), ())), preferred_element_type=jnp.float32)
            for k in keys
        ]
        peak = functools.reduce(
            jnp.maximum, [jnp.max(s, axis=1, keepdims=True) for s in scores]
        )
        peak = peak * EXP2_SCALE
        total = summed = None
        for s, v in zip(scores, values):
            weights = jnp.exp2(s * EXP2_SCALE - peak)
            part_total = jnp.sum(weights, axis=1, keepdims=True)
            part = jnp.dot(weights.astype(jnp.bfloat16), v, preferred_element_type=jnp.float32)
            total = part_total if total is None else total + part_total
            summed = part if summed is None else summed + part
        out = (summed / total).astype(jnp.bfloat16)
        for n, i in enumerate(block):
            for r in range(sources):
                at = (n * sources + r) * rows
                o_refs[i][targets[i] ^ r] = out[at : at + rows]


def attend(queries, keys_values, targets):
    sources, rows, width = queries[0].shape
    key_count = sum(math.prod(kv.shape[:2]) * kv.shape[3] for kv in keys_values)
    result = jax.ShapeDtypeStruct((sources, rows, width), jnp.bfloat16)
    kv_block = keys_values[0].shape[:-1] + (HEAD_DIM,)
    return pl.pallas_call(
        functools.partial(
            attend_kernel,
            sources=sources,
            parts=len(keys_values),
            targets=targets,
            rows_step=2 if key_count <= 4096 else 1,
        ),
        grid=(width // HEAD_DIM,),
        in_specs=[pl.BlockSpec((sources, rows, HEAD_DIM), lambda h: (0, 0, h))] * sources
        + [pl.BlockSpec(kv_block, lambda h: (0, 0, 0, 0, h))] * len(keys_values),
        out_specs=[pl.BlockSpec((sources, rows, HEAD_DIM), lambda h: (0, 0, h))] * len(targets),
        out_shape=[result] * len(targets),
        compiler_params=pltpu.CompilerParams(vmem_limit_bytes=VMEM_LIMIT),
    )(*queries, *keys_values)


def final_kernel(where_ref, *refs, groups, planes, rows_dev):
    o_refs = refs[:groups]
    w_ref, scale_ref, shift_ref, w_final_ref, even_ref, odd_ref, projected = refs[groups:]
    step = pl.program_id(0)
    heads_at, plane_at = where_ref[0], where_ref[1]
    tokens = projected.shape[1]
    width = o_refs[0].shape[2]
    tile = w_ref.shape[1]
    acc = None
    for t in range(groups):
        rows = pl.ds(pl.multiple_of((heads_at ^ t) * width, 128), width)
        part = jnp.dot(
            o_refs[t][...].reshape(tokens, width), w_ref[rows, :], preferred_element_type=jnp.float32
        )
        acc = part if acc is None else acc + part
    projected[step] = acc

    @pl.when(step == pl.num_programs(0) - 1)
    def _():
        steps = projected.shape[0]
        features = steps * tile
        total = projected[0]
        for i in range(1, steps):
            total = total + projected[i]
        mean = jnp.sum(total, axis=1, keepdims=True) * (1.0 / features)
        squares = None
        for i in range(steps):
            centered = projected[i] - mean
            squares = centered * centered if squares is None else squares + centered * centered
        variance = jnp.sum(squares, axis=1, keepdims=True) * (1.0 / features)
        inverse = lax.rsqrt(variance + 1e-06)
        patches = None
        for i in range(steps):
            lanes = slice(i * tile, (i + 1) * tile)
            normed = (projected[i] - mean) * inverse * (1.0 + scale_ref[:, lanes]) + shift_ref[:, lanes]
            part = jnp.dot(
                normed.astype(jnp.bfloat16), w_final_ref[lanes, :], preferred_element_type=jnp.float32
            )
            patches = part if patches is None else patches + part
        patches = patches.astype(jnp.bfloat16)
        channels = patches.shape[1]
        half = channels // 2
        source = lax.broadcasted_iota(jnp.int32, (channels, channels), 0)
        target = lax.broadcasted_iota(jnp.int32, (channels, channels), 1)
        q, p, c = target // half, (target // LATENT_CH) % 2, target % LATENT_CH
        lane_order = (source == 4 * c + 2 * p + q).astype(jnp.bfloat16)
        to = lax.broadcasted_iota(jnp.int32, (tokens, tokens), 0)
        at = lax.broadcasted_iota(jnp.int32, (tokens, tokens), 1)
        share = planes * rows_dev
        place = ((to // share) ^ heads_at) * share
        place = place + (((to % share) // rows_dev) ^ plane_at) * rows_dev + to % rows_dev
        row_order = (at == place).astype(jnp.bfloat16)
        cells = jnp.dot(patches, lane_order, preferred_element_type=jnp.float32)
        cells = jnp.dot(row_order, cells.astype(jnp.bfloat16), preferred_element_type=jnp.float32)
        cells = cells.astype(jnp.bfloat16)
        even_ref[...] = cells[:, :half]
        odd_ref[...] = cells[:, half:]


def final_layer(where, attended, w_out, scale_mod, shift_mod, w_final, rows_dev, planes):
    groups = len(attended)
    sources, rows, width = attended[0].shape
    tokens = sources * rows
    inner, features = w_out.shape
    channels = w_final.shape[1]
    tile = 512
    steps = features // tile
    whole = lambda shape: pl.BlockSpec(shape, lambda i, *_: (0,) * len(shape))
    result = jax.ShapeDtypeStruct((tokens, channels // 2), jnp.bfloat16)
    return pl.pallas_call(
        functools.partial(final_kernel, groups=groups, planes=planes, rows_dev=rows_dev),
        grid_spec=pltpu.PrefetchScalarGridSpec(
            num_scalar_prefetch=1,
            grid=(steps,),
            in_specs=[whole((sources, rows, width))] * groups
            + [
                pl.BlockSpec((inner, tile), lambda i, *_: (0, i)),
                whole((1, features)),
                whole((1, features)),
                whole((features, channels)),
            ],
            out_specs=[whole((tokens, channels // 2))] * 2,
            scratch_shapes=[pltpu.VMEM((steps, tokens, tile), jnp.float32)],
        ),
        out_shape=[result] * 2,
        compiler_params=pltpu.CompilerParams(vmem_limit_bytes=VMEM_LIMIT),
    )(where, *attended, w_out, scale_mod[None], shift_mod[None], w_final)


def convolve_kernel(where_ref, even_ref, odd_ref, left_ref, right_ref, w_ref, bias_ref, out_ref, latent):
    frames, cols, _, ch = latent.shape
    rows = even_ref.shape[0] // frames
    height = 2 * rows
    even = even_ref[...].astype(jnp.float32)
    odd = odd_ref[...].astype(jnp.float32)
    left = jnp.where(where_ref[0] == 0, even, left_ref[...].astype(jnp.float32))
    right = jnp.where(where_ref[0] == where_ref[1] - 1, odd, right_ref[...].astype(jnp.float32))
    for x, cells in enumerate((left, even, odd, right)):
        for f in range(frames):
            own = cells[f * rows : (f + 1) * rows]
            for p in range(2):
                latent[f, x, pl.ds(8 + p, rows, stride=2), :] = own[:, p * ch : (p + 1) * ch]
            latent[f, x, 7:8, :] = own[:1, :ch]
            latent[f, x, 8 + height : 9 + height, :] = own[rows - 1 :, ch:]
    depth = 9 * ch
    for x in range(cols - 2):
        stacked = []
        for f in range(frames):
            taps = [latent[f, x + b, 7 + e : 7 + e + height, :] for b in range(3) for e in range(3)]
            stacked.append(jnp.concatenate(taps, axis=1).astype(jnp.bfloat16))
        stacked = [stacked[0]] * 2 + stacked
        acc = None
        for a in range(3):
            flat = jnp.concatenate(stacked[a : a + frames], axis=0)
            part = jnp.dot(
                flat, w_ref[a * depth : (a + 1) * depth, :], preferred_element_type=jnp.float32
            )
            acc = part if acc is None else acc + part
        acc = (acc + bias_ref[...]).astype(jnp.bfloat16)
        out_ref[:, x] = acc.reshape(frames, height, acc.shape[1])


def convolve(where, even, odd, left, right, conv_weight, conv_bias):
    rows = even.shape[0] // FRAMES
    channels = conv_weight.shape[1]
    smem = pl.BlockSpec(memory_space=pltpu.SMEM)
    vmem = pl.BlockSpec(memory_space=pltpu.VMEM)
    return pl.pallas_call(
        convolve_kernel,
        in_specs=[smem] + [vmem] * 6,
        out_specs=vmem,
        out_shape=jax.ShapeDtypeStruct((FRAMES, 2, 2 * rows, channels), jnp.bfloat16),
        scratch_shapes=[pltpu.VMEM((FRAMES, 4, 2 * rows + 16, LATENT_CH), jnp.float32)],
        compiler_params=pltpu.CompilerParams(vmem_limit_bytes=VMEM_LIMIT),
    )(where, even, odd, left, right, conv_weight, conv_bias[None])


def gather_plane(batch):
    planes = lax.axis_size("plane")
    same = [batch] + [swap(batch, "plane", d) for d in range(2, planes, 2)]
    same = jnp.concatenate(same, axis=0)
    return [same, swap(same, "plane", 1)]


def shards(queries, keys, values, w_out, shift_mod, scale_mod, w_final, conv_weight, conv_bias):
    groups = lax.axis_size("heads")
    planes = lax.axis_size("plane")
    heads_at = lax.axis_index("heads")
    plane_at = lax.axis_index("plane")
    devices = groups * planes
    tokens, width = queries.shape
    group_width = width // groups
    rows_dev = tokens // devices

    def group_of(source, r):
        return lax.dynamic_slice_in_dim(source, (heads_at ^ r) * group_width, group_width, axis=1)

    piece = [jnp.stack([group_of(keys, r), group_of(values, r)]) for r in range(groups)]
    got = [piece[0]] + [swap(piece[r], "heads", r) for r in range(1, groups)]

    to = lax.broadcasted_iota(jnp.int32, (tokens, tokens), 0)
    at = lax.broadcasted_iota(jnp.int32, (tokens, tokens), 1)
    j, u, row = to // (groups * rows_dev), (to // rows_dev) % groups, to % rows_dev
    place = row * devices + (u ^ heads_at) * planes + (j ^ plane_at)
    mixed = jnp.concatenate([group_of(queries, r) for r in range(groups)], axis=1)
    mixed = jnp.dot((at == place).astype(jnp.bfloat16), mixed, preferred_element_type=jnp.float32)
    mixed = mixed.astype(jnp.bfloat16).reshape(planes, groups, rows_dev, width)
    in_plane = jnp.stack([mixed[0]] + [swap(mixed[d], "plane", d) for d in range(1, planes)], axis=1)
    in_plane = in_plane.reshape(groups, planes * rows_dev, width)

    early = gather_plane(jnp.stack([got[r] for r in EARLY]))
    late = gather_plane(jnp.stack([got[r] for r in LATE]))
    keys_values = [kv.reshape((-1, 2) + kv.shape[1:]) for kv in early + late]

    asked = []
    for r in range(groups):
        lanes = slice(r * group_width, (r + 1) * group_width)
        own = jnp.stack([in_plane[r ^ t, :, lanes] for t in range(groups)])
        asked.append(own if r == 0 else swap(own, "heads", r))

    attended = [None] * groups
    for targets in (LATE, EARLY):
        for t, result in zip(targets, attend(asked, keys_values, targets)):
            attended[t] = result if t == 0 else swap(result, "heads", t)

    where = jnp.stack([heads_at, plane_at]).astype(jnp.int32)
    even, odd = final_layer(where, attended, w_out, scale_mod, shift_mod, w_final, rows_dev, planes)
    both = ("heads", "plane")
    left = lax.ppermute(odd, both, [(i, i + 1) for i in range(devices - 1)])
    right = lax.ppermute(even, both, [(i + 1, i) for i in range(devices - 1)])
    spot = jnp.stack([heads_at * planes + plane_at, jnp.int32(devices)]).astype(jnp.int32)
    return convolve(spot, even, odd, left, right, conv_weight, conv_bias)


def solution(mesh):
    groups, seq = mesh.devices.shape
    split = Mesh(
        mesh.devices.reshape(groups, HEAD_GROUPS, seq // HEAD_GROUPS), ("groups", "heads", "plane")
    )
    by_token = P(("groups", "heads", "plane"), None)
    placed = (by_token, by_token, by_token, P(), P("groups"), P("groups"), P(), P(), P())
    return jax.shard_map(
        shards,
        mesh=split,
        in_specs=placed,
        out_specs=P("groups", ("heads", "plane"), None, None),
        check_vma=False,
    )
```

```python
import functools
import math

import jax
import jax.numpy as jnp
from jax import lax
from jax.experimental import pallas as pl
from jax.experimental.pallas import tpu as pltpu
from jax.sharding import Mesh
from jax.sharding import PartitionSpec as P

HEAD_DIM = 128
HEAD_GROUPS = 4
LATENT_CH = 16
FRAMES = 4
VMEM_LIMIT = 16 * 1024 * 1024
EXP2_SCALE = math.log2(math.e) / math.sqrt(HEAD_DIM)


def swap(source, axis, distance):
    count = lax.axis_size(axis)
    return lax.ppermute(source, axis, [(i, i ^ distance) for i in range(count)])


def attend_kernel(*refs, sources, parts, targets, rows_step):
    q_refs = refs[:sources]
    kv_refs = refs[sources : sources + parts]
    o_refs = refs[sources + parts :]
    rows, width = q_refs[0].shape[1:]
    key_rows = [r.shape[0] * r.shape[2] for r in kv_refs]
    works = [
        (h, range(first, min(first + rows_step, len(targets))))
        for h in range(width // HEAD_DIM)
        for first in range(0, len(targets), rows_step)
    ]

    def lanes(h):
        return slice(h * HEAD_DIM, (h + 1) * HEAD_DIM)

    def scores_of(work):
        h, block = work
        query = jnp.concatenate([q[targets[i], :, lanes(h)] for i in block for q in q_refs], axis=0)
        return [
            lax.dot_general(
                query,
                kv[:, 0, :, lanes(h)].reshape(count, HEAD_DIM),
                (((1,), (1,)), ((), ())),
                preferred_element_type=jnp.float32,
            )
            for kv, count in zip(kv_refs, key_rows)
        ]

    def finish(work, scores):
        h, block = work
        peak = functools.reduce(jnp.maximum, [jnp.max(s, axis=1, keepdims=True) for s in scores])
        peak = peak * EXP2_SCALE
        summed = None
        for s, kv, count in zip(scores, kv_refs, key_rows):
            weights = jnp.exp2(s * EXP2_SCALE - peak).astype(jnp.bfloat16)
            value = kv[:, 1, :, lanes(h)].reshape(count, HEAD_DIM)
            value = jnp.concatenate([value, jnp.ones_like(value)], axis=1)
            part = jnp.dot(weights, value, preferred_element_type=jnp.float32)
            summed = part if summed is None else summed + part
        out = (summed[:, :HEAD_DIM] / summed[:, HEAD_DIM:]).astype(jnp.bfloat16)
        for n, i in enumerate(block):
            for r in range(sources):
                at = (n * sources + r) * rows
                o_refs[i][targets[i] ^ r, :, lanes(h)] = out[at : at + rows]

    scores = scores_of(works[0])
    for n, work in enumerate(works):
        following = scores_of(works[n + 1]) if n + 1 < len(works) else None
        finish(work, scores)
        scores = following


def attend(queries, keys_values, targets):
    sources, rows, width = queries[0].shape
    key_count = sum(kv.shape[0] * kv.shape[2] for kv in keys_values)
    small = key_count <= 4096
    rows_step, step_width = (2, width) if small else (1, HEAD_DIM)
    score_bytes = rows_step * sources * rows * key_count * 4
    limit = 8 * key_count * step_width + 3 * score_bytes + 6 * 1024 * 1024
    q_spec = pl.BlockSpec((sources, rows, step_width), lambda h: (0, 0, h))
    return pl.pallas_call(
        functools.partial(
            attend_kernel,
            sources=sources,
            parts=len(keys_values),
            targets=targets,
            rows_step=rows_step,
        ),
        grid=(width // step_width,),
        in_specs=[q_spec] * sources
        + [
            pl.BlockSpec(kv.shape[:-1] + (step_width,), lambda h: (0, 0, 0, h))
            for kv in keys_values
        ],
        out_specs=[q_spec] * len(targets),
        out_shape=[jax.ShapeDtypeStruct((sources, rows, width), jnp.bfloat16)] * len(targets),
        compiler_params=pltpu.CompilerParams(vmem_limit_bytes=min(limit, 60 * 1024 * 1024)),
    )(*queries, *keys_values)


def project_kernel(where_ref, *refs, targets):
    o_refs = refs[: len(targets)]
    w_ref, out_ref, lined = refs[len(targets) :]
    width = o_refs[0].shape[2]
    tokens = lined.shape[0]
    for n in range(len(targets)):
        lined[:, n * width : (n + 1) * width] = o_refs[n][...].reshape(tokens, width)
    rows = [pl.ds(pl.multiple_of((where_ref[0] ^ t) * width, 128), width) for t in targets]
    weights = jnp.concatenate([w_ref[r, :] for r in rows], axis=0)
    out_ref[...] = jnp.dot(lined[...], weights, preferred_element_type=jnp.float32)


def project(where, attended, targets, w_out, tile):
    sources, rows, width = attended[0].shape
    tokens = sources * rows
    inner, features = w_out.shape
    return pl.pallas_call(
        functools.partial(project_kernel, targets=targets),
        grid_spec=pltpu.PrefetchScalarGridSpec(
            num_scalar_prefetch=1,
            grid=(features // tile,),
            in_specs=[pl.BlockSpec((sources, rows, width), lambda i, *_: (0, 0, 0))] * len(targets)
            + [pl.BlockSpec((inner, tile), lambda i, *_: (0, i))],
            out_specs=pl.BlockSpec((None, tokens, tile), lambda i, *_: (i, 0, 0)),
            scratch_shapes=[pltpu.VMEM((tokens, len(targets) * width), jnp.bfloat16)],
        ),
        out_shape=jax.ShapeDtypeStruct((features // tile, tokens, tile), jnp.float32),
        compiler_params=pltpu.CompilerParams(vmem_limit_bytes=VMEM_LIMIT),
    )(where, *attended, w_out)


def final_kernel(where_ref, *refs, targets, planes, rows_dev):
    o_refs = refs[: len(targets)]
    partial_ref, w_ref, scale_ref, shift_ref, w_final_ref, even_ref, odd_ref, lined, projected = refs[
        len(targets) :
    ]
    step = pl.program_id(0)
    heads_at, plane_at = where_ref[0], where_ref[1]
    tokens = lined.shape[0]
    width = o_refs[0].shape[2]
    tile = w_ref.shape[1]
    for n in range(len(targets)):
        lined[:, n * width : (n + 1) * width] = o_refs[n][...].reshape(tokens, width)
    rows = [pl.ds(pl.multiple_of((heads_at ^ t) * width, 128), width) for t in targets]
    weights = jnp.concatenate([w_ref[r, :] for r in rows], axis=0)
    projected[step] = partial_ref[...] + jnp.dot(
        lined[...], weights, preferred_element_type=jnp.float32
    )

    @pl.when(step == pl.num_programs(0) - 1)
    def _():
        steps = projected.shape[0]
        features = steps * tile
        total = projected[0]
        for i in range(1, steps):
            total = total + projected[i]
        mean = jnp.sum(total, axis=1, keepdims=True) * (1.0 / features)
        squares = None
        for i in range(steps):
            centered = projected[i] - mean
            squares = centered * centered if squares is None else squares + centered * centered
        variance = jnp.sum(squares, axis=1, keepdims=True) * (1.0 / features)
        inverse = lax.rsqrt(variance + 1e-06)
        patches = None
        for i in range(steps):
            lanes = slice(i * tile, (i + 1) * tile)
            normed = (projected[i] - mean) * inverse * (1.0 + scale_ref[:, lanes]) + shift_ref[:, lanes]
            part = lax.dot_general(
                normed.astype(jnp.bfloat16),
                w_final_ref[:, lanes],
                (((1,), (1,)), ((), ())),
                preferred_element_type=jnp.float32,
            )
            patches = part if patches is None else patches + part
        patches = patches.astype(jnp.bfloat16)
        channels = patches.shape[1]
        half = channels // 2
        source = lax.broadcasted_iota(jnp.int32, (channels, channels), 0)
        target = lax.broadcasted_iota(jnp.int32, (channels, channels), 1)
        q, p, c = target // half, (target // LATENT_CH) % 2, target % LATENT_CH
        lane_order = (source == 4 * c + 2 * p + q).astype(jnp.bfloat16)
        to = lax.broadcasted_iota(jnp.int32, (tokens, tokens), 0)
        at = lax.broadcasted_iota(jnp.int32, (tokens, tokens), 1)
        share = planes * rows_dev
        place = ((to // share) ^ heads_at) * share
        place = place + (((to % share) // rows_dev) ^ plane_at) * rows_dev + to % rows_dev
        row_order = (at == place).astype(jnp.bfloat16)
        cells = jnp.dot(patches, lane_order, preferred_element_type=jnp.float32)
        cells = jnp.dot(row_order, cells.astype(jnp.bfloat16), preferred_element_type=jnp.float32)
        cells = cells.astype(jnp.bfloat16)
        even_ref[...] = cells[:, :half]
        odd_ref[...] = cells[:, half:]


def final_layer(where, attended, targets, partial, w_out, scale_mod, shift_mod, w_final, rows_dev, planes):
    sources, rows, width = attended[0].shape
    inner, features = w_out.shape
    steps, tokens, tile = partial.shape
    channels = w_final.shape[1]
    whole = lambda shape: pl.BlockSpec(shape, lambda i, *_: (0,) * len(shape))
    result = jax.ShapeDtypeStruct((tokens, channels // 2), jnp.bfloat16)
    return pl.pallas_call(
        functools.partial(final_kernel, targets=targets, planes=planes, rows_dev=rows_dev),
        grid_spec=pltpu.PrefetchScalarGridSpec(
            num_scalar_prefetch=1,
            grid=(steps,),
            in_specs=[whole((sources, rows, width))] * len(targets)
            + [
                pl.BlockSpec((None, tokens, tile), lambda i, *_: (i, 0, 0)),
                pl.BlockSpec((inner, tile), lambda i, *_: (0, i)),
                whole((1, features)),
                whole((1, features)),
                whole((channels, features)),
            ],
            out_specs=[whole((tokens, channels // 2))] * 2,
            scratch_shapes=[
                pltpu.VMEM((tokens, len(targets) * width), jnp.bfloat16),
                pltpu.VMEM((steps, tokens, tile), jnp.float32),
            ],
        ),
        out_shape=[result] * 2,
        compiler_params=pltpu.CompilerParams(vmem_limit_bytes=VMEM_LIMIT),
    )(where, *attended, partial, w_out, scale_mod[None], shift_mod[None], w_final.T)


def convolve_kernel(where_ref, even_ref, odd_ref, left_ref, right_ref, w_ref, bias_ref, out_ref, latent):
    frames, cols, _, ch = latent.shape
    rows = even_ref.shape[0] // frames
    height = 2 * rows
    even = even_ref[...].astype(jnp.float32)
    odd = odd_ref[...].astype(jnp.float32)
    left = jnp.where(where_ref[2] == 0, even, left_ref[...].astype(jnp.float32))
    right = jnp.where(where_ref[2] == where_ref[3] - 1, odd, right_ref[...].astype(jnp.float32))
    for x, cells in enumerate((left, even, odd, right)):
        for f in range(frames):
            own = cells[f * rows : (f + 1) * rows]
            for p in range(2):
                latent[f, x, pl.ds(8 + p, rows, stride=2), :] = own[:, p * ch : (p + 1) * ch]
            latent[f, x, 7:8, :] = own[:1, :ch]
            latent[f, x, 8 + height : 9 + height, :] = own[rows - 1 :, ch:]
    depth = 9 * ch
    for x in range(cols - 2):
        stacked = []
        for f in range(frames):
            taps = [latent[f, x + b, 7 + e : 7 + e + height, :] for b in range(3) for e in range(3)]
            stacked.append(jnp.concatenate(taps, axis=1).astype(jnp.bfloat16))
        stacked = [stacked[0]] * 2 + stacked
        acc = None
        for a in range(3):
            flat = jnp.concatenate(stacked[a : a + frames], axis=0)
            part = jnp.dot(
                flat, w_ref[a * depth : (a + 1) * depth, :], preferred_element_type=jnp.float32
            )
            acc = part if acc is None else acc + part
        acc = (acc + bias_ref[...]).astype(jnp.bfloat16)
        out_ref[:, x] = acc.reshape(frames, height, acc.shape[1])


def convolve(where, even, odd, left, right, conv_weight, conv_bias):
    rows = even.shape[0] // FRAMES
    channels = conv_weight.shape[1]
    smem = pl.BlockSpec(memory_space=pltpu.SMEM)
    vmem = pl.BlockSpec(memory_space=pltpu.VMEM)
    return pl.pallas_call(
        convolve_kernel,
        in_specs=[smem] + [vmem] * 6,
        out_specs=vmem,
        out_shape=jax.ShapeDtypeStruct((FRAMES, 2, 2 * rows, channels), jnp.bfloat16),
        scratch_shapes=[pltpu.VMEM((FRAMES, 4, 2 * rows + 16, LATENT_CH), jnp.float32)],
        compiler_params=pltpu.CompilerParams(vmem_limit_bytes=VMEM_LIMIT),
    )(where, even, odd, left, right, conv_weight, conv_bias[None])


def gather_cores(pieces):
    same = jnp.concatenate(pieces, axis=0) if len(pieces) > 1 else pieces[0]
    return [same, swap(same, "plane", 1)]


def after(value, *others):
    return lax.optimization_barrier((value,) + others)[0]


def shards(queries, keys, values, w_out, shift_mod, scale_mod, w_final, conv_weight, conv_bias):
    groups = lax.axis_size("heads")
    planes = lax.axis_size("plane")
    heads_at = lax.axis_index("heads")
    plane_at = lax.axis_index("plane")
    devices = groups * planes
    tokens, width = queries.shape
    group_width = width // groups
    rows_dev = tokens // devices
    where = jnp.stack(
        [heads_at, plane_at, heads_at * planes + plane_at, jnp.int32(devices)]
    ).astype(jnp.int32)

    def group_of(source, r):
        return lax.dynamic_slice_in_dim(source, (heads_at ^ r) * group_width, group_width, axis=1)

    def across(piece):
        return [piece] + [swap(piece, "plane", d) for d in range(2, planes, 2)]

    piece = [jnp.stack([group_of(keys, r), group_of(values, r)])[None] for r in range(groups)]
    got = [piece[0], swap(piece[1], "heads", 1), swap(piece[2], "heads", 2)]
    got.append(swap(after(piece[3], got[2]), "heads", 3))

    queries = after(queries, *piece)
    to = lax.broadcasted_iota(jnp.int32, (tokens, tokens), 0)
    at = lax.broadcasted_iota(jnp.int32, (tokens, tokens), 1)
    j, t, row = to // (groups * rows_dev), (to // rows_dev) % groups, to % rows_dev
    mixed = []
    for r in range(groups):
        place = row * devices + (t ^ (r ^ heads_at)) * planes + (j ^ plane_at)
        part = jnp.dot(
            (at == place).astype(jnp.bfloat16), group_of(queries, r), preferred_element_type=jnp.float32
        )
        mixed.append(part.astype(jnp.bfloat16).reshape(planes, groups, rows_dev, group_width))
    mixed = jnp.stack(mixed, axis=1)
    in_plane = [mixed[0]] + [swap(mixed[d], "plane", d) for d in range(1, planes)]
    asked = []
    for r in range(groups):
        own = jnp.stack([part[r] for part in in_plane], axis=1)
        own = own.reshape(groups, planes * rows_dev, group_width)
        asked.append(own if r == 0 else swap(after(own, got[3]), "heads", r))

    crossed = [across(p) for p in got]
    keys_values = gather_cores(crossed[0] + crossed[1])
    for r in range(2, groups):
        keys_values += gather_cores(crossed[r])

    near, far = (0, 1), (3, 2)
    sent = [swap(o, "heads", t) for t, o in zip(far, attend(asked, keys_values, far))]
    kept = [o if t == 0 else swap(o, "heads", t) for t, o in zip(near, attend(asked, keys_values, near))]
    partial = project(where, kept, near, w_out, 512)
    even, odd = final_layer(
        where, sent, far, partial, w_out, scale_mod, shift_mod, w_final, rows_dev, planes
    )
    both = ("heads", "plane")
    left = lax.ppermute(odd, both, [(i, i + 1) for i in range(devices - 1)])
    right = lax.ppermute(even, both, [(i + 1, i) for i in range(devices - 1)])
    return convolve(where, even, odd, left, right, conv_weight, conv_bias)


def solution(mesh):
    groups, seq = mesh.devices.shape
    split = Mesh(
        mesh.devices.reshape(groups, HEAD_GROUPS, seq // HEAD_GROUPS), ("groups", "heads", "plane")
    )
    by_token = P(("groups", "heads", "plane"), None)
    placed = (by_token, by_token, by_token, P(), P("groups"), P("groups"), P(), P(), P())
    return jax.shard_map(
        shards,
        mesh=split,
        in_specs=placed,
        out_specs=P("groups", ("heads", "plane"), None, None),
        check_vma=False,
    )
```

```python
import functools
import math

import jax
import jax.numpy as jnp
from jax import lax
from jax.experimental import pallas as pl
from jax.experimental.pallas import tpu as pltpu
from jax.sharding import Mesh
from jax.sharding import PartitionSpec as P

HEAD_DIM = 128
HEAD_GROUPS = 4
LATENT_CH = 16
FRAMES = 4
VMEM_LIMIT = 16 * 1024 * 1024
EXP2_SCALE = math.log2(math.e) / math.sqrt(HEAD_DIM)


def swap(source, axis, distance):
    count = lax.axis_size(axis)
    return lax.ppermute(source, axis, [(i, i ^ distance) for i in range(count)])


def bundle_kernel(where_ref, q_ref, k_ref, v_ref, *out_refs, groups, planes, distances):
    tokens, width = q_ref.shape
    group_width = width // groups
    rows_dev = tokens // (groups * planes)
    to = lax.broadcasted_iota(jnp.int32, (tokens, tokens), 0)
    at = lax.broadcasted_iota(jnp.int32, (tokens, tokens), 1)
    j, t, row = to // (groups * rows_dev), (to // rows_dev) % groups, to % rows_dev
    for r, out_ref in zip(distances, out_refs):
        group = where_ref[0] ^ r
        lanes = pl.ds(pl.multiple_of(group * group_width, 128), group_width)
        place = row * (groups * planes) + (t ^ group) * planes + (j ^ where_ref[1])
        order = (at == place).astype(jnp.bfloat16)
        out_ref[:tokens] = k_ref[:, lanes]
        out_ref[tokens : 2 * tokens] = v_ref[:, lanes]
        mixed = jnp.dot(order, q_ref[:, lanes], preferred_element_type=jnp.float32)
        out_ref[2 * tokens :] = mixed.astype(jnp.bfloat16)


def bundles(where, queries, keys, values, groups, planes, distances):
    tokens, width = queries.shape
    vmem = pl.BlockSpec(memory_space=pltpu.VMEM)
    result = jax.ShapeDtypeStruct((3 * tokens, width // groups), jnp.bfloat16)
    return pl.pallas_call(
        functools.partial(bundle_kernel, groups=groups, planes=planes, distances=distances),
        in_specs=[pl.BlockSpec(memory_space=pltpu.SMEM)] + [vmem] * 3,
        out_specs=[vmem] * len(distances),
        out_shape=[result] * len(distances),
        compiler_params=pltpu.CompilerParams(vmem_limit_bytes=VMEM_LIMIT),
    )(where, queries, keys, values)


def attend_kernel(*refs, sources, planes, blocks, part, targets, rows_step):
    q_refs = refs[:sources]
    kv_refs = refs[sources : sources + len(blocks)]
    o_refs = refs[sources + len(blocks) :]
    tokens, width = q_refs[0].shape
    rows = tokens // sources
    rows_dev = rows // planes
    to = lax.broadcasted_iota(jnp.int32, (tokens, tokens), 0)
    at = lax.broadcasted_iota(jnp.int32, (tokens, tokens), 1)
    t, j, row = to // rows, (to // rows_dev) % planes, to % rows_dev
    place = ((j % 2) * (planes // 2) + j // 2) * rows + t * rows_dev + row
    order = (at == place).astype(jnp.bfloat16)
    asked = [
        jnp.dot(order, q[...], preferred_element_type=jnp.float32).astype(jnp.bfloat16) for q in q_refs
    ]
    works = [
        (h, range(first, min(first + rows_step, len(targets))))
        for h in range(width // HEAD_DIM)
        for first in range(0, len(targets), rows_step)
    ]

    def taken(ref, count, h, which):
        cut = ref[: count * 2 * part, h * HEAD_DIM : (h + 1) * HEAD_DIM]
        return cut.reshape(count, 2, part, HEAD_DIM)[:, which].reshape(count * part, HEAD_DIM)

    def scores_of(work):
        h, block = work
        lanes = slice(h * HEAD_DIM, (h + 1) * HEAD_DIM)
        query = jnp.concatenate(
            [q[targets[i] * rows : (targets[i] + 1) * rows, lanes] for i in block for q in asked], axis=0
        )
        return [
            lax.dot_general(
                query,
                taken(kv, count, h, 0),
                (((1,), (1,)), ((), ())),
                preferred_element_type=jnp.float32,
            )
            for kv, count in zip(kv_refs, blocks)
        ]

    def finish(work, scores):
        h, block = work
        peak = functools.reduce(jnp.maximum, [jnp.max(s, axis=1, keepdims=True) for s in scores])
        peak = peak * EXP2_SCALE
        summed = None
        for s, kv, count in zip(scores, kv_refs, blocks):
            weights = jnp.exp2(s * EXP2_SCALE - peak).astype(jnp.bfloat16)
            value = taken(kv, count, h, 1)
            value = jnp.concatenate([value, jnp.ones_like(value)], axis=1)
            product = jnp.dot(weights, value, preferred_element_type=jnp.float32)
            summed = product if summed is None else summed + product
        out = (summed[:, :HEAD_DIM] / summed[:, HEAD_DIM:]).astype(jnp.bfloat16)
        for n, i in enumerate(block):
            for r in range(sources):
                first = (n * sources + r) * rows
                o_refs[i][targets[i] ^ r, :, h * HEAD_DIM : (h + 1) * HEAD_DIM] = out[first : first + rows]

    scores = scores_of(works[0])
    for n, work in enumerate(works):
        following = scores_of(works[n + 1]) if n + 1 < len(works) else None
        finish(work, scores)
        scores = following


def attend(queries, keys_values, targets, planes):
    sources = len(queries)
    tokens, width = queries[0].shape
    rows = tokens // sources
    blocks = [kv.shape[0] // (2 * tokens) for kv in keys_values]
    key_count = sum(blocks) * tokens
    small = key_count <= 4096
    rows_step, step_width = (2, width) if small else (1, HEAD_DIM)
    score_bytes = rows_step * tokens * key_count * 4
    limit = 8 * key_count * step_width + 3 * score_bytes + 6 * 1024 * 1024
    return pl.pallas_call(
        functools.partial(
            attend_kernel,
            sources=sources,
            planes=planes,
            blocks=blocks,
            part=tokens,
            targets=targets,
            rows_step=rows_step,
        ),
        grid=(width // step_width,),
        in_specs=[pl.BlockSpec((tokens, step_width), lambda h: (0, h))] * sources
        + [pl.BlockSpec((kv.shape[0], step_width), lambda h: (0, h)) for kv in keys_values],
        out_specs=[pl.BlockSpec((sources, rows, step_width), lambda h: (0, 0, h))] * len(targets),
        out_shape=[jax.ShapeDtypeStruct((sources, rows, width), jnp.bfloat16)] * len(targets),
        compiler_params=pltpu.CompilerParams(vmem_limit_bytes=min(limit, 60 * 1024 * 1024)),
    )(*queries, *keys_values)


def project_kernel(where_ref, *refs, targets):
    o_refs = refs[: len(targets)]
    w_ref, out_ref, lined = refs[len(targets) :]
    width = o_refs[0].shape[2]
    tokens = lined.shape[0]
    for n in range(len(targets)):
        lined[:, n * width : (n + 1) * width] = o_refs[n][...].reshape(tokens, width)
    rows = [pl.ds(pl.multiple_of((where_ref[0] ^ t) * width, 128), width) for t in targets]
    weights = jnp.concatenate([w_ref[r, :] for r in rows], axis=0)
    out_ref[...] = jnp.dot(lined[...], weights, preferred_element_type=jnp.float32)


def project(where, attended, targets, w_out, tile):
    sources, rows, width = attended[0].shape
    tokens = sources * rows
    inner, features = w_out.shape
    return pl.pallas_call(
        functools.partial(project_kernel, targets=targets),
        grid_spec=pltpu.PrefetchScalarGridSpec(
            num_scalar_prefetch=1,
            grid=(features // tile,),
            in_specs=[pl.BlockSpec((sources, rows, width), lambda i, *_: (0, 0, 0))] * len(targets)
            + [pl.BlockSpec((inner, tile), lambda i, *_: (0, i))],
            out_specs=pl.BlockSpec((None, tokens, tile), lambda i, *_: (i, 0, 0)),
            scratch_shapes=[pltpu.VMEM((tokens, len(targets) * width), jnp.bfloat16)],
        ),
        out_shape=jax.ShapeDtypeStruct((features // tile, tokens, tile), jnp.float32),
        compiler_params=pltpu.CompilerParams(vmem_limit_bytes=VMEM_LIMIT),
    )(where, *attended, w_out)


def final_kernel(where_ref, *refs, targets, planes, rows_dev):
    o_refs = refs[: len(targets)]
    partial_ref, w_ref, scale_ref, shift_ref, w_final_ref, even_ref, odd_ref, lined, projected = refs[
        len(targets) :
    ]
    step = pl.program_id(0)
    heads_at, plane_at = where_ref[0], where_ref[1]
    tokens = lined.shape[0]
    width = o_refs[0].shape[2]
    tile = w_ref.shape[1]
    for n in range(len(targets)):
        lined[:, n * width : (n + 1) * width] = o_refs[n][...].reshape(tokens, width)
    rows = [pl.ds(pl.multiple_of((heads_at ^ t) * width, 128), width) for t in targets]
    weights = jnp.concatenate([w_ref[r, :] for r in rows], axis=0)
    projected[step] = partial_ref[...] + jnp.dot(
        lined[...], weights, preferred_element_type=jnp.float32
    )

    @pl.when(step == pl.num_programs(0) - 1)
    def _():
        steps = projected.shape[0]
        features = steps * tile
        total = projected[0]
        for i in range(1, steps):
            total = total + projected[i]
        mean = jnp.sum(total, axis=1, keepdims=True) * (1.0 / features)
        squares = None
        for i in range(steps):
            centered = projected[i] - mean
            squares = centered * centered if squares is None else squares + centered * centered
        variance = jnp.sum(squares, axis=1, keepdims=True) * (1.0 / features)
        inverse = lax.rsqrt(variance + 1e-06)
        patches = None
        for i in range(steps):
            lanes = slice(i * tile, (i + 1) * tile)
            normed = (projected[i] - mean) * inverse * (1.0 + scale_ref[:, lanes]) + shift_ref[:, lanes]
            part = lax.dot_general(
                normed.astype(jnp.bfloat16),
                w_final_ref[:, lanes],
                (((1,), (1,)), ((), ())),
                preferred_element_type=jnp.float32,
            )
            patches = part if patches is None else patches + part
        patches = patches.astype(jnp.bfloat16)
        channels = patches.shape[1]
        half = channels // 2
        source = lax.broadcasted_iota(jnp.int32, (channels, channels), 0)
        target = lax.broadcasted_iota(jnp.int32, (channels, channels), 1)
        q, p, c = target // half, (target // LATENT_CH) % 2, target % LATENT_CH
        lane_order = (source == 4 * c + 2 * p + q).astype(jnp.bfloat16)
        to = lax.broadcasted_iota(jnp.int32, (tokens, tokens), 0)
        at = lax.broadcasted_iota(jnp.int32, (tokens, tokens), 1)
        share = planes * rows_dev
        place = ((to // share) ^ heads_at) * share
        place = place + (((to % share) // rows_dev) ^ plane_at) * rows_dev + to % rows_dev
        row_order = (at == place).astype(jnp.bfloat16)
        cells = jnp.dot(patches, lane_order, preferred_element_type=jnp.float32)
        cells = jnp.dot(row_order, cells.astype(jnp.bfloat16), preferred_element_type=jnp.float32)
        cells = cells.astype(jnp.bfloat16)
        even_ref[...] = cells[:, :half]
        odd_ref[...] = cells[:, half:]


def final_layer(where, attended, targets, partial, w_out, scale_mod, shift_mod, w_final, rows_dev, planes):
    sources, rows, width = attended[0].shape
    inner, features = w_out.shape
    steps, tokens, tile = partial.shape
    channels = w_final.shape[1]
    whole = lambda shape: pl.BlockSpec(shape, lambda i, *_: (0,) * len(shape))
    result = jax.ShapeDtypeStruct((tokens, channels // 2), jnp.bfloat16)
    return pl.pallas_call(
        functools.partial(final_kernel, targets=targets, planes=planes, rows_dev=rows_dev),
        grid_spec=pltpu.PrefetchScalarGridSpec(
            num_scalar_prefetch=1,
            grid=(steps,),
            in_specs=[whole((sources, rows, width))] * len(targets)
            + [
                pl.BlockSpec((None, tokens, tile), lambda i, *_: (i, 0, 0)),
                pl.BlockSpec((inner, tile), lambda i, *_: (0, i)),
                whole((1, features)),
                whole((1, features)),
                whole((channels, features)),
            ],
            out_specs=[whole((tokens, channels // 2))] * 2,
            scratch_shapes=[
                pltpu.VMEM((tokens, len(targets) * width), jnp.bfloat16),
                pltpu.VMEM((steps, tokens, tile), jnp.float32),
            ],
        ),
        out_shape=[result] * 2,
        compiler_params=pltpu.CompilerParams(vmem_limit_bytes=VMEM_LIMIT),
    )(where, *attended, partial, w_out, scale_mod[None], shift_mod[None], w_final.T)


def convolve_kernel(where_ref, even_ref, odd_ref, left_ref, right_ref, w_ref, bias_ref, out_ref, latent):
    frames, cols, _, ch = latent.shape
    rows = even_ref.shape[0] // frames
    height = 2 * rows
    even = even_ref[...].astype(jnp.float32)
    odd = odd_ref[...].astype(jnp.float32)
    left = jnp.where(where_ref[2] == 0, even, left_ref[...].astype(jnp.float32))
    right = jnp.where(where_ref[2] == where_ref[3] - 1, odd, right_ref[...].astype(jnp.float32))
    for x, cells in enumerate((left, even, odd, right)):
        for f in range(frames):
            own = cells[f * rows : (f + 1) * rows]
            for p in range(2):
                latent[f, x, pl.ds(8 + p, rows, stride=2), :] = own[:, p * ch : (p + 1) * ch]
            latent[f, x, 7:8, :] = own[:1, :ch]
            latent[f, x, 8 + height : 9 + height, :] = own[rows - 1 :, ch:]
    depth = 9 * ch
    for x in range(cols - 2):
        stacked = []
        for f in range(frames):
            taps = [latent[f, x + b, 7 + e : 7 + e + height, :] for b in range(3) for e in range(3)]
            stacked.append(jnp.concatenate(taps, axis=1).astype(jnp.bfloat16))
        stacked = [stacked[0]] * 2 + stacked
        acc = None
        for a in range(3):
            flat = jnp.concatenate(stacked[a : a + frames], axis=0)
            part = jnp.dot(
                flat, w_ref[a * depth : (a + 1) * depth, :], preferred_element_type=jnp.float32
            )
            acc = part if acc is None else acc + part
        acc = (acc + bias_ref[...]).astype(jnp.bfloat16)
        out_ref[:, x] = acc.reshape(frames, height, acc.shape[1])


def convolve(where, even, odd, left, right, conv_weight, conv_bias):
    rows = even.shape[0] // FRAMES
    channels = conv_weight.shape[1]
    smem = pl.BlockSpec(memory_space=pltpu.SMEM)
    vmem = pl.BlockSpec(memory_space=pltpu.VMEM)
    return pl.pallas_call(
        convolve_kernel,
        in_specs=[smem] + [vmem] * 6,
        out_specs=vmem,
        out_shape=jax.ShapeDtypeStruct((FRAMES, 2, 2 * rows, channels), jnp.bfloat16),
        scratch_shapes=[pltpu.VMEM((FRAMES, 4, 2 * rows + 16, LATENT_CH), jnp.float32)],
        compiler_params=pltpu.CompilerParams(vmem_limit_bytes=VMEM_LIMIT),
    )(where, even, odd, left, right, conv_weight, conv_bias[None])


def shards(queries, keys, values, w_out, shift_mod, scale_mod, w_final, conv_weight, conv_bias):
    groups = lax.axis_size("heads")
    planes = lax.axis_size("plane")
    heads_at = lax.axis_index("heads")
    plane_at = lax.axis_index("plane")
    devices = groups * planes
    tokens = queries.shape[0]
    rows_dev = tokens // devices
    where = jnp.stack(
        [heads_at, plane_at, heads_at * planes + plane_at, jnp.int32(devices)]
    ).astype(jnp.int32)

    made = bundles(where, queries, keys, values, groups, planes, range(groups))
    got = {r: swap(made[r], "heads", r) if r else made[r] for r in range(groups)}

    both_parts, share = 2 * tokens, tokens // planes
    held = {r: [got[r]] for r in range(groups)}
    for r in (0, 1, 2, 3):
        for d in range(2, planes, 2):
            asked = got[r][both_parts + d * share : both_parts + (d + 2) * share]
            held[r].append(swap(jnp.concatenate([got[r][:both_parts], asked], axis=0), "plane", d))

    keys_values, asked = [], {}
    for distances in ((0, 1), (2,), (3,)):
        passed = [h[:both_parts] for r in distances for h in held[r]]
        passed += [h[both_parts + share : both_parts + 2 * share] for r in distances for h in held[r]]
        mine = jnp.concatenate(passed, axis=0)
        other = swap(mine, "plane", 1)
        keys_values += [mine, other]
        half = planes // 2
        first = both_parts * half * len(distances)
        for n, r in enumerate(distances):
            start = first + n * half * share
            asked[r] = jnp.concatenate(
                [h[both_parts : both_parts + share] for h in held[r]]
                + [other[start : start + half * share]],
                axis=0,
            )
    asked = [asked[r] for r in range(groups)]

    first, second = (1, 3), (2, 0)
    near, far = (0, 1), (3, 2)
    results = {}
    for targets in (first, second):
        for t, o in zip(targets, attend(asked, keys_values, targets, planes)):
            results[t] = o if t == 0 else swap(o, "heads", t)
    partial = project(where, [results[t] for t in near], near, w_out, 512)
    sent = [results[t] for t in far]
    even, odd = final_layer(
        where, sent, far, partial, w_out, scale_mod, shift_mod, w_final, rows_dev, planes
    )
    both = ("heads", "plane")
    left = lax.ppermute(odd, both, [(i, i + 1) for i in range(devices - 1)])
    right = lax.ppermute(even, both, [(i + 1, i) for i in range(devices - 1)])
    return convolve(where, even, odd, left, right, conv_weight, conv_bias)


def solution(mesh):
    groups, seq = mesh.devices.shape
    split = Mesh(
        mesh.devices.reshape(groups, HEAD_GROUPS, seq // HEAD_GROUPS), ("groups", "heads", "plane")
    )
    by_token = P(("groups", "heads", "plane"), None)
    placed = (by_token, by_token, by_token, P(), P("groups"), P("groups"), P(), P(), P())
    return jax.shard_map(
        shards,
        mesh=split,
        in_specs=placed,
        out_specs=P("groups", ("heads", "plane"), None, None),
        check_vma=False,
    )
```

```python
import functools
import math

import jax
import jax.numpy as jnp
from jax import lax
from jax.experimental import pallas as pl
from jax.experimental.pallas import tpu as pltpu
from jax.sharding import Mesh
from jax.sharding import PartitionSpec as P

HEAD_DIM = 128
HEAD_GROUPS = 4
LATENT_CH = 16
FRAMES = 4
VMEM_LIMIT = 16 * 1024 * 1024
VMEM_WHOLE = 63 * 1024 * 1024
EXP2_SCALE = math.log2(math.e) / math.sqrt(HEAD_DIM)


def swap(source, axis, distance):
    count = lax.axis_size(axis)
    return lax.ppermute(source, axis, [(i, i ^ distance) for i in range(count)])


def run_copies(copies, semaphores, first=0):
    started = [
        pltpu.make_async_copy(source, target, semaphores.at[first + n])
        for n, (source, target) in enumerate(copies)
    ]
    for copy in started:
        copy.start()
    return started


def group_lanes(ref, r, groups):
    width = ref.shape[1] // groups
    return pl.ds(pl.multiple_of((lax.axis_index("heads") ^ r) * width, 128), width)


def bundle_kernel(q_ref, k_ref, v_ref, *refs, groups, planes, parts):
    out_refs, (mixed, semaphores) = refs[-2 - len(parts) : -2], refs[-2:]
    tokens = q_ref.shape[0]
    rows_dev = tokens // (groups * planes)
    copies = []
    for (r, with_kv, _), out_ref in zip(parts, out_refs):
        if with_kv:
            lanes = group_lanes(k_ref, r, groups)
            copies += [
                (source.at[:, lanes], out_ref.at[pl.ds(n * tokens, tokens)])
                for n, source in enumerate((k_ref, v_ref))
            ]
    waiting = run_copies(copies, semaphores)
    heads_at, plane_at = lax.axis_index("heads"), lax.axis_index("plane")
    to = lax.broadcasted_iota(jnp.int32, (tokens, tokens), 0)
    at = lax.broadcasted_iota(jnp.int32, (tokens, tokens), 1)
    j, t, row = to // (groups * rows_dev), (to // rows_dev) % groups, to % rows_dev
    copies = []
    for (r, with_kv, with_q), out_ref in zip(parts, out_refs):
        if with_q:
            place = row * (groups * planes) + (t ^ (heads_at ^ r)) * planes + (j ^ plane_at)
            order = (at == place).astype(jnp.bfloat16)
            query = jnp.dot(
                order, q_ref[:, group_lanes(q_ref, r, groups)], preferred_element_type=jnp.float32
            )
            mixed[r] = query.astype(jnp.bfloat16)
            first = 2 * tokens if with_kv else 0
            copies.append((mixed.at[r], out_ref.at[pl.ds(first, tokens)]))
    waiting += run_copies(copies, semaphores, len(waiting))
    for copy in waiting:
        copy.wait()


def bundles(queries, keys, values, groups, planes, parts, *tokens_before):
    tokens, width = queries.shape
    group_width = width // groups
    anywhere = pl.BlockSpec(memory_space=pl.ANY)
    copies = sum(2 * kv + q for _, kv, q in parts)
    return pl.pallas_call(
        functools.partial(bundle_kernel, groups=groups, planes=planes, parts=parts),
        in_specs=[pl.BlockSpec(memory_space=pltpu.VMEM)] + [anywhere] * (2 + len(tokens_before)),
        out_specs=[anywhere] * len(parts),
        out_shape=[
            jax.ShapeDtypeStruct(((2 * kv + q) * tokens, group_width), jnp.bfloat16)
            for _, kv, q in parts
        ],
        scratch_shapes=[
            pltpu.VMEM((groups, tokens, group_width), jnp.bfloat16),
            pltpu.SemaphoreType.DMA((copies,)),
        ],
        compiler_params=pltpu.CompilerParams(vmem_limit_bytes=VMEM_WHOLE),
    )(queries, keys, values, *tokens_before)


def attend_kernel(*refs, sources, planes, blocks, part, targets, rows_step):
    q_refs = refs[:sources]
    kv_refs = refs[sources : sources + len(blocks)]
    o_refs = refs[sources + len(blocks) :]
    tokens, width = q_refs[0].shape
    rows = tokens // sources
    rows_dev = rows // planes
    to = lax.broadcasted_iota(jnp.int32, (tokens, tokens), 0)
    at = lax.broadcasted_iota(jnp.int32, (tokens, tokens), 1)
    t, j, row = to // rows, (to // rows_dev) % planes, to % rows_dev
    place = ((j % 2) * (planes // 2) + j // 2) * rows + t * rows_dev + row
    order = (at == place).astype(jnp.bfloat16)
    asked = [
        jnp.dot(order, q[...], preferred_element_type=jnp.float32).astype(jnp.bfloat16) for q in q_refs
    ]
    works = [
        (h, range(first, min(first + rows_step, len(targets))))
        for h in range(width // HEAD_DIM)
        for first in range(0, len(targets), rows_step)
    ]

    def taken(ref, count, h, which):
        cut = ref[: count * 2 * part, h * HEAD_DIM : (h + 1) * HEAD_DIM]
        return cut.reshape(count, 2, part, HEAD_DIM)[:, which].reshape(count * part, HEAD_DIM)

    def scores_of(work):
        h, block = work
        lanes = slice(h * HEAD_DIM, (h + 1) * HEAD_DIM)
        query = jnp.concatenate(
            [q[targets[i] * rows : (targets[i] + 1) * rows, lanes] for i in block for q in asked], axis=0
        )
        return [
            lax.dot_general(
                query,
                taken(kv, count, h, 0),
                (((1,), (1,)), ((), ())),
                preferred_element_type=jnp.float32,
            )
            for kv, count in zip(kv_refs, blocks)
        ]

    def finish(work, scores):
        h, block = work
        peak = functools.reduce(jnp.maximum, [jnp.max(s, axis=1, keepdims=True) for s in scores])
        peak = peak * EXP2_SCALE
        summed = None
        for s, kv, count in zip(scores, kv_refs, blocks):
            weights = jnp.exp2(s * EXP2_SCALE - peak).astype(jnp.bfloat16)
            value = taken(kv, count, h, 1)
            value = jnp.concatenate([value, jnp.ones_like(value)], axis=1)
            product = jnp.dot(weights, value, preferred_element_type=jnp.float32)
            summed = product if summed is None else summed + product
        out = (summed[:, :HEAD_DIM] / summed[:, HEAD_DIM:]).astype(jnp.bfloat16)
        for n, i in enumerate(block):
            for r in range(sources):
                first = (n * sources + r) * rows
                o_refs[i][targets[i] ^ r, :, h * HEAD_DIM : (h + 1) * HEAD_DIM] = out[first : first + rows]

    scores = scores_of(works[0])
    for n, work in enumerate(works):
        following = scores_of(works[n + 1]) if n + 1 < len(works) else None
        finish(work, scores)
        scores = following


def attend(queries, keys_values, targets, planes):
    sources = len(queries)
    tokens, width = queries[0].shape
    rows = tokens // sources
    blocks = [kv.shape[0] // (2 * tokens) for kv in keys_values]
    key_count = sum(blocks) * tokens
    small = key_count <= 4096
    rows_step, step_width = (2, width) if small else (1, HEAD_DIM)
    score_bytes = rows_step * tokens * key_count * 4
    limit = 8 * key_count * step_width + 3 * score_bytes + 6 * 1024 * 1024
    return pl.pallas_call(
        functools.partial(
            attend_kernel,
            sources=sources,
            planes=planes,
            blocks=blocks,
            part=tokens,
            targets=targets,
            rows_step=rows_step,
        ),
        grid=(width // step_width,),
        in_specs=[pl.BlockSpec((tokens, step_width), lambda h: (0, h))] * sources
        + [pl.BlockSpec((kv.shape[0], step_width), lambda h: (0, h)) for kv in keys_values],
        out_specs=[pl.BlockSpec((sources, rows, step_width), lambda h: (0, 0, h))] * len(targets),
        out_shape=[jax.ShapeDtypeStruct((sources, rows, width), jnp.bfloat16)] * len(targets),
        compiler_params=pltpu.CompilerParams(vmem_limit_bytes=min(limit, 60 * 1024 * 1024)),
    )(*queries, *keys_values)


def projection_of(o_refs, w_refs, lined):
    tokens, width = lined.shape[0], o_refs[0].shape[2]
    for n, o_ref in enumerate(o_refs):
        lined[:, n * width : (n + 1) * width] = o_ref[...].reshape(tokens, width)
    weights = jnp.concatenate([w[...] for w in w_refs], axis=0)
    return jnp.dot(lined[...], weights, preferred_element_type=jnp.float32)


def projection_specs(attended, targets, tile):
    o_spec = pl.BlockSpec(attended[0].shape, lambda i, *_: (0, 0, 0))
    width = attended[0].shape[2]
    return [o_spec] * len(targets) + [
        pl.BlockSpec((width, tile), lambda i, where, t=t: (where[0] ^ t, i)) for t in targets
    ]


def project_kernel(where_ref, *refs, targets):
    count = len(targets)
    out_ref, lined = refs[2 * count :]
    out_ref[...] = projection_of(refs[:count], refs[count : 2 * count], lined)


def project(where, attended, targets, w_out, tile):
    sources, rows, width = attended[0].shape
    tokens = sources * rows
    features = w_out.shape[1]
    return pl.pallas_call(
        functools.partial(project_kernel, targets=targets),
        grid_spec=pltpu.PrefetchScalarGridSpec(
            num_scalar_prefetch=1,
            grid=(features // tile,),
            in_specs=projection_specs(attended, targets, tile),
            out_specs=pl.BlockSpec((None, tokens, tile), lambda i, *_: (i, 0, 0)),
            scratch_shapes=[pltpu.VMEM((tokens, len(targets) * width), jnp.bfloat16)],
        ),
        out_shape=jax.ShapeDtypeStruct((features // tile, tokens, tile), jnp.float32),
        compiler_params=pltpu.CompilerParams(vmem_limit_bytes=VMEM_LIMIT),
    )(where, *attended, *[w_out] * len(targets))


def final_kernel(where_ref, *refs, targets, planes, rows_dev):
    count = len(targets)
    partial_ref, scale_ref, shift_ref, w_final_ref, even_ref, odd_ref, lined, projected = refs[2 * count :]
    step = pl.program_id(0)
    heads_at, plane_at = where_ref[0], where_ref[1]
    tokens = lined.shape[0]
    tile = partial_ref.shape[1]
    projected[step] = partial_ref[...] + projection_of(refs[:count], refs[count : 2 * count], lined)

    @pl.when(step == pl.num_programs(0) - 1)
    def _():
        steps = projected.shape[0]
        features = steps * tile
        total = projected[0]
        for i in range(1, steps):
            total = total + projected[i]
        mean = jnp.sum(total, axis=1, keepdims=True) * (1.0 / features)
        squares = None
        for i in range(steps):
            centered = projected[i] - mean
            squares = centered * centered if squares is None else squares + centered * centered
        variance = jnp.sum(squares, axis=1, keepdims=True) * (1.0 / features)
        inverse = lax.rsqrt(variance + 1e-06)
        patches = None
        for i in range(steps):
            lanes = slice(i * tile, (i + 1) * tile)
            normed = (projected[i] - mean) * inverse * (1.0 + scale_ref[:, lanes]) + shift_ref[:, lanes]
            part = lax.dot_general(
                normed.astype(jnp.bfloat16),
                w_final_ref[:, lanes],
                (((1,), (1,)), ((), ())),
                preferred_element_type=jnp.float32,
            )
            patches = part if patches is None else patches + part
        patches = patches.astype(jnp.bfloat16)
        channels = patches.shape[1]
        half = channels // 2
        source = lax.broadcasted_iota(jnp.int32, (channels, channels), 0)
        target = lax.broadcasted_iota(jnp.int32, (channels, channels), 1)
        q, p, c = target // half, (target // LATENT_CH) % 2, target % LATENT_CH
        lane_order = (source == 4 * c + 2 * p + q).astype(jnp.bfloat16)
        to = lax.broadcasted_iota(jnp.int32, (tokens, tokens), 0)
        at = lax.broadcasted_iota(jnp.int32, (tokens, tokens), 1)
        share = planes * rows_dev
        place = ((to // share) ^ heads_at) * share
        place = place + (((to % share) // rows_dev) ^ plane_at) * rows_dev + to % rows_dev
        row_order = (at == place).astype(jnp.bfloat16)
        cells = jnp.dot(patches, lane_order, preferred_element_type=jnp.float32)
        cells = jnp.dot(row_order, cells.astype(jnp.bfloat16), preferred_element_type=jnp.float32)
        cells = cells.astype(jnp.bfloat16)
        even_ref[...] = cells[:, :half]
        odd_ref[...] = cells[:, half:]


def final_layer(where, attended, targets, partial, w_out, scale_mod, shift_mod, w_final, rows_dev, planes):
    sources, rows, width = attended[0].shape
    features = w_out.shape[1]
    steps, tokens, tile = partial.shape
    channels = w_final.shape[1]
    whole = lambda shape: pl.BlockSpec(shape, lambda i, *_: (0,) * len(shape))
    result = jax.ShapeDtypeStruct((tokens, channels // 2), jnp.bfloat16)
    return pl.pallas_call(
        functools.partial(final_kernel, targets=targets, planes=planes, rows_dev=rows_dev),
        grid_spec=pltpu.PrefetchScalarGridSpec(
            num_scalar_prefetch=1,
            grid=(steps,),
            in_specs=projection_specs(attended, targets, tile)
            + [
                pl.BlockSpec((None, tokens, tile), lambda i, *_: (i, 0, 0)),
                whole((1, features)),
                whole((1, features)),
                whole((channels, features)),
            ],
            out_specs=[whole((tokens, channels // 2))] * 2,
            scratch_shapes=[
                pltpu.VMEM((tokens, len(targets) * width), jnp.bfloat16),
                pltpu.VMEM((steps, tokens, tile), jnp.float32),
            ],
        ),
        out_shape=[result] * 2,
        compiler_params=pltpu.CompilerParams(vmem_limit_bytes=VMEM_LIMIT),
    )(where, *attended, *[w_out] * len(targets), partial, scale_mod[None], shift_mod[None], w_final.T)


def convolve_kernel(where_ref, even_ref, odd_ref, left_ref, right_ref, w_ref, bias_ref, out_ref, latent):
    frames, cols, _, ch = latent.shape
    rows = even_ref.shape[0] // frames
    height = 2 * rows
    even = even_ref[...].astype(jnp.float32)
    odd = odd_ref[...].astype(jnp.float32)
    left = jnp.where(where_ref[2] == 0, even, left_ref[...].astype(jnp.float32))
    right = jnp.where(where_ref[2] == where_ref[3] - 1, odd, right_ref[...].astype(jnp.float32))
    for x, cells in enumerate((left, even, odd, right)):
        for f in range(frames):
            own = cells[f * rows : (f + 1) * rows]
            for p in range(2):
                latent[f, x, pl.ds(8 + p, rows, stride=2), :] = own[:, p * ch : (p + 1) * ch]
            latent[f, x, 7:8, :] = own[:1, :ch]
            latent[f, x, 8 + height : 9 + height, :] = own[rows - 1 :, ch:]
    depth = 9 * ch
    for x in range(cols - 2):
        stacked = []
        for f in range(frames):
            taps = [latent[f, x + b, 7 + e : 7 + e + height, :] for b in range(3) for e in range(3)]
            stacked.append(jnp.concatenate(taps, axis=1).astype(jnp.bfloat16))
        stacked = [stacked[0]] * 2 + stacked
        acc = None
        for a in range(3):
            flat = jnp.concatenate(stacked[a : a + frames], axis=0)
            part = jnp.dot(
                flat, w_ref[a * depth : (a + 1) * depth, :], preferred_element_type=jnp.float32
            )
            acc = part if acc is None else acc + part
        acc = (acc + bias_ref[...]).astype(jnp.bfloat16)
        out_ref[:, x] = acc.reshape(frames, height, acc.shape[1])


def convolve(where, even, odd, left, right, conv_weight, conv_bias):
    rows = even.shape[0] // FRAMES
    channels = conv_weight.shape[1]
    smem = pl.BlockSpec(memory_space=pltpu.SMEM)
    vmem = pl.BlockSpec(memory_space=pltpu.VMEM)
    return pl.pallas_call(
        convolve_kernel,
        in_specs=[smem] + [vmem] * 6,
        out_specs=vmem,
        out_shape=jax.ShapeDtypeStruct((FRAMES, 2, 2 * rows, channels), jnp.bfloat16),
        scratch_shapes=[pltpu.VMEM((FRAMES, 4, 2 * rows + 16, LATENT_CH), jnp.float32)],
        compiler_params=pltpu.CompilerParams(vmem_limit_bytes=VMEM_LIMIT),
    )(where, even, odd, left, right, conv_weight, conv_bias[None])


def after(value, *others):
    return lax.optimization_barrier((value,) + others)[0]


def shards(queries, keys, values, w_out, shift_mod, scale_mod, w_final, conv_weight, conv_bias):
    groups = lax.axis_size("heads")
    planes = lax.axis_size("plane")
    heads_at = lax.axis_index("heads")
    plane_at = lax.axis_index("plane")
    devices = groups * planes
    tokens = queries.shape[0]
    rows_dev = tokens // devices
    where = jnp.stack(
        [heads_at, plane_at, heads_at * planes + plane_at, jnp.int32(devices)]
    ).astype(jnp.int32)

    both_parts, share = 2 * tokens, tokens // planes
    got = {2: bundles(queries, keys, values, groups, planes, ((2, 1, 1),))[0]}
    parts = ((1, 1, 1), (3, 1, 0), (0, 1, 1), (3, 0, 1))
    got[1], got[3], got[0], q_3 = bundles(queries, keys, values, groups, planes, parts, got[2])
    got = {r: swap(got[r], "heads", r) if r else got[r] for r in (2, 3, 1, 0)}

    held = {}
    for r in range(groups):
        held[r] = [got[r]]
        for d in range(2, planes, 2):
            sent = got[r]
            if sent.shape[0] > both_parts:
                asked = sent[both_parts + d * share : both_parts + (d + 2) * share]
                sent = jnp.concatenate([sent[:both_parts], asked], axis=0)
            held[r].append(swap(after(sent, got[1]) if r == 0 else sent, "plane", d))
    q_3 = swap(after(q_3, *held[1][1:], *held[2][1:]), "heads", 3)

    keys_values, asked = [], {}
    half = planes // 2
    for distances in ((0, 1), (2,), (3,)):
        passed = [h[:both_parts] for r in distances for h in held[r]]
        passed += [
            h[both_parts + share : both_parts + 2 * share]
            for r in distances
            for h in held[r]
            if h.shape[0] > both_parts
        ]
        mine = jnp.concatenate(passed, axis=0)
        other = swap(mine, "plane", 1)
        keys_values += [mine, other]
        first = both_parts * half * len(distances)
        for n, r in enumerate(distances):
            start = first + n * half * share
            if start < mine.shape[0]:
                asked[r] = [h[both_parts : both_parts + share] for h in held[r]]
                asked[r].append(other[start : start + half * share])
    arrival = list(range(0, planes, 2)) + list(range(1, planes, 2))
    pieces = [q_3[d * share : (d + 1) * share] for d in arrival]
    asked[3] = [swap(piece, "plane", d) if d else piece for d, piece in zip(arrival, pieces)]
    asked = [jnp.concatenate(asked[r], axis=0) for r in range(groups)]

    first, second = (3, 2), (1, 0)
    near, far = (0, 3), (2, 1)
    results = {}
    for targets in (first, second):
        for t, o in zip(targets, attend(asked, keys_values, targets, planes)):
            results[t] = o if t == 0 else swap(o, "heads", t)
    partial = project(where, [results[t] for t in near], near, w_out, 512)
    sent = [results[t] for t in far]
    even, odd = final_layer(
        where, sent, far, partial, w_out, scale_mod, shift_mod, w_final, rows_dev, planes
    )
    both = ("heads", "plane")
    left = lax.ppermute(odd, both, [(i, i + 1) for i in range(devices - 1)])
    right = lax.ppermute(even, both, [(i + 1, i) for i in range(devices - 1)])
    return convolve(where, even, odd, left, right, conv_weight, conv_bias)


def solution(mesh):
    groups, seq = mesh.devices.shape
    split = Mesh(
        mesh.devices.reshape(groups, HEAD_GROUPS, seq // HEAD_GROUPS), ("groups", "heads", "plane")
    )
    by_token = P(("groups", "heads", "plane"), None)
    placed = (by_token, by_token, by_token, P(), P("groups"), P("groups"), P(), P(), P())
    return jax.shard_map(
        shards,
        mesh=split,
        in_specs=placed,
        out_specs=P("groups", ("heads", "plane"), None, None),
        check_vma=False,
    )
```

```python
import functools
import math

import jax
import jax.numpy as jnp
from jax import lax
from jax.experimental import pallas as pl
from jax.experimental.pallas import tpu as pltpu
from jax.sharding import Mesh
from jax.sharding import PartitionSpec as P

HEAD_DIM = 128
HEAD_GROUPS = 4
LATENT_CH = 16
FRAMES = 4
VMEM_LIMIT = 16 * 1024 * 1024
VMEM_WHOLE = 63 * 1024 * 1024
CHUNKS = ((0, 3),)
VMEM_WHOLE = 63 * 1024 * 1024
EXP2_SCALE = math.log2(math.e) / math.sqrt(HEAD_DIM)


def swap(source, axis, distance):
    count = lax.axis_size(axis)
    return lax.ppermute(source, axis, [(i, i ^ distance) for i in range(count)])


def bundle_kernel(q_ref, k_ref, v_ref, *out_refs, groups, planes, cuts):
    tokens, width = q_ref.shape
    group_width = width // groups
    rows_dev = tokens // (groups * planes)
    heads_at, plane_at = lax.axis_index("heads"), lax.axis_index("plane")
    to = lax.broadcasted_iota(jnp.int32, (tokens, tokens), 0)
    at = lax.broadcasted_iota(jnp.int32, (tokens, tokens), 1)
    j, t, row = to // (groups * rows_dev), (to // rows_dev) % groups, to % rows_dev
    for (r, low, high), out_ref in zip(cuts, out_refs):
        group = heads_at ^ r
        first = pl.multiple_of(group * group_width + low * HEAD_DIM, HEAD_DIM)
        lanes = pl.ds(first, (high - low) * HEAD_DIM)
        place = row * (groups * planes) + (t ^ group) * planes + (j ^ plane_at)
        order = (at == place).astype(jnp.bfloat16)
        out_ref[:tokens] = k_ref[:, lanes]
        out_ref[tokens : 2 * tokens] = v_ref[:, lanes]
        mixed = jnp.dot(order, q_ref[:, lanes], preferred_element_type=jnp.float32)
        out_ref[2 * tokens :] = mixed.astype(jnp.bfloat16)


def bundles(queries, keys, values, groups, planes, cuts):
    tokens = queries.shape[0]
    vmem = pl.BlockSpec(memory_space=pltpu.VMEM)
    return pl.pallas_call(
        functools.partial(bundle_kernel, groups=groups, planes=planes, cuts=cuts),
        in_specs=[vmem] * 3,
        out_specs=[vmem] * len(cuts),
        out_shape=[
            jax.ShapeDtypeStruct((3 * tokens, (high - low) * HEAD_DIM), jnp.bfloat16)
            for _, low, high in cuts
        ],
        compiler_params=pltpu.CompilerParams(vmem_limit_bytes=VMEM_WHOLE),
    )(queries, keys, values)


def attend_kernel(*refs, sources, planes, blocks, part, targets, rows_step):
    q_refs = refs[:sources]
    kv_refs = refs[sources : sources + len(blocks)]
    o_refs = refs[sources + len(blocks) :]
    tokens, width = q_refs[0].shape
    rows = tokens // sources
    rows_dev = rows // planes
    to = lax.broadcasted_iota(jnp.int32, (tokens, tokens), 0)
    at = lax.broadcasted_iota(jnp.int32, (tokens, tokens), 1)
    t, j, row = to // rows, (to // rows_dev) % planes, to % rows_dev
    place = ((j % 2) * (planes // 2) + j // 2) * rows + t * rows_dev + row
    order = (at == place).astype(jnp.bfloat16)
    asked = [
        jnp.dot(order, q[...], preferred_element_type=jnp.float32).astype(jnp.bfloat16) for q in q_refs
    ]
    works = [
        (h, range(first, min(first + rows_step, len(targets))))
        for h in range(width // HEAD_DIM)
        for first in range(0, len(targets), rows_step)
    ]

    def taken(ref, count, h, which):
        cut = ref[: count * 2 * part, h * HEAD_DIM : (h + 1) * HEAD_DIM]
        return cut.reshape(count, 2, part, HEAD_DIM)[:, which].reshape(count * part, HEAD_DIM)

    def scores_of(work):
        h, block = work
        lanes = slice(h * HEAD_DIM, (h + 1) * HEAD_DIM)
        query = jnp.concatenate(
            [q[targets[i] * rows : (targets[i] + 1) * rows, lanes] for i in block for q in asked], axis=0
        )
        return [
            lax.dot_general(
                query,
                taken(kv, count, h, 0),
                (((1,), (1,)), ((), ())),
                preferred_element_type=jnp.float32,
            )
            for kv, count in zip(kv_refs, blocks)
        ]

    def finish(work, scores):
        h, block = work
        peak = functools.reduce(jnp.maximum, [jnp.max(s, axis=1, keepdims=True) for s in scores])
        peak = peak * EXP2_SCALE
        summed = None
        for s, kv, count in zip(scores, kv_refs, blocks):
            weights = jnp.exp2(s * EXP2_SCALE - peak).astype(jnp.bfloat16)
            value = taken(kv, count, h, 1)
            value = jnp.concatenate([value, jnp.ones_like(value)], axis=1)
            product = jnp.dot(weights, value, preferred_element_type=jnp.float32)
            summed = product if summed is None else summed + product
        out = (summed[:, :HEAD_DIM] / summed[:, HEAD_DIM:]).astype(jnp.bfloat16)
        for n, i in enumerate(block):
            for r in range(sources):
                first = (n * sources + r) * rows
                o_refs[i][targets[i] ^ r, :, h * HEAD_DIM : (h + 1) * HEAD_DIM] = out[first : first + rows]

    scores = scores_of(works[0])
    for n, work in enumerate(works):
        following = scores_of(works[n + 1]) if n + 1 < len(works) else None
        finish(work, scores)
        scores = following


def attend(queries, keys_values, targets, planes):
    sources = len(queries)
    tokens, width = queries[0].shape
    rows = tokens // sources
    blocks = [kv.shape[0] // (2 * tokens) for kv in keys_values]
    key_count = sum(blocks) * tokens
    small = key_count <= 4096
    rows_step, step_width = (2, width) if small else (1, HEAD_DIM)
    score_bytes = rows_step * tokens * key_count * 4
    limit = 8 * key_count * step_width + 3 * score_bytes + 6 * 1024 * 1024
    return pl.pallas_call(
        functools.partial(
            attend_kernel,
            sources=sources,
            planes=planes,
            blocks=blocks,
            part=tokens,
            targets=targets,
            rows_step=rows_step,
        ),
        grid=(width // step_width,),
        in_specs=[pl.BlockSpec((tokens, step_width), lambda h: (0, h))] * sources
        + [pl.BlockSpec((kv.shape[0], step_width), lambda h: (0, h)) for kv in keys_values],
        out_specs=[pl.BlockSpec((sources, rows, step_width), lambda h: (0, 0, h))] * len(targets),
        out_shape=[jax.ShapeDtypeStruct((sources, rows, width), jnp.bfloat16)] * len(targets),
        compiler_params=pltpu.CompilerParams(vmem_limit_bytes=min(limit, 60 * 1024 * 1024)),
    )(*queries, *keys_values)


def projection_of(o_refs, w_refs, lined):
    tokens = lined.shape[0]
    first = 0
    for o_ref in o_refs:
        width = o_ref.shape[2]
        lined[:, first : first + width] = o_ref[...].reshape(tokens, width)
        first += width
    weights = jnp.concatenate([w[...] for w in w_refs], axis=0)
    return jnp.dot(lined[...], weights, preferred_element_type=jnp.float32)


def projection_specs(taken, tile, group_heads):
    whole = [pl.BlockSpec(o.shape, lambda i, *_: (0, 0, 0)) for _, _, o in taken]
    heads = [(t, low + n) for t, low, o in taken for n in range(o.shape[2] // HEAD_DIM)]
    return whole + [
        pl.BlockSpec(
            (HEAD_DIM, tile), lambda i, where, t=t, h=h: ((where[0] ^ t) * group_heads + h, i)
        )
        for t, h in heads
    ]


def project_kernel(where_ref, *refs, count):
    out_ref, lined = refs[-2:]
    out_ref[...] = projection_of(refs[:count], refs[count:-2], lined)


def project(where, taken, w_out, tile):
    sources, rows, _ = taken[0][2].shape
    tokens = sources * rows
    depth = sum(o.shape[2] for _, _, o in taken)
    inner, features = w_out.shape
    return pl.pallas_call(
        functools.partial(project_kernel, count=len(taken)),
        grid_spec=pltpu.PrefetchScalarGridSpec(
            num_scalar_prefetch=1,
            grid=(features // tile,),
            in_specs=projection_specs(taken, tile, inner // HEAD_DIM // HEAD_GROUPS),
            out_specs=pl.BlockSpec((None, tokens, tile), lambda i, *_: (i, 0, 0)),
            scratch_shapes=[pltpu.VMEM((tokens, depth), jnp.bfloat16)],
        ),
        out_shape=jax.ShapeDtypeStruct((features // tile, tokens, tile), jnp.float32),
        compiler_params=pltpu.CompilerParams(vmem_limit_bytes=VMEM_LIMIT),
    )(where, *[o for _, _, o in taken], *[w_out] * (depth // HEAD_DIM))


def final_kernel(where_ref, *refs, count, planes, rows_dev):
    partial_ref, scale_ref, shift_ref, w_final_ref, even_ref, odd_ref, lined, projected = refs[-8:]
    step = pl.program_id(0)
    heads_at, plane_at = where_ref[0], where_ref[1]
    tokens = lined.shape[0]
    tile = partial_ref.shape[1]
    projected[step] = partial_ref[...] + projection_of(refs[:count], refs[count:-8], lined)

    @pl.when(step == pl.num_programs(0) - 1)
    def _():
        steps = projected.shape[0]
        features = steps * tile
        total = projected[0]
        for i in range(1, steps):
            total = total + projected[i]
        mean = jnp.sum(total, axis=1, keepdims=True) * (1.0 / features)
        squares = None
        for i in range(steps):
            centered = projected[i] - mean
            squares = centered * centered if squares is None else squares + centered * centered
        variance = jnp.sum(squares, axis=1, keepdims=True) * (1.0 / features)
        inverse = lax.rsqrt(variance + 1e-06)
        patches = None
        for i in range(steps):
            lanes = slice(i * tile, (i + 1) * tile)
            normed = (projected[i] - mean) * inverse * (1.0 + scale_ref[:, lanes]) + shift_ref[:, lanes]
            part = lax.dot_general(
                normed.astype(jnp.bfloat16),
                w_final_ref[:, lanes],
                (((1,), (1,)), ((), ())),
                preferred_element_type=jnp.float32,
            )
            patches = part if patches is None else patches + part
        patches = patches.astype(jnp.bfloat16)
        channels = patches.shape[1]
        half = channels // 2
        source = lax.broadcasted_iota(jnp.int32, (channels, channels), 0)
        target = lax.broadcasted_iota(jnp.int32, (channels, channels), 1)
        q, p, c = target // half, (target // LATENT_CH) % 2, target % LATENT_CH
        lane_order = (source == 4 * c + 2 * p + q).astype(jnp.bfloat16)
        to = lax.broadcasted_iota(jnp.int32, (tokens, tokens), 0)
        at = lax.broadcasted_iota(jnp.int32, (tokens, tokens), 1)
        share = planes * rows_dev
        place = ((to // share) ^ heads_at) * share
        place = place + (((to % share) // rows_dev) ^ plane_at) * rows_dev + to % rows_dev
        row_order = (at == place).astype(jnp.bfloat16)
        cells = jnp.dot(patches, lane_order, preferred_element_type=jnp.float32)
        cells = jnp.dot(row_order, cells.astype(jnp.bfloat16), preferred_element_type=jnp.float32)
        cells = cells.astype(jnp.bfloat16)
        even_ref[...] = cells[:, :half]
        odd_ref[...] = cells[:, half:]


def final_layer(where, taken, partial, w_out, scale_mod, shift_mod, w_final, rows_dev, planes):
    depth = sum(o.shape[2] for _, _, o in taken)
    inner, features = w_out.shape
    steps, tokens, tile = partial.shape
    channels = w_final.shape[1]
    whole = lambda shape: pl.BlockSpec(shape, lambda i, *_: (0,) * len(shape))
    result = jax.ShapeDtypeStruct((tokens, channels // 2), jnp.bfloat16)
    return pl.pallas_call(
        functools.partial(final_kernel, count=len(taken), planes=planes, rows_dev=rows_dev),
        grid_spec=pltpu.PrefetchScalarGridSpec(
            num_scalar_prefetch=1,
            grid=(steps,),
            in_specs=projection_specs(taken, tile, inner // HEAD_DIM // HEAD_GROUPS)
            + [
                pl.BlockSpec((None, tokens, tile), lambda i, *_: (i, 0, 0)),
                whole((1, features)),
                whole((1, features)),
                whole((channels, features)),
            ],
            out_specs=[whole((tokens, channels // 2))] * 2,
            scratch_shapes=[
                pltpu.VMEM((tokens, depth), jnp.bfloat16),
                pltpu.VMEM((steps, tokens, tile), jnp.float32),
            ],
        ),
        out_shape=[result] * 2,
        compiler_params=pltpu.CompilerParams(vmem_limit_bytes=VMEM_LIMIT),
    )(
        where,
        *[o for _, _, o in taken],
        *[w_out] * (depth // HEAD_DIM),
        partial,
        scale_mod[None],
        shift_mod[None],
        w_final.T,
    )


def convolve_kernel(where_ref, even_ref, odd_ref, left_ref, right_ref, w_ref, bias_ref, out_ref, latent):
    frames, cols, _, ch = latent.shape
    rows = even_ref.shape[0] // frames
    height = 2 * rows
    even = even_ref[...].astype(jnp.float32)
    odd = odd_ref[...].astype(jnp.float32)
    left = jnp.where(where_ref[2] == 0, even, left_ref[...].astype(jnp.float32))
    right = jnp.where(where_ref[2] == where_ref[3] - 1, odd, right_ref[...].astype(jnp.float32))
    for x, cells in enumerate((left, even, odd, right)):
        for f in range(frames):
            own = cells[f * rows : (f + 1) * rows]
            for p in range(2):
                latent[f, x, pl.ds(8 + p, rows, stride=2), :] = own[:, p * ch : (p + 1) * ch]
            latent[f, x, 7:8, :] = own[:1, :ch]
            latent[f, x, 8 + height : 9 + height, :] = own[rows - 1 :, ch:]
    depth = 9 * ch
    for x in range(cols - 2):
        stacked = []
        for f in range(frames):
            taps = [latent[f, x + b, 7 + e : 7 + e + height, :] for b in range(3) for e in range(3)]
            stacked.append(jnp.concatenate(taps, axis=1).astype(jnp.bfloat16))
        stacked = [stacked[0]] * 2 + stacked
        acc = None
        for a in range(3):
            flat = jnp.concatenate(stacked[a : a + frames], axis=0)
            part = jnp.dot(
                flat, w_ref[a * depth : (a + 1) * depth, :], preferred_element_type=jnp.float32
            )
            acc = part if acc is None else acc + part
        acc = (acc + bias_ref[...]).astype(jnp.bfloat16)
        out_ref[:, x] = acc.reshape(frames, height, acc.shape[1])


def convolve(where, even, odd, left, right, conv_weight, conv_bias):
    rows = even.shape[0] // FRAMES
    channels = conv_weight.shape[1]
    smem = pl.BlockSpec(memory_space=pltpu.SMEM)
    vmem = pl.BlockSpec(memory_space=pltpu.VMEM)
    return pl.pallas_call(
        convolve_kernel,
        in_specs=[smem] + [vmem] * 6,
        out_specs=vmem,
        out_shape=jax.ShapeDtypeStruct((FRAMES, 2, 2 * rows, channels), jnp.bfloat16),
        scratch_shapes=[pltpu.VMEM((FRAMES, 4, 2 * rows + 16, LATENT_CH), jnp.float32)],
        compiler_params=pltpu.CompilerParams(vmem_limit_bytes=VMEM_LIMIT),
    )(where, even, odd, left, right, conv_weight, conv_bias[None])


def after(value, *others):
    return lax.optimization_barrier((value,) + others)[0]


def gather_plane(got, batch, both_parts, share):
    planes = lax.axis_size("plane")
    half, count = planes // 2, len(batch)
    kv_rows = both_parts * count
    crossed = []
    for d in range(2, planes, 2):
        sent = [got[r][:both_parts] for r in batch]
        sent += [got[r][both_parts + d * share : both_parts + (d + 2) * share] for r in batch]
        crossed.append(swap(jnp.concatenate(sent, axis=0), "plane", d))
    near = [[got[r][both_parts : both_parts + share] for r in batch]]
    far = [[got[r][both_parts + share : both_parts + 2 * share] for r in batch]]
    for x in crossed:
        firsts = [kv_rows + 2 * n * share for n in range(count)]
        near.append([x[first : first + share] for first in firsts])
        far.append([x[first + share : first + 2 * share] for first in firsts])
    mine = [got[r][:both_parts] for r in batch] + [x[:kv_rows] for x in crossed]
    mine = jnp.concatenate(mine + [q for pieces in far for q in pieces], axis=0)
    other = swap(mine, "plane", 1)
    asked = []
    for n in range(count):
        firsts = [kv_rows * half + (k * count + n) * share for k in range(half)]
        asked.append(
            jnp.concatenate(
                [pieces[n] for pieces in near] + [other[first : first + share] for first in firsts],
                axis=0,
            )
        )
    return [mine, other], asked


def shards(queries, keys, values, w_out, shift_mod, scale_mod, w_final, conv_weight, conv_bias):
    groups = lax.axis_size("heads")
    planes = lax.axis_size("plane")
    heads_at = lax.axis_index("heads")
    plane_at = lax.axis_index("plane")
    devices = groups * planes
    tokens = queries.shape[0]
    rows_dev = tokens // devices
    both_parts, share = 2 * tokens, tokens // planes
    where = jnp.stack(
        [heads_at, plane_at, heads_at * planes + plane_at, jnp.int32(devices)]
    ).astype(jnp.int32)

    cuts = [(r, low, high) for low, high in CHUNKS for r in (2, 1, 3, 0)]
    made = dict(zip(cuts, bundles(queries, keys, values, groups, planes, cuts)))
    made = {cut: swap(made[cut], "heads", cut[0]) if cut[0] else made[cut] for cut in cuts}

    chunks = []
    for low, high in CHUNKS:
        got = [made[r, low, high] for r in range(groups)]
        keys_values, asked = [], []
        for batch in ((0, 1), (2,), (3,)):
            kv, q = gather_plane(got, batch, both_parts, share)
            keys_values += kv
            asked += q
        taken = []
        for targets in ((3, 2), (1, 0)):
            for t, o in zip(targets, attend(asked, keys_values, targets, planes)):
                taken.append((t, low, o if t == 0 else swap(o, "heads", t)))
        chunks.append(taken)

    if len(chunks) == 1:
        near, far = [chunks[0][n] for n in (3, 0)], [chunks[0][n] for n in (1, 2)]
    else:
        near, far = sum(chunks[:-1], []), chunks[-1]
    partial = project(where, near, w_out, 512)
    even, odd = final_layer(
        where, far, partial, w_out, scale_mod, shift_mod, w_final, rows_dev, planes
    )
    both = ("heads", "plane")
    left = lax.ppermute(odd, both, [(i, i + 1) for i in range(devices - 1)])
    right = lax.ppermute(even, both, [(i + 1, i) for i in range(devices - 1)])
    return convolve(where, even, odd, left, right, conv_weight, conv_bias)


def solution(mesh):
    groups, seq = mesh.devices.shape
    split = Mesh(
        mesh.devices.reshape(groups, HEAD_GROUPS, seq // HEAD_GROUPS), ("groups", "heads", "plane")
    )
    by_token = P(("groups", "heads", "plane"), None)
    placed = (by_token, by_token, by_token, P(), P("groups"), P("groups"), P(), P(), P())
    return jax.shard_map(
        shards,
        mesh=split,
        in_specs=placed,
        out_specs=P("groups", ("heads", "plane"), None, None),
        check_vma=False,
    )
```

```python
import functools
import math

import jax
import jax.numpy as jnp
from jax import lax
from jax.experimental import pallas as pl
from jax.experimental.pallas import tpu as pltpu
from jax.sharding import Mesh
from jax.sharding import PartitionSpec as P

HEAD_DIM = 128
HEAD_GROUPS = 4
LATENT_CH = 16
FRAMES = 4
VMEM_LIMIT = 16 * 1024 * 1024
CHUNKS = ((0, 3),)
EXP2_SCALE = math.log2(math.e) / math.sqrt(HEAD_DIM)


def swap(source, axis, distance):
    count = lax.axis_size(axis)
    return lax.ppermute(source, axis, [(i, i ^ distance) for i in range(count)])


def attend_kernel(*refs, sources, planes, blocks, part, targets, rows_step):
    q_refs = refs[:sources]
    kv_refs = refs[sources : sources + len(blocks)]
    o_refs = refs[sources + len(blocks) :]
    tokens, width = q_refs[0].shape
    rows = tokens // sources
    rows_dev = rows // planes
    to = lax.broadcasted_iota(jnp.int32, (tokens, tokens), 0)
    at = lax.broadcasted_iota(jnp.int32, (tokens, tokens), 1)
    t, j, row = to // rows, (to // rows_dev) % planes, to % rows_dev
    place = ((j % 2) * (planes // 2) + j // 2) * rows + t * rows_dev + row
    order = (at == place).astype(jnp.bfloat16)
    asked = [
        jnp.dot(order, q[...], preferred_element_type=jnp.float32).astype(jnp.bfloat16) for q in q_refs
    ]
    works = [
        (h, range(first, min(first + rows_step, len(targets))))
        for h in range(width // HEAD_DIM)
        for first in range(0, len(targets), rows_step)
    ]

    def taken(ref, count, h, which):
        cut = ref[: count * 2 * part, h * HEAD_DIM : (h + 1) * HEAD_DIM]
        return cut.reshape(count, 2, part, HEAD_DIM)[:, which].reshape(count * part, HEAD_DIM)

    def scores_of(work):
        h, block = work
        lanes = slice(h * HEAD_DIM, (h + 1) * HEAD_DIM)
        query = jnp.concatenate(
            [q[targets[i] * rows : (targets[i] + 1) * rows, lanes] for i in block for q in asked], axis=0
        )
        return [
            lax.dot_general(
                query,
                taken(kv, count, h, 0),
                (((1,), (1,)), ((), ())),
                preferred_element_type=jnp.float32,
            )
            for kv, count in zip(kv_refs, blocks)
        ]

    def finish(work, scores):
        h, block = work
        peak = functools.reduce(jnp.maximum, [jnp.max(s, axis=1, keepdims=True) for s in scores])
        peak = peak * EXP2_SCALE
        summed = None
        for s, kv, count in zip(scores, kv_refs, blocks):
            weights = jnp.exp2(s * EXP2_SCALE - peak).astype(jnp.bfloat16)
            value = taken(kv, count, h, 1)
            value = jnp.concatenate([value, jnp.ones_like(value)], axis=1)
            product = jnp.dot(weights, value, preferred_element_type=jnp.float32)
            summed = product if summed is None else summed + product
        out = (summed[:, :HEAD_DIM] / summed[:, HEAD_DIM:]).astype(jnp.bfloat16)
        for n, i in enumerate(block):
            for r in range(sources):
                first = (n * sources + r) * rows
                o_refs[i][targets[i] ^ r, :, h * HEAD_DIM : (h + 1) * HEAD_DIM] = out[first : first + rows]

    scores = scores_of(works[0])
    for n, work in enumerate(works):
        following = scores_of(works[n + 1]) if n + 1 < len(works) else None
        finish(work, scores)
        scores = following


def attend(queries, keys_values, targets, planes):
    sources = len(queries)
    tokens, width = queries[0].shape
    rows = tokens // sources
    blocks = [kv.shape[0] // (2 * tokens) for kv in keys_values]
    key_count = sum(blocks) * tokens
    small = key_count <= 4096
    rows_step, step_width = (2, width) if small else (1, HEAD_DIM)
    score_bytes = rows_step * tokens * key_count * 4
    limit = 8 * key_count * step_width + 3 * score_bytes + 6 * 1024 * 1024
    return pl.pallas_call(
        functools.partial(
            attend_kernel,
            sources=sources,
            planes=planes,
            blocks=blocks,
            part=tokens,
            targets=targets,
            rows_step=rows_step,
        ),
        grid=(width // step_width,),
        in_specs=[pl.BlockSpec((tokens, step_width), lambda h: (0, h))] * sources
        + [pl.BlockSpec((kv.shape[0], step_width), lambda h: (0, h)) for kv in keys_values],
        out_specs=[pl.BlockSpec((sources, rows, step_width), lambda h: (0, 0, h))] * len(targets),
        out_shape=[jax.ShapeDtypeStruct((sources, rows, width), jnp.bfloat16)] * len(targets),
        compiler_params=pltpu.CompilerParams(vmem_limit_bytes=min(limit, 60 * 1024 * 1024)),
    )(*queries, *keys_values)


def projection_of(o_refs, w_refs, lined):
    tokens = lined.shape[0]
    first = 0
    for o_ref in o_refs:
        width = o_ref.shape[2]
        lined[:, first : first + width] = o_ref[...].reshape(tokens, width)
        first += width
    weights = jnp.concatenate([w[...] for w in w_refs], axis=0)
    return jnp.dot(lined[...], weights, preferred_element_type=jnp.float32)


def projection_specs(taken, tile, group_heads):
    whole = [pl.BlockSpec(o.shape, lambda i, *_: (0, 0, 0)) for _, _, o in taken]
    heads = [(t, low + n) for t, low, o in taken for n in range(o.shape[2] // HEAD_DIM)]
    return whole + [
        pl.BlockSpec(
            (HEAD_DIM, tile), lambda i, where, t=t, h=h: ((where[0] ^ t) * group_heads + h, i)
        )
        for t, h in heads
    ]


def project_kernel(where_ref, *refs, count):
    out_ref, lined = refs[-2:]
    out_ref[...] = projection_of(refs[:count], refs[count:-2], lined)


def project(where, taken, w_out, tile):
    sources, rows, _ = taken[0][2].shape
    tokens = sources * rows
    depth = sum(o.shape[2] for _, _, o in taken)
    inner, features = w_out.shape
    return pl.pallas_call(
        functools.partial(project_kernel, count=len(taken)),
        grid_spec=pltpu.PrefetchScalarGridSpec(
            num_scalar_prefetch=1,
            grid=(features // tile,),
            in_specs=projection_specs(taken, tile, inner // HEAD_DIM // HEAD_GROUPS),
            out_specs=pl.BlockSpec((None, tokens, tile), lambda i, *_: (i, 0, 0)),
            scratch_shapes=[pltpu.VMEM((tokens, depth), jnp.bfloat16)],
        ),
        out_shape=jax.ShapeDtypeStruct((features // tile, tokens, tile), jnp.float32),
        compiler_params=pltpu.CompilerParams(vmem_limit_bytes=VMEM_LIMIT),
    )(where, *[o for _, _, o in taken], *[w_out] * (depth // HEAD_DIM))


def final_kernel(where_ref, *refs, count, planes, rows_dev):
    partial_ref, scale_ref, shift_ref, w_final_ref, even_ref, odd_ref, lined, projected = refs[-8:]
    step = pl.program_id(0)
    heads_at, plane_at = where_ref[0], where_ref[1]
    tokens = lined.shape[0]
    tile = partial_ref.shape[1]
    projected[step] = partial_ref[...] + projection_of(refs[:count], refs[count:-8], lined)

    @pl.when(step == pl.num_programs(0) - 1)
    def _():
        steps = projected.shape[0]
        features = steps * tile
        total = projected[0]
        for i in range(1, steps):
            total = total + projected[i]
        mean = jnp.sum(total, axis=1, keepdims=True) * (1.0 / features)
        squares = None
        for i in range(steps):
            centered = projected[i] - mean
            squares = centered * centered if squares is None else squares + centered * centered
        variance = jnp.sum(squares, axis=1, keepdims=True) * (1.0 / features)
        inverse = lax.rsqrt(variance + 1e-06)
        patches = None
        for i in range(steps):
            lanes = slice(i * tile, (i + 1) * tile)
            normed = (projected[i] - mean) * inverse * (1.0 + scale_ref[:, lanes]) + shift_ref[:, lanes]
            part = lax.dot_general(
                normed.astype(jnp.bfloat16),
                w_final_ref[:, lanes],
                (((1,), (1,)), ((), ())),
                preferred_element_type=jnp.float32,
            )
            patches = part if patches is None else patches + part
        patches = patches.astype(jnp.bfloat16)
        channels = patches.shape[1]
        half = channels // 2
        source = lax.broadcasted_iota(jnp.int32, (channels, channels), 0)
        target = lax.broadcasted_iota(jnp.int32, (channels, channels), 1)
        q, p, c = target // half, (target // LATENT_CH) % 2, target % LATENT_CH
        lane_order = (source == 4 * c + 2 * p + q).astype(jnp.bfloat16)
        to = lax.broadcasted_iota(jnp.int32, (tokens, tokens), 0)
        at = lax.broadcasted_iota(jnp.int32, (tokens, tokens), 1)
        share = planes * rows_dev
        place = ((to // share) ^ heads_at) * share
        place = place + (((to % share) // rows_dev) ^ plane_at) * rows_dev + to % rows_dev
        row_order = (at == place).astype(jnp.bfloat16)
        cells = jnp.dot(patches, lane_order, preferred_element_type=jnp.float32)
        cells = jnp.dot(row_order, cells.astype(jnp.bfloat16), preferred_element_type=jnp.float32)
        cells = cells.astype(jnp.bfloat16)
        even_ref[...] = cells[:, :half]
        odd_ref[...] = cells[:, half:]


def final_layer(where, taken, partial, w_out, scale_mod, shift_mod, w_final, rows_dev, planes):
    depth = sum(o.shape[2] for _, _, o in taken)
    inner, features = w_out.shape
    steps, tokens, tile = partial.shape
    channels = w_final.shape[1]
    whole = lambda shape: pl.BlockSpec(shape, lambda i, *_: (0,) * len(shape))
    result = jax.ShapeDtypeStruct((tokens, channels // 2), jnp.bfloat16)
    return pl.pallas_call(
        functools.partial(final_kernel, count=len(taken), planes=planes, rows_dev=rows_dev),
        grid_spec=pltpu.PrefetchScalarGridSpec(
            num_scalar_prefetch=1,
            grid=(steps,),
            in_specs=projection_specs(taken, tile, inner // HEAD_DIM // HEAD_GROUPS)
            + [
                pl.BlockSpec((None, tokens, tile), lambda i, *_: (i, 0, 0)),
                whole((1, features)),
                whole((1, features)),
                whole((channels, features)),
            ],
            out_specs=[whole((tokens, channels // 2))] * 2,
            scratch_shapes=[
                pltpu.VMEM((tokens, depth), jnp.bfloat16),
                pltpu.VMEM((steps, tokens, tile), jnp.float32),
            ],
        ),
        out_shape=[result] * 2,
        compiler_params=pltpu.CompilerParams(vmem_limit_bytes=VMEM_LIMIT),
    )(
        where,
        *[o for _, _, o in taken],
        *[w_out] * (depth // HEAD_DIM),
        partial,
        scale_mod[None],
        shift_mod[None],
        w_final.T,
    )


def convolve_kernel(where_ref, even_ref, odd_ref, left_ref, right_ref, w_ref, bias_ref, out_ref, latent):
    frames, cols, _, ch = latent.shape
    rows = even_ref.shape[0] // frames
    height = 2 * rows
    even = even_ref[...].astype(jnp.float32)
    odd = odd_ref[...].astype(jnp.float32)
    left = jnp.where(where_ref[2] == 0, even, left_ref[...].astype(jnp.float32))
    right = jnp.where(where_ref[2] == where_ref[3] - 1, odd, right_ref[...].astype(jnp.float32))
    for x, cells in enumerate((left, even, odd, right)):
        for f in range(frames):
            own = cells[f * rows : (f + 1) * rows]
            for p in range(2):
                latent[f, x, pl.ds(8 + p, rows, stride=2), :] = own[:, p * ch : (p + 1) * ch]
            latent[f, x, 7:8, :] = own[:1, :ch]
            latent[f, x, 8 + height : 9 + height, :] = own[rows - 1 :, ch:]
    depth = 9 * ch
    for x in range(cols - 2):
        stacked = []
        for f in range(frames):
            taps = [latent[f, x + b, 7 + e : 7 + e + height, :] for b in range(3) for e in range(3)]
            stacked.append(jnp.concatenate(taps, axis=1).astype(jnp.bfloat16))
        stacked = [stacked[0]] * 2 + stacked
        acc = None
        for a in range(3):
            flat = jnp.concatenate(stacked[a : a + frames], axis=0)
            part = jnp.dot(
                flat, w_ref[a * depth : (a + 1) * depth, :], preferred_element_type=jnp.float32
            )
            acc = part if acc is None else acc + part
        acc = (acc + bias_ref[...]).astype(jnp.bfloat16)
        out_ref[:, x] = acc.reshape(frames, height, acc.shape[1])


def convolve(where, even, odd, left, right, conv_weight, conv_bias):
    rows = even.shape[0] // FRAMES
    channels = conv_weight.shape[1]
    smem = pl.BlockSpec(memory_space=pltpu.SMEM)
    vmem = pl.BlockSpec(memory_space=pltpu.VMEM)
    return pl.pallas_call(
        convolve_kernel,
        in_specs=[smem] + [vmem] * 6,
        out_specs=vmem,
        out_shape=jax.ShapeDtypeStruct((FRAMES, 2, 2 * rows, channels), jnp.bfloat16),
        scratch_shapes=[pltpu.VMEM((FRAMES, 4, 2 * rows + 16, LATENT_CH), jnp.float32)],
        compiler_params=pltpu.CompilerParams(vmem_limit_bytes=VMEM_LIMIT),
    )(where, even, odd, left, right, conv_weight, conv_bias[None])


def after(value, *others):
    return lax.optimization_barrier((value,) + others)[0]


def gather_plane(got, batch, both_parts, share, waits):
    planes = lax.axis_size("plane")
    half, count = planes // 2, len(batch)
    kv_rows = both_parts * count
    crossed = []
    for d in range(2, planes, 2):
        sent = [got[r][:both_parts] for r in batch]
        sent += [got[r][both_parts + d * share : both_parts + (d + 2) * share] for r in batch]
        crossed.append(swap(jnp.concatenate(sent, axis=0), "plane", d))
    near = [[got[r][both_parts : both_parts + share] for r in batch]]
    far = [[got[r][both_parts + share : both_parts + 2 * share] for r in batch]]
    for x in crossed:
        firsts = [kv_rows + 2 * n * share for n in range(count)]
        near.append([x[first : first + share] for first in firsts])
        far.append([x[first + share : first + 2 * share] for first in firsts])
    mine = [got[r][:both_parts] for r in batch] + [x[:kv_rows] for x in crossed]
    mine = jnp.concatenate(mine + [q for pieces in far for q in pieces], axis=0)
    if waits and batch == (3,):
        mine = after(mine, *waits)
    other = swap(mine, "plane", 1)
    asked = []
    for n in range(count):
        firsts = [kv_rows * half + (k * count + n) * share for k in range(half)]
        asked.append(
            jnp.concatenate(
                [pieces[n] for pieces in near] + [other[first : first + share] for first in firsts],
                axis=0,
            )
        )
    return [mine, other], asked


def shards(queries, keys, values, w_out, shift_mod, scale_mod, w_final, conv_weight, conv_bias):
    groups = lax.axis_size("heads")
    planes = lax.axis_size("plane")
    heads_at = lax.axis_index("heads")
    plane_at = lax.axis_index("plane")
    devices = groups * planes
    tokens = queries.shape[0]
    rows_dev = tokens // devices
    both_parts, share = 2 * tokens, tokens // planes
    group_heads = queries.shape[1] // HEAD_DIM // groups
    where = jnp.stack(
        [heads_at, plane_at, heads_at * planes + plane_at, jnp.int32(devices)]
    ).astype(jnp.int32)

    to = lax.broadcasted_iota(jnp.int32, (tokens, tokens), 0)
    at = lax.broadcasted_iota(jnp.int32, (tokens, tokens), 1)
    j, t, row = to // (groups * rows_dev), (to // rows_dev) % groups, to % rows_dev

    def bundle(r, low, high):
        first = (heads_at ^ r) * (HEAD_DIM * group_heads) + low * HEAD_DIM
        cut = [
            lax.dynamic_slice_in_dim(source, first, (high - low) * HEAD_DIM, axis=1)
            for source in (keys, values, queries)
        ]
        place = row * devices + (t ^ (r ^ heads_at)) * planes + (j ^ plane_at)
        order = (at == place).astype(jnp.bfloat16)
        cut[2] = jnp.dot(order, cut[2], preferred_element_type=jnp.float32).astype(jnp.bfloat16)
        return jnp.concatenate(cut, axis=0)

    chunks, begun, done = [], None, None
    for low, high in CHUNKS:
        got = [bundle(r, low, high) for r in range(groups)]
        if begun is not None:
            got = [after(b, begun) for b in got]
        got = [swap(b, "heads", r) if r else b for r, b in enumerate(got)]
        begun = got[1]
        keys_values, asked = [], []
        for batch in ((0, 1), (2,), (3,)):
            kv, q = gather_plane(got, batch, both_parts, share, done)
            keys_values += kv
            asked += q
        taken, done = [], []
        for targets in ((3, 2), (1, 0)):
            for target, o in zip(targets, attend(asked, keys_values, targets, planes)):
                done.append(o)
                taken.append((target, low, o if target == 0 else swap(o, "heads", target)))
        chunks.append(taken)

    if len(chunks) == 1:
        near, far = [chunks[0][n] for n in (3, 0)], [chunks[0][n] for n in (1, 2)]
    else:
        near, far = sum(chunks[:-1], []), chunks[-1]
    partial = project(where, near, w_out, 512)
    even, odd = final_layer(
        where, far, partial, w_out, scale_mod, shift_mod, w_final, rows_dev, planes
    )
    both = ("heads", "plane")
    left = lax.ppermute(odd, both, [(i, i + 1) for i in range(devices - 1)])
    right = lax.ppermute(even, both, [(i + 1, i) for i in range(devices - 1)])
    return convolve(where, even, odd, left, right, conv_weight, conv_bias)


def solution(mesh):
    groups, seq = mesh.devices.shape
    split = Mesh(
        mesh.devices.reshape(groups, HEAD_GROUPS, seq // HEAD_GROUPS), ("groups", "heads", "plane")
    )
    by_token = P(("groups", "heads", "plane"), None)
    placed = (by_token, by_token, by_token, P(), P("groups"), P("groups"), P(), P(), P())
    return jax.shard_map(
        shards,
        mesh=split,
        in_specs=placed,
        out_specs=P("groups", ("heads", "plane"), None, None),
        check_vma=False,
    )
```

```python
import functools
import math

import jax
import jax.numpy as jnp
from jax import lax
from jax.experimental import pallas as pl
from jax.experimental.pallas import tpu as pltpu
from jax.sharding import Mesh
from jax.sharding import PartitionSpec as P

HEAD_DIM = 128
HEAD_GROUPS = 4
LATENT_CH = 16
FRAMES = 4
VMEM_LIMIT = 16 * 1024 * 1024
CHUNKS = ((0, 3),)

EXP2_SCALE = math.log2(math.e) / math.sqrt(HEAD_DIM)


def swap(source, axis, distance):
    count = lax.axis_size(axis)
    return lax.ppermute(source, axis, [(i, i ^ distance) for i in range(count)])


def attend_kernel(*refs, planes, tokens, sources, targets, rows_step):
    held = [refs[4 * r : 4 * r + 4] for r in range(sources)]
    o_refs = refs[4 * sources :]
    width = o_refs[0].shape[2]
    rows = tokens // sources
    rows_dev = rows // planes
    share = tokens // planes
    stride = 2 * tokens + 2 * share
    to = lax.broadcasted_iota(jnp.int32, (tokens, tokens), 0)
    at = lax.broadcasted_iota(jnp.int32, (tokens, tokens), 1)
    t, j, row = to // rows, (to // rows_dev) % planes, to % rows_dev
    place = ((j % 2) * (planes // 2) + j // 2) * rows + t * rows_dev + row
    order = (at == place).astype(jnp.bfloat16)
    passed = [k * stride for k in range(planes // 2 - 1)]
    asked = []
    for own, crossed, other, other_crossed in held:
        pieces = [own[:share]]
        pieces += [crossed[at_row + 2 * tokens + share : at_row + stride] for at_row in passed]
        pieces += [other[share : 2 * share]]
        pieces += [other_crossed[at_row + 2 * tokens : at_row + 2 * tokens + share] for at_row in passed]
        mixed = jnp.dot(order, jnp.concatenate(pieces, axis=0), preferred_element_type=jnp.float32)
        asked.append(mixed.astype(jnp.bfloat16))
    parts = []
    for own, crossed, other, other_crossed in held:
        for whole, several in ((own, crossed), (other, other_crossed)):
            parts += [(whole, 2 * share)] + [(several, at_row) for at_row in passed]
    parts = [parts[n : n + 4] for n in range(0, len(parts), 4)]
    works = [
        (h, range(first, min(first + rows_step, len(targets))))
        for h in range(width // HEAD_DIM)
        for first in range(0, len(targets), rows_step)
    ]

    def taken(part, h, which):
        lanes = slice(h * HEAD_DIM, (h + 1) * HEAD_DIM)
        firsts = [(ref, first + which * tokens) for ref, first in part]
        return jnp.concatenate([ref[first : first + tokens, lanes] for ref, first in firsts], axis=0)

    def scores_of(work):
        h, block = work
        lanes = slice(h * HEAD_DIM, (h + 1) * HEAD_DIM)
        query = jnp.concatenate(
            [q[targets[i] * rows : (targets[i] + 1) * rows, lanes] for i in block for q in asked], axis=0
        )
        return [
            lax.dot_general(
                query,
                taken(part, h, 0),
                (((1,), (1,)), ((), ())),
                preferred_element_type=jnp.float32,
            )
            for part in parts
        ]

    def finish(work, scores):
        h, block = work
        peak = functools.reduce(jnp.maximum, [jnp.max(s, axis=1, keepdims=True) for s in scores])
        peak = peak * EXP2_SCALE
        summed = None
        for s, part in zip(scores, parts):
            weights = jnp.exp2(s * EXP2_SCALE - peak).astype(jnp.bfloat16)
            value = taken(part, h, 1)
            value = jnp.concatenate([value, jnp.ones_like(value)], axis=1)
            product = jnp.dot(weights, value, preferred_element_type=jnp.float32)
            summed = product if summed is None else summed + product
        out = (summed[:, :HEAD_DIM] / summed[:, HEAD_DIM:]).astype(jnp.bfloat16)
        for n, i in enumerate(block):
            for r in range(sources):
                first = (n * sources + r) * rows
                o_refs[i][targets[i] ^ r, :, h * HEAD_DIM : (h + 1) * HEAD_DIM] = out[first : first + rows]

    scores = scores_of(works[0])
    for n, work in enumerate(works):
        following = scores_of(works[n + 1]) if n + 1 < len(works) else None
        finish(work, scores)
        scores = following


def attend(held, targets, tokens, planes):
    width = held[0].shape[1]
    sources = len(held) // 4
    rows = tokens // sources
    key_count = sources * planes * tokens
    small = key_count <= 4096
    rows_step, step_width = (2, width) if small else (1, HEAD_DIM)
    score_bytes = rows_step * tokens * key_count * 4
    limit = 2 * key_count * step_width * (2 if small else 8) + 3 * score_bytes + 4 * 1024 * 1024
    return pl.pallas_call(
        functools.partial(
            attend_kernel,
            planes=planes,
            tokens=tokens,
            sources=sources,
            targets=targets,
            rows_step=rows_step,
        ),
        grid=(width // step_width,),
        in_specs=[pl.BlockSpec((array.shape[0], step_width), lambda h: (0, h)) for array in held],
        out_specs=[pl.BlockSpec((sources, rows, step_width), lambda h: (0, 0, h))] * len(targets),
        out_shape=[jax.ShapeDtypeStruct((sources, rows, width), jnp.bfloat16)] * len(targets),
        compiler_params=pltpu.CompilerParams(vmem_limit_bytes=min(limit, 60 * 1024 * 1024)),
    )(*held)


def projection_of(o_refs, w_refs, lined):
    tokens = lined.shape[0]
    first = 0
    for o_ref in o_refs:
        width = o_ref.shape[2]
        lined[:, first : first + width] = o_ref[...].reshape(tokens, width)
        first += width
    weights = jnp.concatenate([w[...] for w in w_refs], axis=0)
    return jnp.dot(lined[...], weights, preferred_element_type=jnp.float32)


def row_blocks(taken, group_heads):
    blocks = []
    for target, low, o in taken:
        heads = o.shape[2] // HEAD_DIM
        step = heads if group_heads % heads == 0 and low % heads == 0 else 1
        blocks += [
            (target, (low + n) // step, step, group_heads // step) for n in range(0, heads, step)
        ]
    return blocks


def projection_specs(taken, tile, group_heads):
    whole = [pl.BlockSpec(o.shape, lambda i, *_: (0, 0, 0)) for _, _, o in taken]
    return whole + [
        pl.BlockSpec(
            (HEAD_DIM * step, tile),
            lambda i, where, target=target, block=block, count=count: (
                (where[0] ^ target) * count + block,
                i,
            ),
        )
        for target, block, step, count in row_blocks(taken, group_heads)
    ]


def project_kernel(where_ref, *refs, count):
    out_ref, lined = refs[-2:]
    out_ref[...] = projection_of(refs[:count], refs[count:-2], lined)


def project(where, taken, w_out, tile):
    sources, rows, _ = taken[0][2].shape
    tokens = sources * rows
    depth = sum(o.shape[2] for _, _, o in taken)
    inner, features = w_out.shape
    return pl.pallas_call(
        functools.partial(project_kernel, count=len(taken)),
        grid_spec=pltpu.PrefetchScalarGridSpec(
            num_scalar_prefetch=1,
            grid=(features // tile,),
            in_specs=projection_specs(taken, tile, inner // HEAD_DIM // HEAD_GROUPS),
            out_specs=pl.BlockSpec((None, tokens, tile), lambda i, *_: (i, 0, 0)),
            scratch_shapes=[pltpu.VMEM((tokens, depth), jnp.bfloat16)],
        ),
        out_shape=jax.ShapeDtypeStruct((features // tile, tokens, tile), jnp.float32),
        compiler_params=pltpu.CompilerParams(vmem_limit_bytes=VMEM_LIMIT),
    )(where, *[o for _, _, o in taken], *[w_out] * len(row_blocks(taken, inner // HEAD_DIM // HEAD_GROUPS)))


def final_kernel(where_ref, *refs, count, planes, rows_dev):
    partial_ref, scale_ref, shift_ref, w_final_ref, even_ref, odd_ref, lined, projected = refs[-8:]
    step = pl.program_id(0)
    heads_at, plane_at = where_ref[0], where_ref[1]
    tokens = lined.shape[0]
    tile = partial_ref.shape[1]
    projected[step] = partial_ref[...] + projection_of(refs[:count], refs[count:-8], lined)

    @pl.when(step == pl.num_programs(0) - 1)
    def _():
        steps = projected.shape[0]
        features = steps * tile
        total = projected[0]
        for i in range(1, steps):
            total = total + projected[i]
        mean = jnp.sum(total, axis=1, keepdims=True) * (1.0 / features)
        squares = None
        for i in range(steps):
            centered = projected[i] - mean
            squares = centered * centered if squares is None else squares + centered * centered
        variance = jnp.sum(squares, axis=1, keepdims=True) * (1.0 / features)
        inverse = lax.rsqrt(variance + 1e-06)
        patches = None
        for i in range(steps):
            lanes = slice(i * tile, (i + 1) * tile)
            normed = (projected[i] - mean) * inverse * (1.0 + scale_ref[:, lanes]) + shift_ref[:, lanes]
            part = lax.dot_general(
                normed.astype(jnp.bfloat16),
                w_final_ref[:, lanes],
                (((1,), (1,)), ((), ())),
                preferred_element_type=jnp.float32,
            )
            patches = part if patches is None else patches + part
        patches = patches.astype(jnp.bfloat16)
        channels = patches.shape[1]
        half = channels // 2
        source = lax.broadcasted_iota(jnp.int32, (channels, channels), 0)
        target = lax.broadcasted_iota(jnp.int32, (channels, channels), 1)
        q, p, c = target // half, (target // LATENT_CH) % 2, target % LATENT_CH
        lane_order = (source == 4 * c + 2 * p + q).astype(jnp.bfloat16)
        to = lax.broadcasted_iota(jnp.int32, (tokens, tokens), 0)
        at = lax.broadcasted_iota(jnp.int32, (tokens, tokens), 1)
        share = planes * rows_dev
        place = ((to // share) ^ heads_at) * share
        place = place + (((to % share) // rows_dev) ^ plane_at) * rows_dev + to % rows_dev
        row_order = (at == place).astype(jnp.bfloat16)
        cells = jnp.dot(patches, lane_order, preferred_element_type=jnp.float32)
        cells = jnp.dot(row_order, cells.astype(jnp.bfloat16), preferred_element_type=jnp.float32)
        cells = cells.astype(jnp.bfloat16)
        even_ref[...] = cells[:, :half]
        odd_ref[...] = cells[:, half:]


def final_layer(where, taken, partial, w_out, scale_mod, shift_mod, w_final, rows_dev, planes):
    depth = sum(o.shape[2] for _, _, o in taken)
    inner, features = w_out.shape
    steps, tokens, tile = partial.shape
    channels = w_final.shape[1]
    whole = lambda shape: pl.BlockSpec(shape, lambda i, *_: (0,) * len(shape))
    result = jax.ShapeDtypeStruct((tokens, channels // 2), jnp.bfloat16)
    return pl.pallas_call(
        functools.partial(final_kernel, count=len(taken), planes=planes, rows_dev=rows_dev),
        grid_spec=pltpu.PrefetchScalarGridSpec(
            num_scalar_prefetch=1,
            grid=(steps,),
            in_specs=projection_specs(taken, tile, inner // HEAD_DIM // HEAD_GROUPS)
            + [
                pl.BlockSpec((None, tokens, tile), lambda i, *_: (i, 0, 0)),
                whole((1, features)),
                whole((1, features)),
                whole((channels, features)),
            ],
            out_specs=[whole((tokens, channels // 2))] * 2,
            scratch_shapes=[
                pltpu.VMEM((tokens, depth), jnp.bfloat16),
                pltpu.VMEM((steps, tokens, tile), jnp.float32),
            ],
        ),
        out_shape=[result] * 2,
        compiler_params=pltpu.CompilerParams(vmem_limit_bytes=VMEM_LIMIT),
    )(
        where,
        *[o for _, _, o in taken],
        *[w_out] * len(row_blocks(taken, inner // HEAD_DIM // HEAD_GROUPS)),
        partial,
        scale_mod[None],
        shift_mod[None],
        w_final.T,
    )


def convolve_kernel(where_ref, even_ref, odd_ref, left_ref, right_ref, w_ref, bias_ref, out_ref, latent):
    frames, cols, _, ch = latent.shape
    rows = even_ref.shape[0] // frames
    height = 2 * rows
    even = even_ref[...].astype(jnp.float32)
    odd = odd_ref[...].astype(jnp.float32)
    left = jnp.where(where_ref[2] == 0, even, left_ref[...].astype(jnp.float32))
    right = jnp.where(where_ref[2] == where_ref[3] - 1, odd, right_ref[...].astype(jnp.float32))
    for x, cells in enumerate((left, even, odd, right)):
        for f in range(frames):
            own = cells[f * rows : (f + 1) * rows]
            for p in range(2):
                latent[f, x, pl.ds(8 + p, rows, stride=2), :] = own[:, p * ch : (p + 1) * ch]
            latent[f, x, 7:8, :] = own[:1, :ch]
            latent[f, x, 8 + height : 9 + height, :] = own[rows - 1 :, ch:]
    depth = 9 * ch
    for x in range(cols - 2):
        stacked = []
        for f in range(frames):
            taps = [latent[f, x + b, 7 + e : 7 + e + height, :] for b in range(3) for e in range(3)]
            stacked.append(jnp.concatenate(taps, axis=1).astype(jnp.bfloat16))
        stacked = [stacked[0]] * 2 + stacked
        acc = None
        for a in range(3):
            flat = jnp.concatenate(stacked[a : a + frames], axis=0)
            part = jnp.dot(
                flat, w_ref[a * depth : (a + 1) * depth, :], preferred_element_type=jnp.float32
            )
            acc = part if acc is None else acc + part
        acc = (acc + bias_ref[...]).astype(jnp.bfloat16)
        out_ref[:, x] = acc.reshape(frames, height, acc.shape[1])


def convolve(where, even, odd, left, right, conv_weight, conv_bias):
    rows = even.shape[0] // FRAMES
    channels = conv_weight.shape[1]
    smem = pl.BlockSpec(memory_space=pltpu.SMEM)
    vmem = pl.BlockSpec(memory_space=pltpu.VMEM)
    return pl.pallas_call(
        convolve_kernel,
        in_specs=[smem] + [vmem] * 6,
        out_specs=vmem,
        out_shape=jax.ShapeDtypeStruct((FRAMES, 2, 2 * rows, channels), jnp.bfloat16),
        scratch_shapes=[pltpu.VMEM((FRAMES, 4, 2 * rows + 16, LATENT_CH), jnp.float32)],
        compiler_params=pltpu.CompilerParams(vmem_limit_bytes=VMEM_LIMIT),
    )(where, even, odd, left, right, conv_weight, conv_bias[None])


def after(value, *others):
    return lax.optimization_barrier((value,) + others)[0]


def gather_plane(bundle, both_parts, share, waits):
    planes = lax.axis_size("plane")
    crossed = []
    for d in range(2, planes, 2):
        if d == 2:
            sent = bundle[2 * share : both_parts + 4 * share]
        else:
            asked = bundle[both_parts + d * share : both_parts + (d + 2) * share]
            sent = jnp.concatenate([bundle[2 * share : both_parts + 2 * share], asked], axis=0)
        crossed.append(swap(after(sent, *waits), "plane", d))
    crossed = jnp.concatenate(crossed, axis=0) if len(crossed) > 1 else crossed[0]
    return [bundle, crossed, swap(bundle, "plane", 1), swap(crossed, "plane", 1)]


def shards(queries, keys, values, w_out, shift_mod, scale_mod, w_final, conv_weight, conv_bias):
    groups = lax.axis_size("heads")
    planes = lax.axis_size("plane")
    heads_at = lax.axis_index("heads")
    plane_at = lax.axis_index("plane")
    devices = groups * planes
    tokens = queries.shape[0]
    rows_dev = tokens // devices
    both_parts, share = 2 * tokens, tokens // planes
    group_heads = queries.shape[1] // HEAD_DIM // groups
    where = jnp.stack(
        [heads_at, plane_at, heads_at * planes + plane_at, jnp.int32(devices)]
    ).astype(jnp.int32)

    to = lax.broadcasted_iota(jnp.int32, (tokens, tokens), 0)
    at = lax.broadcasted_iota(jnp.int32, (tokens, tokens), 1)
    j, t, row = to // (groups * rows_dev), (to // rows_dev) % groups, to % rows_dev
    j = jnp.where(j < 2, j, j ^ 1)

    def bundle(r, low, high):
        first = (heads_at ^ r) * (HEAD_DIM * group_heads) + low * HEAD_DIM
        cut = [
            lax.dynamic_slice_in_dim(source, first, (high - low) * HEAD_DIM, axis=1)
            for source in (keys, values, queries)
        ]
        place = row * devices + (t ^ (r ^ heads_at)) * planes + (j ^ plane_at)
        order = (at == place).astype(jnp.bfloat16)
        cut[2] = jnp.dot(order, cut[2], preferred_element_type=jnp.float32).astype(jnp.bfloat16)
        return jnp.concatenate([cut[2][: 2 * share], cut[0], cut[1], cut[2][2 * share :]], axis=0)

    chunks, begun, done = [], None, None
    for low, high in CHUNKS:
        got = [bundle(r, low, high) for r in range(groups)]
        if begun is not None:
            got = [after(b, begun) for b in got]
        got = [swap(b, "heads", r) if r else b for r, b in enumerate(got)]
        begun = got[1]
        held = []
        for r, piece in enumerate(got):
            held += gather_plane(piece, both_parts, share, got[1:2] if r == 0 else [])
        taken, done = [], []
        for targets in ((3, 2), (1, 0)):
            for target, o in zip(targets, attend(held, targets, tokens, planes)):
                done.append(o)
                taken.append((target, low, o if target == 0 else swap(o, "heads", target)))
        chunks.append(taken)

    if len(chunks) == 1:
        near, far = [chunks[0][n] for n in (3, 0)], [chunks[0][n] for n in (1, 2)]
    else:
        near, far = sum(chunks[:-1], []), chunks[-1]
    partial = project(where, near, w_out, 512)
    even, odd = final_layer(
        where, far, partial, w_out, scale_mod, shift_mod, w_final, rows_dev, planes
    )
    both = ("heads", "plane")
    left = lax.ppermute(odd, both, [(i, i + 1) for i in range(devices - 1)])
    right = lax.ppermute(even, both, [(i + 1, i) for i in range(devices - 1)])
    return convolve(where, even, odd, left, right, conv_weight, conv_bias)


def solution(mesh):
    groups, seq = mesh.devices.shape
    split = Mesh(
        mesh.devices.reshape(groups, HEAD_GROUPS, seq // HEAD_GROUPS), ("groups", "heads", "plane")
    )
    by_token = P(("groups", "heads", "plane"), None)
    placed = (by_token, by_token, by_token, P(), P("groups"), P("groups"), P(), P(), P())
    return jax.shard_map(
        shards,
        mesh=split,
        in_specs=placed,
        out_specs=P("groups", ("heads", "plane"), None, None),
        check_vma=False,
    )
```

```python
import functools
import math

import jax
import jax.numpy as jnp
from jax import lax
from jax.experimental import pallas as pl
from jax.experimental.pallas import tpu as pltpu
from jax.sharding import Mesh
from jax.sharding import PartitionSpec as P

HEAD_DIM = 128
HEAD_GROUPS = 4
LATENT_CH = 16
FRAMES = 4
VMEM_LIMIT = 16 * 1024 * 1024
EXP2_SCALE = math.log2(math.e) / math.sqrt(HEAD_DIM)


def swap(source, axis, distance):
    count = lax.axis_size(axis)
    return lax.ppermute(source, axis, [(i, i ^ distance) for i in range(count)])


def bundle_kernel(where_ref, q_ref, k_ref, v_ref, *out_refs, groups, planes, parts):
    tokens, width = q_ref.shape
    group_width = width // groups
    rows_dev = tokens // (groups * planes)
    to = lax.broadcasted_iota(jnp.int32, (tokens, tokens), 0)
    at = lax.broadcasted_iota(jnp.int32, (tokens, tokens), 1)
    j, t, row = to // (groups * rows_dev), (to // rows_dev) % groups, to % rows_dev
    for (r, with_kv, with_q), out_ref in zip(parts, out_refs):
        group = where_ref[0] ^ r
        lanes = pl.ds(pl.multiple_of(group * group_width, 128), group_width)
        if with_kv:
            out_ref[:tokens] = k_ref[:, lanes]
            out_ref[tokens : 2 * tokens] = v_ref[:, lanes]
        if with_q:
            place = row * (groups * planes) + (t ^ group) * planes + (j ^ where_ref[1])
            order = (at == place).astype(jnp.bfloat16)
            mixed = jnp.dot(order, q_ref[:, lanes], preferred_element_type=jnp.float32)
            first = 2 * tokens if with_kv else 0
            out_ref[first : first + tokens] = mixed.astype(jnp.bfloat16)


def bundles(where, queries, keys, values, groups, planes, parts):
    tokens, width = queries.shape
    vmem = pl.BlockSpec(memory_space=pltpu.VMEM)
    return pl.pallas_call(
        functools.partial(bundle_kernel, groups=groups, planes=planes, parts=parts),
        in_specs=[pl.BlockSpec(memory_space=pltpu.SMEM)] + [vmem] * 3,
        out_specs=[vmem] * len(parts),
        out_shape=[
            jax.ShapeDtypeStruct(((2 * kv + q) * tokens, width // groups), jnp.bfloat16)
            for _, kv, q in parts
        ],
        compiler_params=pltpu.CompilerParams(vmem_limit_bytes=VMEM_LIMIT),
    )(where, queries, keys, values)


def attend_kernel(*refs, sources, planes, blocks, part, targets, rows_step):
    q_refs = refs[:sources]
    kv_refs = refs[sources : sources + len(blocks)]
    o_refs = refs[sources + len(blocks) :]
    tokens, width = q_refs[0].shape
    rows = tokens // sources
    rows_dev = rows // planes
    to = lax.broadcasted_iota(jnp.int32, (tokens, tokens), 0)
    at = lax.broadcasted_iota(jnp.int32, (tokens, tokens), 1)
    t, j, row = to // rows, (to // rows_dev) % planes, to % rows_dev
    place = ((j % 2) * (planes // 2) + j // 2) * rows + t * rows_dev + row
    order = (at == place).astype(jnp.bfloat16)
    asked = [
        jnp.dot(order, q[...], preferred_element_type=jnp.float32).astype(jnp.bfloat16) for q in q_refs
    ]
    works = [
        (h, range(first, min(first + rows_step, len(targets))))
        for h in range(width // HEAD_DIM)
        for first in range(0, len(targets), rows_step)
    ]

    def taken(ref, count, h, which):
        cut = ref[: count * 2 * part, h * HEAD_DIM : (h + 1) * HEAD_DIM]
        return cut.reshape(count, 2, part, HEAD_DIM)[:, which].reshape(count * part, HEAD_DIM)

    def scores_of(work):
        h, block = work
        lanes = slice(h * HEAD_DIM, (h + 1) * HEAD_DIM)
        query = jnp.concatenate(
            [q[targets[i] * rows : (targets[i] + 1) * rows, lanes] for i in block for q in asked], axis=0
        )
        return [
            lax.dot_general(
                query,
                taken(kv, count, h, 0),
                (((1,), (1,)), ((), ())),
                preferred_element_type=jnp.float32,
            )
            for kv, count in zip(kv_refs, blocks)
        ]

    def finish(work, scores):
        h, block = work
        peak = functools.reduce(jnp.maximum, [jnp.max(s, axis=1, keepdims=True) for s in scores])
        peak = peak * EXP2_SCALE
        summed = None
        for s, kv, count in zip(scores, kv_refs, blocks):
            weights = jnp.exp2(s * EXP2_SCALE - peak).astype(jnp.bfloat16)
            value = taken(kv, count, h, 1)
            value = jnp.concatenate([value, jnp.ones_like(value)], axis=1)
            product = jnp.dot(weights, value, preferred_element_type=jnp.float32)
            summed = product if summed is None else summed + product
        out = (summed[:, :HEAD_DIM] / summed[:, HEAD_DIM:]).astype(jnp.bfloat16)
        for n, i in enumerate(block):
            for r in range(sources):
                first = (n * sources + r) * rows
                o_refs[i][targets[i] ^ r, :, h * HEAD_DIM : (h + 1) * HEAD_DIM] = out[first : first + rows]

    scores = scores_of(works[0])
    for n, work in enumerate(works):
        following = scores_of(works[n + 1]) if n + 1 < len(works) else None
        finish(work, scores)
        scores = following


def attend(queries, keys_values, targets, planes):
    sources = len(queries)
    tokens, width = queries[0].shape
    rows = tokens // sources
    blocks = [kv.shape[0] // (2 * tokens) for kv in keys_values]
    key_count = sum(blocks) * tokens
    small = key_count <= 4096
    rows_step, step_width = (2, width) if small else (1, HEAD_DIM)
    score_bytes = rows_step * tokens * key_count * 4
    limit = 8 * key_count * step_width + 3 * score_bytes + 6 * 1024 * 1024
    return pl.pallas_call(
        functools.partial(
            attend_kernel,
            sources=sources,
            planes=planes,
            blocks=blocks,
            part=tokens,
            targets=targets,
            rows_step=rows_step,
        ),
        grid=(width // step_width,),
        in_specs=[pl.BlockSpec((tokens, step_width), lambda h: (0, h))] * sources
        + [pl.BlockSpec((kv.shape[0], step_width), lambda h: (0, h)) for kv in keys_values],
        out_specs=[pl.BlockSpec((sources, rows, step_width), lambda h: (0, 0, h))] * len(targets),
        out_shape=[jax.ShapeDtypeStruct((sources, rows, width), jnp.bfloat16)] * len(targets),
        compiler_params=pltpu.CompilerParams(vmem_limit_bytes=min(limit, 60 * 1024 * 1024)),
    )(*queries, *keys_values)


def project_kernel(where_ref, *refs, targets):
    o_refs = refs[: len(targets)]
    w_ref, out_ref, lined = refs[len(targets) :]
    width = o_refs[0].shape[2]
    tokens = lined.shape[0]
    for n in range(len(targets)):
        lined[:, n * width : (n + 1) * width] = o_refs[n][...].reshape(tokens, width)
    rows = [pl.ds(pl.multiple_of((where_ref[0] ^ t) * width, 128), width) for t in targets]
    weights = jnp.concatenate([w_ref[r, :] for r in rows], axis=0)
    out_ref[...] = jnp.dot(lined[...], weights, preferred_element_type=jnp.float32)


def project(where, attended, targets, w_out, tile):
    sources, rows, width = attended[0].shape
    tokens = sources * rows
    inner, features = w_out.shape
    return pl.pallas_call(
        functools.partial(project_kernel, targets=targets),
        grid_spec=pltpu.PrefetchScalarGridSpec(
            num_scalar_prefetch=1,
            grid=(features // tile,),
            in_specs=[pl.BlockSpec((sources, rows, width), lambda i, *_: (0, 0, 0))] * len(targets)
            + [pl.BlockSpec((inner, tile), lambda i, *_: (0, i))],
            out_specs=pl.BlockSpec((None, tokens, tile), lambda i, *_: (i, 0, 0)),
            scratch_shapes=[pltpu.VMEM((tokens, len(targets) * width), jnp.bfloat16)],
        ),
        out_shape=jax.ShapeDtypeStruct((features // tile, tokens, tile), jnp.float32),
        compiler_params=pltpu.CompilerParams(vmem_limit_bytes=VMEM_LIMIT),
    )(where, *attended, w_out)


def final_kernel(where_ref, *refs, targets, planes, rows_dev):
    o_refs = refs[: len(targets)]
    partial_ref, w_ref, scale_ref, shift_ref, w_final_ref, even_ref, odd_ref, lined, projected = refs[
        len(targets) :
    ]
    step = pl.program_id(0)
    heads_at, plane_at = where_ref[0], where_ref[1]
    tokens = lined.shape[0]
    width = o_refs[0].shape[2]
    tile = w_ref.shape[1]
    for n in range(len(targets)):
        lined[:, n * width : (n + 1) * width] = o_refs[n][...].reshape(tokens, width)
    rows = [pl.ds(pl.multiple_of((heads_at ^ t) * width, 128), width) for t in targets]
    weights = jnp.concatenate([w_ref[r, :] for r in rows], axis=0)
    projected[step] = partial_ref[...] + jnp.dot(
        lined[...], weights, preferred_element_type=jnp.float32
    )

    @pl.when(step == pl.num_programs(0) - 1)
    def _():
        steps = projected.shape[0]
        features = steps * tile
        total = projected[0]
        for i in range(1, steps):
            total = total + projected[i]
        mean = jnp.sum(total, axis=1, keepdims=True) * (1.0 / features)
        squares = None
        for i in range(steps):
            centered = projected[i] - mean
            squares = centered * centered if squares is None else squares + centered * centered
        variance = jnp.sum(squares, axis=1, keepdims=True) * (1.0 / features)
        inverse = lax.rsqrt(variance + 1e-06)
        patches = None
        for i in range(steps):
            lanes = slice(i * tile, (i + 1) * tile)
            normed = (projected[i] - mean) * inverse * (1.0 + scale_ref[:, lanes]) + shift_ref[:, lanes]
            part = lax.dot_general(
                normed.astype(jnp.bfloat16),
                w_final_ref[:, lanes],
                (((1,), (1,)), ((), ())),
                preferred_element_type=jnp.float32,
            )
            patches = part if patches is None else patches + part
        patches = patches.astype(jnp.bfloat16)
        channels = patches.shape[1]
        half = channels // 2
        source = lax.broadcasted_iota(jnp.int32, (channels, channels), 0)
        target = lax.broadcasted_iota(jnp.int32, (channels, channels), 1)
        q, p, c = target // half, (target // LATENT_CH) % 2, target % LATENT_CH
        lane_order = (source == 4 * c + 2 * p + q).astype(jnp.bfloat16)
        to = lax.broadcasted_iota(jnp.int32, (tokens, tokens), 0)
        at = lax.broadcasted_iota(jnp.int32, (tokens, tokens), 1)
        share = planes * rows_dev
        place = ((to // share) ^ heads_at) * share
        place = place + (((to % share) // rows_dev) ^ plane_at) * rows_dev + to % rows_dev
        row_order = (at == place).astype(jnp.bfloat16)
        cells = jnp.dot(patches, lane_order, preferred_element_type=jnp.float32)
        cells = jnp.dot(row_order, cells.astype(jnp.bfloat16), preferred_element_type=jnp.float32)
        cells = cells.astype(jnp.bfloat16)
        even_ref[...] = cells[:, :half]
        odd_ref[...] = cells[:, half:]


def final_layer(where, attended, targets, partial, w_out, scale_mod, shift_mod, w_final, rows_dev, planes):
    sources, rows, width = attended[0].shape
    inner, features = w_out.shape
    steps, tokens, tile = partial.shape
    channels = w_final.shape[1]
    whole = lambda shape: pl.BlockSpec(shape, lambda i, *_: (0,) * len(shape))
    result = jax.ShapeDtypeStruct((tokens, channels // 2), jnp.bfloat16)
    return pl.pallas_call(
        functools.partial(final_kernel, targets=targets, planes=planes, rows_dev=rows_dev),
        grid_spec=pltpu.PrefetchScalarGridSpec(
            num_scalar_prefetch=1,
            grid=(steps,),
            in_specs=[whole((sources, rows, width))] * len(targets)
            + [
                pl.BlockSpec((None, tokens, tile), lambda i, *_: (i, 0, 0)),
                pl.BlockSpec((inner, tile), lambda i, *_: (0, i)),
                whole((1, features)),
                whole((1, features)),
                whole((channels, features)),
            ],
            out_specs=[whole((tokens, channels // 2))] * 2,
            scratch_shapes=[
                pltpu.VMEM((tokens, len(targets) * width), jnp.bfloat16),
                pltpu.VMEM((steps, tokens, tile), jnp.float32),
            ],
        ),
        out_shape=[result] * 2,
        compiler_params=pltpu.CompilerParams(vmem_limit_bytes=VMEM_LIMIT),
    )(where, *attended, partial, w_out, scale_mod[None], shift_mod[None], w_final.T)


def convolve_kernel(where_ref, even_ref, odd_ref, left_ref, right_ref, w_ref, bias_ref, out_ref, latent):
    frames, cols, _, ch = latent.shape
    rows = even_ref.shape[0] // frames
    height = 2 * rows
    even = even_ref[...].astype(jnp.float32)
    odd = odd_ref[...].astype(jnp.float32)
    left = jnp.where(where_ref[2] == 0, even, left_ref[...].astype(jnp.float32))
    right = jnp.where(where_ref[2] == where_ref[3] - 1, odd, right_ref[...].astype(jnp.float32))
    for x, cells in enumerate((left, even, odd, right)):
        for f in range(frames):
            own = cells[f * rows : (f + 1) * rows]
            for p in range(2):
                latent[f, x, pl.ds(8 + p, rows, stride=2), :] = own[:, p * ch : (p + 1) * ch]
            latent[f, x, 7:8, :] = own[:1, :ch]
            latent[f, x, 8 + height : 9 + height, :] = own[rows - 1 :, ch:]
    depth = 9 * ch
    for x in range(cols - 2):
        stacked = []
        for f in range(frames):
            taps = [latent[f, x + b, 7 + e : 7 + e + height, :] for b in range(3) for e in range(3)]
            stacked.append(jnp.concatenate(taps, axis=1).astype(jnp.bfloat16))
        stacked = [stacked[0]] * 2 + stacked
        acc = None
        for a in range(3):
            flat = jnp.concatenate(stacked[a : a + frames], axis=0)
            part = jnp.dot(
                flat, w_ref[a * depth : (a + 1) * depth, :], preferred_element_type=jnp.float32
            )
            acc = part if acc is None else acc + part
        acc = (acc + bias_ref[...]).astype(jnp.bfloat16)
        out_ref[:, x] = acc.reshape(frames, height, acc.shape[1])


def convolve(where, even, odd, left, right, conv_weight, conv_bias):
    rows = even.shape[0] // FRAMES
    channels = conv_weight.shape[1]
    smem = pl.BlockSpec(memory_space=pltpu.SMEM)
    vmem = pl.BlockSpec(memory_space=pltpu.VMEM)
    return pl.pallas_call(
        convolve_kernel,
        in_specs=[smem] + [vmem] * 6,
        out_specs=vmem,
        out_shape=jax.ShapeDtypeStruct((FRAMES, 2, 2 * rows, channels), jnp.bfloat16),
        scratch_shapes=[pltpu.VMEM((FRAMES, 4, 2 * rows + 16, LATENT_CH), jnp.float32)],
        compiler_params=pltpu.CompilerParams(vmem_limit_bytes=VMEM_LIMIT),
    )(where, even, odd, left, right, conv_weight, conv_bias[None])


def after(value, *others):
    return lax.optimization_barrier((value,) + others)[0]


def shards(queries, keys, values, w_out, shift_mod, scale_mod, w_final, conv_weight, conv_bias):
    groups = lax.axis_size("heads")
    planes = lax.axis_size("plane")
    heads_at = lax.axis_index("heads")
    plane_at = lax.axis_index("plane")
    devices = groups * planes
    tokens = queries.shape[0]
    rows_dev = tokens // devices
    where = jnp.stack(
        [heads_at, plane_at, heads_at * planes + plane_at, jnp.int32(devices)]
    ).astype(jnp.int32)

    parts = ((2, 1, 0), (3, 1, 0), (1, 1, 1), (0, 1, 1), (2, 0, 1), (3, 0, 1))
    made = bundles(where, queries, keys, values, groups, planes, parts)
    w_out = after(w_out, *made)
    both_parts, share = 2 * tokens, tokens // planes

    def across(bundle, *waits):
        crossed = []
        for d in range(2, planes, 2):
            sent = bundle
            if bundle.shape[0] > both_parts:
                queried = bundle[both_parts + d * share : both_parts + (d + 2) * share]
                sent = jnp.concatenate([bundle[:both_parts], queried], axis=0)
            crossed.append(swap(after(sent, *waits), "plane", d))
        return crossed

    got = {0: made[3], 2: swap(made[0], "heads", 2), 1: swap(made[2], "heads", 1)}
    held = {0: across(got[0])}
    got[3] = swap(after(made[1], held[0][-1]), "heads", 3)
    for r in (1, 2, 3):
        held[r] = across(got[r])
    late_q = [swap(after(made[2 + r], held[1][-1], held[2][-1]), "heads", r) for r in (2, 3)]
    held = {r: [got[r]] + held[r] for r in range(groups)}

    keys_values, asked = [], {}
    for distances in ((0, 1), (2,), (3,)):
        passed = [h[:both_parts] for r in distances for h in held[r]]
        passed += [
            h[both_parts + share : both_parts + 2 * share]
            for r in distances
            for h in held[r]
            if h.shape[0] > both_parts
        ]
        mine = jnp.concatenate(passed, axis=0)
        other = swap(mine, "plane", 1)
        keys_values += [mine, other]
        half = planes // 2
        first = both_parts * half * len(distances)
        for n, r in enumerate(distances):
            start = first + n * half * share
            if start < mine.shape[0]:
                asked[r] = [h[both_parts : both_parts + share] for h in held[r]]
                asked[r].append(other[start : start + half * share])
    arrival = list(range(0, planes, 2)) + list(range(1, planes, 2))
    by_distance = []
    for d in arrival:
        pair = jnp.concatenate([q[d * share : (d + 1) * share] for q in late_q], axis=0)
        by_distance.append(swap(pair, "plane", d) if d else pair)
    for n, r in enumerate((2, 3)):
        asked[r] = [pair[n * share : (n + 1) * share] for pair in by_distance]
    asked = [jnp.concatenate(asked[r], axis=0) for r in range(groups)]

    first, second = (3, 2), (1, 0)
    near, far = (0, 3), (2, 1)
    results = {}
    for targets in (first, second):
        for t, o in zip(targets, attend(asked, keys_values, targets, planes)):
            results[t] = o if t == 0 else swap(o, "heads", t)
    partial = project(where, [results[t] for t in near], near, w_out, 512)
    sent = [results[t] for t in far]
    even, odd = final_layer(
        where, sent, far, partial, w_out, scale_mod, shift_mod, w_final, rows_dev, planes
    )
    both = ("heads", "plane")
    left = lax.ppermute(odd, both, [(i, i + 1) for i in range(devices - 1)])
    right = lax.ppermute(even, both, [(i + 1, i) for i in range(devices - 1)])
    return convolve(where, even, odd, left, right, conv_weight, conv_bias)


def solution(mesh):
    groups, seq = mesh.devices.shape
    split = Mesh(
        mesh.devices.reshape(groups, HEAD_GROUPS, seq // HEAD_GROUPS), ("groups", "heads", "plane")
    )
    by_token = P(("groups", "heads", "plane"), None)
    placed = (by_token, by_token, by_token, P(), P("groups"), P("groups"), P(), P(), P())
    return jax.shard_map(
        shards,
        mesh=split,
        in_specs=placed,
        out_specs=P("groups", ("heads", "plane"), None, None),
        check_vma=False,
    )
```

```python
import functools
import math

import jax
import jax.numpy as jnp
from jax import lax
from jax.experimental import pallas as pl
from jax.experimental.pallas import tpu as pltpu
from jax.sharding import Mesh
from jax.sharding import PartitionSpec as P

HEAD_DIM = 128
HEAD_GROUPS = 4
LATENT_CH = 16
FRAMES = 4
VMEM_LIMIT = 16 * 1024 * 1024
EXP2_SCALE = math.log2(math.e) / math.sqrt(HEAD_DIM)


def swap(source, axis, distance):
    count = lax.axis_size(axis)
    return lax.ppermute(source, axis, [(i, i ^ distance) for i in range(count)])


def bundle_kernel(where_ref, *refs, groups, planes, distances):
    tokens = refs[0].shape[0]
    rows_dev = tokens // (groups * planes)
    to = lax.broadcasted_iota(jnp.int32, (tokens, tokens), 0)
    at = lax.broadcasted_iota(jnp.int32, (tokens, tokens), 1)
    j, t, row = to // (groups * rows_dev), (to // rows_dev) % groups, to % rows_dev
    count = len(distances)
    cut = [refs[n * count : (n + 1) * count] for n in range(4)]
    for r, q_ref, k_ref, v_ref, out_ref in zip(distances, *cut):
        group = where_ref[0] ^ r
        place = row * (groups * planes) + (t ^ group) * planes + (j ^ where_ref[1])
        order = (at == place).astype(jnp.bfloat16)
        out_ref[:tokens] = k_ref[...]
        out_ref[tokens : 2 * tokens] = v_ref[...]
        mixed = jnp.dot(order, q_ref[...], preferred_element_type=jnp.float32)
        out_ref[2 * tokens :] = mixed.astype(jnp.bfloat16)


def bundles(where, queries, keys, values, groups, planes, distances):
    def cut(source, r):
        width = source.shape[1] // groups
        return lax.dynamic_slice_in_dim(source, (lax.axis_index("heads") ^ r) * width, width, axis=1)

    tokens, width = queries.shape
    vmem = pl.BlockSpec(memory_space=pltpu.VMEM)
    result = jax.ShapeDtypeStruct((3 * tokens, width // groups), jnp.bfloat16)
    return pl.pallas_call(
        functools.partial(bundle_kernel, groups=groups, planes=planes, distances=distances),
        in_specs=[pl.BlockSpec(memory_space=pltpu.SMEM)] + [vmem] * (3 * len(distances)),
        out_specs=[vmem] * len(distances),
        out_shape=[result] * len(distances),
        compiler_params=pltpu.CompilerParams(vmem_limit_bytes=VMEM_LIMIT),
    )(where, *[cut(source, r) for source in (queries, keys, values) for r in distances])


def attend_kernel(*refs, sources, planes, blocks, part, targets, rows_step):
    q_refs = refs[:sources]
    kv_refs = refs[sources : sources + len(blocks)]
    o_refs = refs[sources + len(blocks) :]
    tokens, width = q_refs[0].shape
    rows = tokens // sources
    rows_dev = rows // planes
    to = lax.broadcasted_iota(jnp.int32, (tokens, tokens), 0)
    at = lax.broadcasted_iota(jnp.int32, (tokens, tokens), 1)
    t, j, row = to // rows, (to // rows_dev) % planes, to % rows_dev
    place = ((j % 2) * (planes // 2) + j // 2) * rows + t * rows_dev + row
    order = (at == place).astype(jnp.bfloat16)
    asked = [
        jnp.dot(order, q[...], preferred_element_type=jnp.float32).astype(jnp.bfloat16) for q in q_refs
    ]
    works = [
        (h, range(first, min(first + rows_step, len(targets))))
        for h in range(width // HEAD_DIM)
        for first in range(0, len(targets), rows_step)
    ]

    def taken(ref, count, h, which):
        cut = ref[: count * 2 * part, h * HEAD_DIM : (h + 1) * HEAD_DIM]
        return cut.reshape(count, 2, part, HEAD_DIM)[:, which].reshape(count * part, HEAD_DIM)

    def scores_of(work):
        h, block = work
        lanes = slice(h * HEAD_DIM, (h + 1) * HEAD_DIM)
        query = jnp.concatenate(
            [q[targets[i] * rows : (targets[i] + 1) * rows, lanes] for i in block for q in asked], axis=0
        )
        return [
            lax.dot_general(
                query,
                taken(kv, count, h, 0),
                (((1,), (1,)), ((), ())),
                preferred_element_type=jnp.float32,
            )
            for kv, count in zip(kv_refs, blocks)
        ]

    def finish(work, scores):
        h, block = work
        peak = functools.reduce(jnp.maximum, [jnp.max(s, axis=1, keepdims=True) for s in scores])
        peak = peak * EXP2_SCALE
        summed = None
        for s, kv, count in zip(scores, kv_refs, blocks):
            weights = jnp.exp2(s * EXP2_SCALE - peak).astype(jnp.bfloat16)
            value = taken(kv, count, h, 1)
            value = jnp.concatenate([value, jnp.ones_like(value)], axis=1)
            product = jnp.dot(weights, value, preferred_element_type=jnp.float32)
            summed = product if summed is None else summed + product
        out = (summed[:, :HEAD_DIM] / summed[:, HEAD_DIM:]).astype(jnp.bfloat16)
        for n, i in enumerate(block):
            for r in range(sources):
                first = (n * sources + r) * rows
                o_refs[i][targets[i] ^ r, :, h * HEAD_DIM : (h + 1) * HEAD_DIM] = out[first : first + rows]

    scores = scores_of(works[0])
    for n, work in enumerate(works):
        following = scores_of(works[n + 1]) if n + 1 < len(works) else None
        finish(work, scores)
        scores = following


def attend(queries, keys_values, targets, planes):
    sources = len(queries)
    tokens, width = queries[0].shape
    rows = tokens // sources
    blocks = [kv.shape[0] // (2 * tokens) for kv in keys_values]
    key_count = sum(blocks) * tokens
    small = key_count <= 4096
    rows_step, step_width = (2, width) if small else (1, HEAD_DIM)
    score_bytes = rows_step * tokens * key_count * 4
    limit = 8 * key_count * step_width + 3 * score_bytes + 6 * 1024 * 1024
    return pl.pallas_call(
        functools.partial(
            attend_kernel,
            sources=sources,
            planes=planes,
            blocks=blocks,
            part=tokens,
            targets=targets,
            rows_step=rows_step,
        ),
        grid=(width // step_width,),
        in_specs=[pl.BlockSpec((tokens, step_width), lambda h: (0, h))] * sources
        + [pl.BlockSpec((kv.shape[0], step_width), lambda h: (0, h)) for kv in keys_values],
        out_specs=[pl.BlockSpec((sources, rows, step_width), lambda h: (0, 0, h))] * len(targets),
        out_shape=[jax.ShapeDtypeStruct((sources, rows, width), jnp.bfloat16)] * len(targets),
        compiler_params=pltpu.CompilerParams(vmem_limit_bytes=min(limit, 60 * 1024 * 1024)),
    )(*queries, *keys_values)


def projection_of(o_refs, w_refs, lined):
    tokens, width = lined.shape[0], o_refs[0].shape[2]
    for n, o_ref in enumerate(o_refs):
        lined[:, n * width : (n + 1) * width] = o_ref[...].reshape(tokens, width)
    weights = jnp.concatenate([w[...] for w in w_refs], axis=0)
    return jnp.dot(lined[...], weights, preferred_element_type=jnp.float32)


def projection_specs(attended, targets, tile):
    o_spec = pl.BlockSpec(attended[0].shape, lambda i, *_: (0, 0, 0))
    width = attended[0].shape[2]
    return [o_spec] * len(targets) + [
        pl.BlockSpec((width, tile), lambda i, where, t=t: (where[0] ^ t, i)) for t in targets
    ]


def project_kernel(where_ref, *refs, targets):
    count = len(targets)
    out_ref, lined = refs[2 * count :]
    out_ref[...] = projection_of(refs[:count], refs[count : 2 * count], lined)


def project(where, attended, targets, w_out, tile):
    sources, rows, width = attended[0].shape
    tokens = sources * rows
    features = w_out.shape[1]
    return pl.pallas_call(
        functools.partial(project_kernel, targets=targets),
        grid_spec=pltpu.PrefetchScalarGridSpec(
            num_scalar_prefetch=1,
            grid=(features // tile,),
            in_specs=projection_specs(attended, targets, tile),
            out_specs=pl.BlockSpec((None, tokens, tile), lambda i, *_: (i, 0, 0)),
            scratch_shapes=[pltpu.VMEM((tokens, len(targets) * width), jnp.bfloat16)],
        ),
        out_shape=jax.ShapeDtypeStruct((features // tile, tokens, tile), jnp.float32),
        compiler_params=pltpu.CompilerParams(vmem_limit_bytes=VMEM_LIMIT),
    )(where, *attended, *[w_out] * len(targets))


def final_kernel(where_ref, *refs, targets, planes, rows_dev):
    count = len(targets)
    partial_ref, scale_ref, shift_ref, w_final_ref, even_ref, odd_ref, lined, projected = refs[2 * count :]
    step = pl.program_id(0)
    heads_at, plane_at = where_ref[0], where_ref[1]
    tokens = lined.shape[0]
    tile = partial_ref.shape[1]
    projected[step] = partial_ref[...] + projection_of(refs[:count], refs[count : 2 * count], lined)

    @pl.when(step == pl.num_programs(0) - 1)
    def _():
        steps = projected.shape[0]
        features = steps * tile
        total = projected[0]
        for i in range(1, steps):
            total = total + projected[i]
        mean = jnp.sum(total, axis=1, keepdims=True) * (1.0 / features)
        squares = None
        for i in range(steps):
            centered = projected[i] - mean
            squares = centered * centered if squares is None else squares + centered * centered
        variance = jnp.sum(squares, axis=1, keepdims=True) * (1.0 / features)
        inverse = lax.rsqrt(variance + 1e-06)
        patches = None
        for i in range(steps):
            lanes = slice(i * tile, (i + 1) * tile)
            normed = (projected[i] - mean) * inverse * (1.0 + scale_ref[:, lanes]) + shift_ref[:, lanes]
            part = lax.dot_general(
                normed.astype(jnp.bfloat16),
                w_final_ref[:, lanes],
                (((1,), (1,)), ((), ())),
                preferred_element_type=jnp.float32,
            )
            patches = part if patches is None else patches + part
        patches = patches.astype(jnp.bfloat16)
        channels = patches.shape[1]
        half = channels // 2
        source = lax.broadcasted_iota(jnp.int32, (channels, channels), 0)
        target = lax.broadcasted_iota(jnp.int32, (channels, channels), 1)
        q, p, c = target // half, (target // LATENT_CH) % 2, target % LATENT_CH
        lane_order = (source == 4 * c + 2 * p + q).astype(jnp.bfloat16)
        to = lax.broadcasted_iota(jnp.int32, (tokens, tokens), 0)
        at = lax.broadcasted_iota(jnp.int32, (tokens, tokens), 1)
        share = planes * rows_dev
        place = ((to // share) ^ heads_at) * share
        place = place + (((to % share) // rows_dev) ^ plane_at) * rows_dev + to % rows_dev
        row_order = (at == place).astype(jnp.bfloat16)
        cells = jnp.dot(patches, lane_order, preferred_element_type=jnp.float32)
        cells = jnp.dot(row_order, cells.astype(jnp.bfloat16), preferred_element_type=jnp.float32)
        cells = cells.astype(jnp.bfloat16)
        even_ref[...] = cells[:, :half]
        odd_ref[...] = cells[:, half:]


def final_layer(where, attended, targets, partial, w_out, scale_mod, shift_mod, w_final, rows_dev, planes):
    sources, rows, width = attended[0].shape
    features = w_out.shape[1]
    steps, tokens, tile = partial.shape
    channels = w_final.shape[1]
    whole = lambda shape: pl.BlockSpec(shape, lambda i, *_: (0,) * len(shape))
    result = jax.ShapeDtypeStruct((tokens, channels // 2), jnp.bfloat16)
    return pl.pallas_call(
        functools.partial(final_kernel, targets=targets, planes=planes, rows_dev=rows_dev),
        grid_spec=pltpu.PrefetchScalarGridSpec(
            num_scalar_prefetch=1,
            grid=(steps,),
            in_specs=projection_specs(attended, targets, tile)
            + [
                pl.BlockSpec((None, tokens, tile), lambda i, *_: (i, 0, 0)),
                whole((1, features)),
                whole((1, features)),
                whole((channels, features)),
            ],
            out_specs=[whole((tokens, channels // 2))] * 2,
            scratch_shapes=[
                pltpu.VMEM((tokens, len(targets) * width), jnp.bfloat16),
                pltpu.VMEM((steps, tokens, tile), jnp.float32),
            ],
        ),
        out_shape=[result] * 2,
        compiler_params=pltpu.CompilerParams(vmem_limit_bytes=VMEM_LIMIT),
    )(where, *attended, *[w_out] * len(targets), partial, scale_mod[None], shift_mod[None], w_final.T)


def convolve_kernel(where_ref, even_ref, odd_ref, left_ref, right_ref, w_ref, bias_ref, out_ref, latent):
    frames, cols, _, ch = latent.shape
    rows = even_ref.shape[0] // frames
    height = 2 * rows
    even = even_ref[...].astype(jnp.float32)
    odd = odd_ref[...].astype(jnp.float32)
    left = jnp.where(where_ref[2] == 0, even, left_ref[...].astype(jnp.float32))
    right = jnp.where(where_ref[2] == where_ref[3] - 1, odd, right_ref[...].astype(jnp.float32))
    for x, cells in enumerate((left, even, odd, right)):
        for f in range(frames):
            own = cells[f * rows : (f + 1) * rows]
            for p in range(2):
                latent[f, x, pl.ds(8 + p, rows, stride=2), :] = own[:, p * ch : (p + 1) * ch]
            latent[f, x, 7:8, :] = own[:1, :ch]
            latent[f, x, 8 + height : 9 + height, :] = own[rows - 1 :, ch:]
    depth = 9 * ch
    for x in range(cols - 2):
        stacked = []
        for f in range(frames):
            taps = [latent[f, x + b, 7 + e : 7 + e + height, :] for b in range(3) for e in range(3)]
            stacked.append(jnp.concatenate(taps, axis=1).astype(jnp.bfloat16))
        stacked = [stacked[0]] * 2 + stacked
        acc = None
        for a in range(3):
            flat = jnp.concatenate(stacked[a : a + frames], axis=0)
            part = jnp.dot(
                flat, w_ref[a * depth : (a + 1) * depth, :], preferred_element_type=jnp.float32
            )
            acc = part if acc is None else acc + part
        acc = (acc + bias_ref[...]).astype(jnp.bfloat16)
        out_ref[:, x] = acc.reshape(frames, height, acc.shape[1])


def convolve(where, even, odd, left, right, conv_weight, conv_bias):
    rows = even.shape[0] // FRAMES
    channels = conv_weight.shape[1]
    smem = pl.BlockSpec(memory_space=pltpu.SMEM)
    vmem = pl.BlockSpec(memory_space=pltpu.VMEM)
    return pl.pallas_call(
        convolve_kernel,
        in_specs=[smem] + [vmem] * 6,
        out_specs=vmem,
        out_shape=jax.ShapeDtypeStruct((FRAMES, 2, 2 * rows, channels), jnp.bfloat16),
        scratch_shapes=[pltpu.VMEM((FRAMES, 4, 2 * rows + 16, LATENT_CH), jnp.float32)],
        compiler_params=pltpu.CompilerParams(vmem_limit_bytes=VMEM_LIMIT),
    )(where, even, odd, left, right, conv_weight, conv_bias[None])


def shards(queries, keys, values, w_out, shift_mod, scale_mod, w_final, conv_weight, conv_bias):
    groups = lax.axis_size("heads")
    planes = lax.axis_size("plane")
    heads_at = lax.axis_index("heads")
    plane_at = lax.axis_index("plane")
    devices = groups * planes
    tokens = queries.shape[0]
    rows_dev = tokens // devices
    where = jnp.stack(
        [heads_at, plane_at, heads_at * planes + plane_at, jnp.int32(devices)]
    ).astype(jnp.int32)

    made = bundles(where, queries, keys, values, groups, planes, range(groups))
    got = {r: swap(made[r], "heads", r) if r else made[r] for r in range(groups)}

    both_parts, share = 2 * tokens, tokens // planes
    held = {r: [got[r]] for r in range(groups)}
    for r in (0, 1, 2, 3):
        for d in range(2, planes, 2):
            asked = got[r][both_parts + d * share : both_parts + (d + 2) * share]
            held[r].append(swap(jnp.concatenate([got[r][:both_parts], asked], axis=0), "plane", d))

    keys_values, asked = [], {}
    for distances in ((0, 1), (2,), (3,)):
        passed = [h[:both_parts] for r in distances for h in held[r]]
        passed += [h[both_parts + share : both_parts + 2 * share] for r in distances for h in held[r]]
        mine = jnp.concatenate(passed, axis=0)
        other = swap(mine, "plane", 1)
        keys_values += [mine, other]
        half = planes // 2
        first = both_parts * half * len(distances)
        for n, r in enumerate(distances):
            start = first + n * half * share
            asked[r] = jnp.concatenate(
                [h[both_parts : both_parts + share] for h in held[r]]
                + [other[start : start + half * share]],
                axis=0,
            )
    asked = [asked[r] for r in range(groups)]

    first, second = (3, 2), (1, 0)
    near, far = (0, 3), (2, 1)
    results = {}
    for targets in (first, second):
        for t, o in zip(targets, attend(asked, keys_values, targets, planes)):
            results[t] = o if t == 0 else swap(o, "heads", t)
    partial = project(where, [results[t] for t in near], near, w_out, 512)
    sent = [results[t] for t in far]
    even, odd = final_layer(
        where, sent, far, partial, w_out, scale_mod, shift_mod, w_final, rows_dev, planes
    )
    both = ("heads", "plane")
    left = lax.ppermute(odd, both, [(i, i + 1) for i in range(devices - 1)])
    right = lax.ppermute(even, both, [(i + 1, i) for i in range(devices - 1)])
    return convolve(where, even, odd, left, right, conv_weight, conv_bias)


def solution(mesh):
    groups, seq = mesh.devices.shape
    split = Mesh(
        mesh.devices.reshape(groups, HEAD_GROUPS, seq // HEAD_GROUPS), ("groups", "heads", "plane")
    )
    by_token = P(("groups", "heads", "plane"), None)
    placed = (by_token, by_token, by_token, P(), P("groups"), P("groups"), P(), P(), P())
    return jax.shard_map(
        shards,
        mesh=split,
        in_specs=placed,
        out_specs=P("groups", ("heads", "plane"), None, None),
        check_vma=False,
    )
```

```python
import functools
import math

import jax
import jax.numpy as jnp
from jax import lax
from jax.experimental import pallas as pl
from jax.experimental.pallas import tpu as pltpu
from jax.sharding import Mesh
from jax.sharding import PartitionSpec as P

HEAD_DIM = 128
HEAD_GROUPS = 4
LATENT_CH = 16
FRAMES = 4
VMEM_LIMIT = 16 * 1024 * 1024
EXP2_SCALE = math.log2(math.e) / math.sqrt(HEAD_DIM)


def swap(source, axis, distance):
    count = lax.axis_size(axis)
    return lax.ppermute(source, axis, [(i, i ^ distance) for i in range(count)])


def bundle_kernel(where_ref, *refs, groups, planes, distances):
    tokens = refs[0].shape[0]
    rows_dev = tokens // (groups * planes)
    to = lax.broadcasted_iota(jnp.int32, (tokens, tokens), 0)
    at = lax.broadcasted_iota(jnp.int32, (tokens, tokens), 1)
    j, t, row = to // (groups * rows_dev), (to // rows_dev) % groups, to % rows_dev
    count = len(distances)
    cut = [refs[n * count : (n + 1) * count] for n in range(4)]
    for r, q_ref, k_ref, v_ref, out_ref in zip(distances, *cut):
        group = where_ref[0] ^ r
        place = row * (groups * planes) + (t ^ group) * planes + (j ^ where_ref[1])
        order = (at == place).astype(jnp.bfloat16)
        out_ref[:tokens] = k_ref[...]
        out_ref[tokens : 2 * tokens] = v_ref[...]
        mixed = jnp.dot(order, q_ref[...], preferred_element_type=jnp.float32)
        out_ref[2 * tokens :] = mixed.astype(jnp.bfloat16)


def bundles(where, queries, keys, values, groups, planes, distances):
    def cut(source, r):
        width = source.shape[1] // groups
        return lax.dynamic_slice_in_dim(source, (lax.axis_index("heads") ^ r) * width, width, axis=1)

    tokens, width = queries.shape
    vmem = pl.BlockSpec(memory_space=pltpu.VMEM)
    result = jax.ShapeDtypeStruct((3 * tokens, width // groups), jnp.bfloat16)
    return pl.pallas_call(
        functools.partial(bundle_kernel, groups=groups, planes=planes, distances=distances),
        in_specs=[pl.BlockSpec(memory_space=pltpu.SMEM)] + [vmem] * (3 * len(distances)),
        out_specs=[vmem] * len(distances),
        out_shape=[result] * len(distances),
        compiler_params=pltpu.CompilerParams(vmem_limit_bytes=VMEM_LIMIT),
    )(where, *[cut(source, r) for source in (queries, keys, values) for r in distances])


def attend_kernel(*refs, sources, planes, blocks, part, targets, rows_step):
    q_refs = refs[:sources]
    kv_refs = refs[sources : sources + len(blocks)]
    o_refs = refs[sources + len(blocks) :]
    tokens, width = q_refs[0].shape
    rows = tokens // sources
    rows_dev = rows // planes
    to = lax.broadcasted_iota(jnp.int32, (tokens, tokens), 0)
    at = lax.broadcasted_iota(jnp.int32, (tokens, tokens), 1)
    t, j, row = to // rows, (to // rows_dev) % planes, to % rows_dev
    place = ((j % 2) * (planes // 2) + j // 2) * rows + t * rows_dev + row
    order = (at == place).astype(jnp.bfloat16)
    asked = [
        jnp.dot(order, q[...], preferred_element_type=jnp.float32).astype(jnp.bfloat16) for q in q_refs
    ]
    works = [
        (h, range(first, min(first + rows_step, len(targets))))
        for h in range(width // HEAD_DIM)
        for first in range(0, len(targets), rows_step)
    ]

    def taken(ref, count, h, which):
        cut = ref[: count * 2 * part, h * HEAD_DIM : (h + 1) * HEAD_DIM]
        return cut.reshape(count, 2, part, HEAD_DIM)[:, which].reshape(count * part, HEAD_DIM)

    def scores_of(work):
        h, block = work
        lanes = slice(h * HEAD_DIM, (h + 1) * HEAD_DIM)
        query = jnp.concatenate(
            [q[targets[i] * rows : (targets[i] + 1) * rows, lanes] for i in block for q in asked], axis=0
        )
        return [
            lax.dot_general(
                query,
                taken(kv, count, h, 0),
                (((1,), (1,)), ((), ())),
                preferred_element_type=jnp.float32,
            )
            for kv, count in zip(kv_refs, blocks)
        ]

    def finish(work, scores):
        h, block = work
        peak = functools.reduce(jnp.maximum, [jnp.max(s, axis=1, keepdims=True) for s in scores])
        peak = peak * EXP2_SCALE
        summed = None
        for s, kv, count in zip(scores, kv_refs, blocks):
            weights = jnp.exp2(s * EXP2_SCALE - peak).astype(jnp.bfloat16)
            value = taken(kv, count, h, 1)
            value = jnp.concatenate([value, jnp.ones_like(value)], axis=1)
            product = jnp.dot(weights, value, preferred_element_type=jnp.float32)
            summed = product if summed is None else summed + product
        out = (summed[:, :HEAD_DIM] / summed[:, HEAD_DIM:]).astype(jnp.bfloat16)
        for n, i in enumerate(block):
            for r in range(sources):
                first = (n * sources + r) * rows
                o_refs[i][targets[i] ^ r, :, h * HEAD_DIM : (h + 1) * HEAD_DIM] = out[first : first + rows]

    scores = scores_of(works[0])
    for n, work in enumerate(works):
        following = scores_of(works[n + 1]) if n + 1 < len(works) else None
        finish(work, scores)
        scores = following


def attend(queries, keys_values, targets, planes):
    sources = len(queries)
    tokens, width = queries[0].shape
    rows = tokens // sources
    blocks = [kv.shape[0] // (2 * tokens) for kv in keys_values]
    key_count = sum(blocks) * tokens
    small = key_count <= 4096
    rows_step, step_width = (2, width) if small else (1, HEAD_DIM)
    score_bytes = rows_step * tokens * key_count * 4
    limit = 8 * key_count * step_width + 3 * score_bytes + 6 * 1024 * 1024
    return pl.pallas_call(
        functools.partial(
            attend_kernel,
            sources=sources,
            planes=planes,
            blocks=blocks,
            part=tokens,
            targets=targets,
            rows_step=rows_step,
        ),
        grid=(width // step_width,),
        in_specs=[pl.BlockSpec((tokens, step_width), lambda h: (0, h))] * sources
        + [pl.BlockSpec((kv.shape[0], step_width), lambda h: (0, h)) for kv in keys_values],
        out_specs=[pl.BlockSpec((sources, rows, step_width), lambda h: (0, 0, h))] * len(targets),
        out_shape=[jax.ShapeDtypeStruct((sources, rows, width), jnp.bfloat16)] * len(targets),
        compiler_params=pltpu.CompilerParams(vmem_limit_bytes=min(limit, 60 * 1024 * 1024)),
    )(*queries, *keys_values)


def projection_of(o_refs, w_refs, lined):
    tokens, width = lined.shape[0], o_refs[0].shape[2]
    for n, o_ref in enumerate(o_refs):
        lined[:, n * width : (n + 1) * width] = o_ref[...].reshape(tokens, width)
    pieces = [(w, first) for w in w_refs for first in range(0, width, 128)]
    total = None
    for n in range(0, len(pieces), 2):
        rows = [w[first : first + 128, :] for w, first in pieces[n : n + 2]]
        lanes = lined[:, n * 128 : (n + len(rows)) * 128]
        part = jnp.dot(lanes, jnp.concatenate(rows, axis=0), preferred_element_type=jnp.float32)
        total = part if total is None else total + part
    return total


def projection_specs(attended, targets, tile):
    o_spec = pl.BlockSpec(attended[0].shape, lambda i, *_: (0, 0, 0))
    width = attended[0].shape[2]
    return [o_spec] * len(targets) + [
        pl.BlockSpec((width, tile), lambda i, where, t=t: (where[0] ^ t, i)) for t in targets
    ]


def project_kernel(where_ref, *refs, targets):
    count = len(targets)
    out_ref, lined = refs[2 * count :]
    out_ref[...] = projection_of(refs[:count], refs[count : 2 * count], lined)


def project(where, attended, targets, w_out, tile):
    sources, rows, width = attended[0].shape
    tokens = sources * rows
    features = w_out.shape[1]
    return pl.pallas_call(
        functools.partial(project_kernel, targets=targets),
        grid_spec=pltpu.PrefetchScalarGridSpec(
            num_scalar_prefetch=1,
            grid=(features // tile,),
            in_specs=projection_specs(attended, targets, tile),
            out_specs=pl.BlockSpec((None, tokens, tile), lambda i, *_: (i, 0, 0)),
            scratch_shapes=[pltpu.VMEM((tokens, len(targets) * width), jnp.bfloat16)],
        ),
        out_shape=jax.ShapeDtypeStruct((features // tile, tokens, tile), jnp.float32),
        compiler_params=pltpu.CompilerParams(vmem_limit_bytes=VMEM_LIMIT),
    )(where, *attended, *[w_out] * len(targets))


def final_kernel(where_ref, *refs, targets, planes, rows_dev):
    count = len(targets)
    partial_ref, scale_ref, shift_ref, w_final_ref, even_ref, odd_ref, lined, projected, pivot, sums = refs[
        2 * count :
    ]
    step = pl.program_id(0)
    heads_at, plane_at = where_ref[0], where_ref[1]
    tokens = lined.shape[0]
    tile = partial_ref.shape[1]
    row = partial_ref[...] + projection_of(refs[:count], refs[count : 2 * count], lined)
    projected[step] = row

    @pl.when(step == 0)
    def _():
        pivot[...] = jnp.broadcast_to(jnp.mean(row, axis=1, keepdims=True), pivot.shape)
        sums[...] = jnp.zeros_like(sums)

    for first in range(0, tile, 128):
        off = row[:, first : first + 128] - pivot[...]
        sums[0] += off
        sums[1] += off * off

    @pl.when(step == pl.num_programs(0) - 1)
    def _():
        steps = projected.shape[0]
        features = steps * tile
        off_mean = jnp.sum(sums[0], axis=1, keepdims=True) * (1.0 / features)
        mean = pivot[:, :1] + off_mean
        variance = jnp.sum(sums[1], axis=1, keepdims=True) * (1.0 / features) - off_mean * off_mean
        variance = jnp.maximum(variance, 0.0)
        inverse = lax.rsqrt(variance + 1e-06)
        patches = None
        for i in range(steps):
            lanes = slice(i * tile, (i + 1) * tile)
            normed = (projected[i] - mean) * inverse * (1.0 + scale_ref[:, lanes]) + shift_ref[:, lanes]
            part = lax.dot_general(
                normed.astype(jnp.bfloat16),
                w_final_ref[:, lanes],
                (((1,), (1,)), ((), ())),
                preferred_element_type=jnp.float32,
            )
            patches = part if patches is None else patches + part
        patches = patches.astype(jnp.bfloat16)
        channels = patches.shape[1]
        half = channels // 2
        source = lax.broadcasted_iota(jnp.int32, (channels, channels), 0)
        target = lax.broadcasted_iota(jnp.int32, (channels, channels), 1)
        q, p, c = target // half, (target // LATENT_CH) % 2, target % LATENT_CH
        lane_order = (source == 4 * c + 2 * p + q).astype(jnp.bfloat16)
        to = lax.broadcasted_iota(jnp.int32, (tokens, tokens), 0)
        at = lax.broadcasted_iota(jnp.int32, (tokens, tokens), 1)
        share = planes * rows_dev
        place = ((to // share) ^ heads_at) * share
        place = place + (((to % share) // rows_dev) ^ plane_at) * rows_dev + to % rows_dev
        row_order = (at == place).astype(jnp.bfloat16)
        cells = jnp.dot(patches, lane_order, preferred_element_type=jnp.float32)
        cells = jnp.dot(row_order, cells.astype(jnp.bfloat16), preferred_element_type=jnp.float32)
        cells = cells.astype(jnp.bfloat16)
        even_ref[...] = cells[:, :half]
        odd_ref[...] = cells[:, half:]


def final_layer(where, attended, targets, partial, w_out, scale_mod, shift_mod, w_final, rows_dev, planes):
    sources, rows, width = attended[0].shape
    features = w_out.shape[1]
    steps, tokens, tile = partial.shape
    channels = w_final.shape[1]
    whole = lambda shape: pl.BlockSpec(shape, lambda i, *_: (0,) * len(shape))
    result = jax.ShapeDtypeStruct((tokens, channels // 2), jnp.bfloat16)
    return pl.pallas_call(
        functools.partial(final_kernel, targets=targets, planes=planes, rows_dev=rows_dev),
        grid_spec=pltpu.PrefetchScalarGridSpec(
            num_scalar_prefetch=1,
            grid=(steps,),
            in_specs=projection_specs(attended, targets, tile)
            + [
                pl.BlockSpec((None, tokens, tile), lambda i, *_: (i, 0, 0)),
                whole((1, features)),
                whole((1, features)),
                whole((channels, features)),
            ],
            out_specs=[whole((tokens, channels // 2))] * 2,
            scratch_shapes=[
                pltpu.VMEM((tokens, len(targets) * width), jnp.bfloat16),
                pltpu.VMEM((steps, tokens, tile), jnp.float32),
                pltpu.VMEM((tokens, 128), jnp.float32),
                pltpu.VMEM((2, tokens, 128), jnp.float32),
            ],
        ),
        out_shape=[result] * 2,
        compiler_params=pltpu.CompilerParams(vmem_limit_bytes=VMEM_LIMIT),
    )(where, *attended, *[w_out] * len(targets), partial, scale_mod[None], shift_mod[None], w_final.T)


def convolve_kernel(where_ref, even_ref, odd_ref, left_ref, right_ref, w_ref, bias_ref, out_ref, latent):
    frames, cols, _, ch = latent.shape
    rows = even_ref.shape[0] // frames
    height = 2 * rows
    even = even_ref[...].astype(jnp.float32)
    odd = odd_ref[...].astype(jnp.float32)
    left = jnp.where(where_ref[2] == 0, even, left_ref[...].astype(jnp.float32))
    right = jnp.where(where_ref[2] == where_ref[3] - 1, odd, right_ref[...].astype(jnp.float32))
    for x, cells in enumerate((left, even, odd, right)):
        for f in range(frames):
            own = cells[f * rows : (f + 1) * rows]
            for p in range(2):
                latent[f, x, pl.ds(8 + p, rows, stride=2), :] = own[:, p * ch : (p + 1) * ch]
            latent[f, x, 7:8, :] = own[:1, :ch]
            latent[f, x, 8 + height : 9 + height, :] = own[rows - 1 :, ch:]
    depth = 9 * ch
    for x in range(cols - 2):
        stacked = []
        for f in range(frames):
            taps = [latent[f, x + b, 7 + e : 7 + e + height, :] for b in range(3) for e in range(3)]
            stacked.append(jnp.concatenate(taps, axis=1).astype(jnp.bfloat16))
        stacked = [stacked[0]] * 2 + stacked
        acc = None
        for a in range(3):
            flat = jnp.concatenate(stacked[a : a + frames], axis=0)
            part = jnp.dot(
                flat, w_ref[a * depth : (a + 1) * depth, :], preferred_element_type=jnp.float32
            )
            acc = part if acc is None else acc + part
        acc = (acc + bias_ref[...]).astype(jnp.bfloat16)
        out_ref[:, x] = acc.reshape(frames, height, acc.shape[1])


def convolve(where, even, odd, left, right, conv_weight, conv_bias):
    rows = even.shape[0] // FRAMES
    channels = conv_weight.shape[1]
    smem = pl.BlockSpec(memory_space=pltpu.SMEM)
    vmem = pl.BlockSpec(memory_space=pltpu.VMEM)
    return pl.pallas_call(
        convolve_kernel,
        in_specs=[smem] + [vmem] * 6,
        out_specs=vmem,
        out_shape=jax.ShapeDtypeStruct((FRAMES, 2, 2 * rows, channels), jnp.bfloat16),
        scratch_shapes=[pltpu.VMEM((FRAMES, 4, 2 * rows + 16, LATENT_CH), jnp.float32)],
        compiler_params=pltpu.CompilerParams(vmem_limit_bytes=VMEM_LIMIT),
    )(where, even, odd, left, right, conv_weight, conv_bias[None])


def shards(queries, keys, values, w_out, shift_mod, scale_mod, w_final, conv_weight, conv_bias):
    groups = lax.axis_size("heads")
    planes = lax.axis_size("plane")
    heads_at = lax.axis_index("heads")
    plane_at = lax.axis_index("plane")
    devices = groups * planes
    tokens = queries.shape[0]
    rows_dev = tokens // devices
    where = jnp.stack(
        [heads_at, plane_at, heads_at * planes + plane_at, jnp.int32(devices)]
    ).astype(jnp.int32)

    made = bundles(where, queries, keys, values, groups, planes, range(groups))
    got = {r: swap(made[r], "heads", r) if r else made[r] for r in range(groups)}

    both_parts, share = 2 * tokens, tokens // planes
    held = {r: [got[r]] for r in range(groups)}
    for r in (0, 1, 2, 3):
        for d in range(2, planes, 2):
            asked = got[r][both_parts + d * share : both_parts + (d + 2) * share]
            held[r].append(swap(jnp.concatenate([got[r][:both_parts], asked], axis=0), "plane", d))

    keys_values, asked = [], {}
    for distances in ((0, 1), (2,), (3,)):
        passed = [h[:both_parts] for r in distances for h in held[r]]
        passed += [h[both_parts + share : both_parts + 2 * share] for r in distances for h in held[r]]
        mine = jnp.concatenate(passed, axis=0)
        other = swap(mine, "plane", 1)
        keys_values += [mine, other]
        half = planes // 2
        first = both_parts * half * len(distances)
        for n, r in enumerate(distances):
            start = first + n * half * share
            asked[r] = jnp.concatenate(
                [h[both_parts : both_parts + share] for h in held[r]]
                + [other[start : start + half * share]],
                axis=0,
            )
    asked = [asked[r] for r in range(groups)]

    near, far = (0, 3), (2, 1)
    results = {}
    for targets in ((3,), (2,), (1, 0)):
        for t, o in zip(targets, attend(asked, keys_values, targets, planes)):
            results[t] = o if t == 0 else swap(o, "heads", t)
    partial = project(where, [results[t] for t in near], near, w_out, 512)
    sent = [results[t] for t in far]
    even, odd = final_layer(
        where, sent, far, partial, w_out, scale_mod, shift_mod, w_final, rows_dev, planes
    )
    both = ("heads", "plane")
    left = lax.ppermute(odd, both, [(i, i + 1) for i in range(devices - 1)])
    right = lax.ppermute(even, both, [(i + 1, i) for i in range(devices - 1)])
    return convolve(where, even, odd, left, right, conv_weight, conv_bias)


def solution(mesh):
    groups, seq = mesh.devices.shape
    split = Mesh(
        mesh.devices.reshape(groups, HEAD_GROUPS, seq // HEAD_GROUPS), ("groups", "heads", "plane")
    )
    by_token = P(("groups", "heads", "plane"), None)
    placed = (by_token, by_token, by_token, P(), P("groups"), P("groups"), P(), P(), P())
    return jax.shard_map(
        shards,
        mesh=split,
        in_specs=placed,
        out_specs=P("groups", ("heads", "plane"), None, None),
        check_vma=False,
    )
```

```python
import functools
import math

import jax
import jax.numpy as jnp
from jax import lax
from jax.experimental import pallas as pl
from jax.experimental.pallas import tpu as pltpu
from jax.sharding import Mesh
from jax.sharding import PartitionSpec as P

HEAD_DIM = 128
HEAD_GROUPS = 4
CHUNKS = ((0, 1), (1, 3))
LATENT_CH = 16
FRAMES = 4
VMEM_LIMIT = 16 * 1024 * 1024
EXP2_SCALE = math.log2(math.e) / math.sqrt(HEAD_DIM)


def swap(source, axis, distance):
    count = lax.axis_size(axis)
    return lax.ppermute(source, axis, [(i, i ^ distance) for i in range(count)])


def bundle_kernel(where_ref, *refs, groups, planes, distances):
    tokens = refs[0].shape[0]
    rows_dev = tokens // (groups * planes)
    to = lax.broadcasted_iota(jnp.int32, (tokens, tokens), 0)
    at = lax.broadcasted_iota(jnp.int32, (tokens, tokens), 1)
    j, t, row = to // (groups * rows_dev), (to // rows_dev) % groups, to % rows_dev
    count = len(distances)
    cut = [refs[n * count : (n + 1) * count] for n in range(3)]
    out_refs = refs[3 * count :]
    for n, (r, q_ref, k_ref, v_ref) in enumerate(zip(distances, *cut)):
        group = where_ref[0] ^ r
        place = row * (groups * planes) + (t ^ group) * planes + (j ^ where_ref[1])
        order = (at == place).astype(jnp.bfloat16)
        mixed = jnp.dot(order, q_ref[...], preferred_element_type=jnp.float32).astype(jnp.bfloat16)
        for c, (low, high) in enumerate(CHUNKS):
            lanes = slice(low * HEAD_DIM, high * HEAD_DIM)
            out_ref = out_refs[c * count + n]
            out_ref[:tokens] = k_ref[:, lanes]
            out_ref[tokens : 2 * tokens] = v_ref[:, lanes]
            out_ref[2 * tokens :] = mixed[:, lanes]


def bundles(where, queries, keys, values, groups, planes, distances):
    def cut(source, r):
        width = source.shape[1] // groups
        return lax.dynamic_slice_in_dim(source, (lax.axis_index("heads") ^ r) * width, width, axis=1)

    tokens = queries.shape[0]
    vmem = pl.BlockSpec(memory_space=pltpu.VMEM)
    return pl.pallas_call(
        functools.partial(bundle_kernel, groups=groups, planes=planes, distances=distances),
        in_specs=[pl.BlockSpec(memory_space=pltpu.SMEM)] + [vmem] * (3 * len(distances)),
        out_specs=[vmem] * (len(distances) * len(CHUNKS)),
        out_shape=[
            jax.ShapeDtypeStruct((3 * tokens, (high - low) * HEAD_DIM), jnp.bfloat16)
            for low, high in CHUNKS
            for _ in distances
        ],
        compiler_params=pltpu.CompilerParams(vmem_limit_bytes=VMEM_LIMIT),
    )(where, *[cut(source, r) for source in (queries, keys, values) for r in distances])


def attend_kernel(*refs, sources, planes, blocks, part, targets, rows_step):
    q_refs = refs[:sources]
    kv_refs = refs[sources : sources + len(blocks)]
    o_refs = refs[sources + len(blocks) :]
    tokens, width = q_refs[0].shape
    rows = tokens // sources
    rows_dev = rows // planes
    to = lax.broadcasted_iota(jnp.int32, (tokens, tokens), 0)
    at = lax.broadcasted_iota(jnp.int32, (tokens, tokens), 1)
    t, j, row = to // rows, (to // rows_dev) % planes, to % rows_dev
    place = ((j % 2) * (planes // 2) + j // 2) * rows + t * rows_dev + row
    order = (at == place).astype(jnp.bfloat16)
    asked = [
        jnp.dot(order, q[...], preferred_element_type=jnp.float32).astype(jnp.bfloat16) for q in q_refs
    ]
    works = [
        (h, range(first, min(first + rows_step, len(targets))))
        for h in range(width // HEAD_DIM)
        for first in range(0, len(targets), rows_step)
    ]

    def taken(ref, count, h, which):
        cut = ref[: count * 2 * part, h * HEAD_DIM : (h + 1) * HEAD_DIM]
        return cut.reshape(count, 2, part, HEAD_DIM)[:, which].reshape(count * part, HEAD_DIM)

    def scores_of(work):
        h, block = work
        lanes = slice(h * HEAD_DIM, (h + 1) * HEAD_DIM)
        query = jnp.concatenate(
            [q[targets[i] * rows : (targets[i] + 1) * rows, lanes] for i in block for q in asked], axis=0
        )
        return [
            lax.dot_general(
                query,
                taken(kv, count, h, 0),
                (((1,), (1,)), ((), ())),
                preferred_element_type=jnp.float32,
            )
            for kv, count in zip(kv_refs, blocks)
        ]

    def finish(work, scores):
        h, block = work
        peak = functools.reduce(jnp.maximum, [jnp.max(s, axis=1, keepdims=True) for s in scores])
        peak = peak * EXP2_SCALE
        summed = None
        for s, kv, count in zip(scores, kv_refs, blocks):
            weights = jnp.exp2(s * EXP2_SCALE - peak).astype(jnp.bfloat16)
            value = taken(kv, count, h, 1)
            value = jnp.concatenate([value, jnp.ones_like(value)], axis=1)
            product = jnp.dot(weights, value, preferred_element_type=jnp.float32)
            summed = product if summed is None else summed + product
        out = (summed[:, :HEAD_DIM] / summed[:, HEAD_DIM:]).astype(jnp.bfloat16)
        for n, i in enumerate(block):
            for r in range(sources):
                first = (n * sources + r) * rows
                o_refs[i][targets[i] ^ r, :, h * HEAD_DIM : (h + 1) * HEAD_DIM] = out[first : first + rows]

    scores = scores_of(works[0])
    for n, work in enumerate(works):
        following = scores_of(works[n + 1]) if n + 1 < len(works) else None
        finish(work, scores)
        scores = following


def attend(queries, keys_values, targets, planes):
    sources = len(queries)
    tokens, width = queries[0].shape
    rows = tokens // sources
    blocks = [kv.shape[0] // (2 * tokens) for kv in keys_values]
    key_count = sum(blocks) * tokens
    small = key_count <= 4096
    rows_step, step_width = (2, width) if small else (1, HEAD_DIM)
    score_bytes = rows_step * tokens * key_count * 4
    limit = 8 * key_count * step_width + 3 * score_bytes + 6 * 1024 * 1024
    return pl.pallas_call(
        functools.partial(
            attend_kernel,
            sources=sources,
            planes=planes,
            blocks=blocks,
            part=tokens,
            targets=targets,
            rows_step=rows_step,
        ),
        grid=(width // step_width,),
        in_specs=[pl.BlockSpec((tokens, step_width), lambda h: (0, h))] * sources
        + [pl.BlockSpec((kv.shape[0], step_width), lambda h: (0, h)) for kv in keys_values],
        out_specs=[pl.BlockSpec((sources, rows, step_width), lambda h: (0, 0, h))] * len(targets),
        out_shape=[jax.ShapeDtypeStruct((sources, rows, width), jnp.bfloat16)] * len(targets),
        compiler_params=pltpu.CompilerParams(vmem_limit_bytes=min(limit, 60 * 1024 * 1024)),
    )(*queries, *keys_values)


def projection_of(o_refs, w_refs, lined):
    tokens = lined.shape[0]
    first = 0
    for o_ref in o_refs:
        width = o_ref.shape[2]
        lined[:, first : first + width] = o_ref[...].reshape(tokens, width)
        first += width
    weights = jnp.concatenate([w[...] for w in w_refs], axis=0)
    return jnp.dot(lined[...], weights, preferred_element_type=jnp.float32)


def row_blocks(taken, group_heads):
    blocks = []
    for target, low, o in taken:
        heads = o.shape[2] // HEAD_DIM
        step = heads if group_heads % heads == 0 and low % heads == 0 else 1
        blocks += [
            (target, (low + n) // step, step, group_heads // step) for n in range(0, heads, step)
        ]
    return blocks


def projection_specs(taken, tile, group_heads):
    whole = [pl.BlockSpec(o.shape, lambda i, *_: (0, 0, 0)) for _, _, o in taken]
    return whole + [
        pl.BlockSpec(
            (HEAD_DIM * step, tile),
            lambda i, where, target=target, block=block, count=count: (
                (where[0] ^ target) * count + block,
                i,
            ),
        )
        for target, block, step, count in row_blocks(taken, group_heads)
    ]


def project_kernel(where_ref, *refs, count):
    out_ref, lined = refs[-2:]
    out_ref[...] = projection_of(refs[:count], refs[count:-2], lined)


def project(where, taken, w_out, tile):
    sources, rows, _ = taken[0][2].shape
    tokens = sources * rows
    depth = sum(o.shape[2] for _, _, o in taken)
    inner, features = w_out.shape
    return pl.pallas_call(
        functools.partial(project_kernel, count=len(taken)),
        grid_spec=pltpu.PrefetchScalarGridSpec(
            num_scalar_prefetch=1,
            grid=(features // tile,),
            in_specs=projection_specs(taken, tile, inner // HEAD_DIM // HEAD_GROUPS),
            out_specs=pl.BlockSpec((None, tokens, tile), lambda i, *_: (i, 0, 0)),
            scratch_shapes=[pltpu.VMEM((tokens, depth), jnp.bfloat16)],
        ),
        out_shape=jax.ShapeDtypeStruct((features // tile, tokens, tile), jnp.float32),
        compiler_params=pltpu.CompilerParams(vmem_limit_bytes=VMEM_LIMIT),
    )(where, *[o for _, _, o in taken], *[w_out] * len(row_blocks(taken, inner // HEAD_DIM // HEAD_GROUPS)))


def final_kernel(where_ref, *refs, count, planes, rows_dev):
    partial_ref, scale_ref, shift_ref, w_final_ref, even_ref, odd_ref, lined, projected = refs[-8:]
    step = pl.program_id(0)
    heads_at, plane_at = where_ref[0], where_ref[1]
    tokens = lined.shape[0]
    tile = partial_ref.shape[1]
    projected[step] = partial_ref[...] + projection_of(refs[:count], refs[count:-8], lined)

    @pl.when(step == pl.num_programs(0) - 1)
    def _():
        steps = projected.shape[0]
        features = steps * tile
        total = projected[0]
        for i in range(1, steps):
            total = total + projected[i]
        mean = jnp.sum(total, axis=1, keepdims=True) * (1.0 / features)
        squares = None
        for i in range(steps):
            centered = projected[i] - mean
            squares = centered * centered if squares is None else squares + centered * centered
        variance = jnp.sum(squares, axis=1, keepdims=True) * (1.0 / features)
        inverse = lax.rsqrt(variance + 1e-06)
        patches = None
        for i in range(steps):
            lanes = slice(i * tile, (i + 1) * tile)
            normed = (projected[i] - mean) * inverse * (1.0 + scale_ref[:, lanes]) + shift_ref[:, lanes]
            part = lax.dot_general(
                normed.astype(jnp.bfloat16),
                w_final_ref[:, lanes],
                (((1,), (1,)), ((), ())),
                preferred_element_type=jnp.float32,
            )
            patches = part if patches is None else patches + part
        patches = patches.astype(jnp.bfloat16)
        channels = patches.shape[1]
        half = channels // 2
        source = lax.broadcasted_iota(jnp.int32, (channels, channels), 0)
        target = lax.broadcasted_iota(jnp.int32, (channels, channels), 1)
        q, p, c = target // half, (target // LATENT_CH) % 2, target % LATENT_CH
        lane_order = (source == 4 * c + 2 * p + q).astype(jnp.bfloat16)
        to = lax.broadcasted_iota(jnp.int32, (tokens, tokens), 0)
        at = lax.broadcasted_iota(jnp.int32, (tokens, tokens), 1)
        share = planes * rows_dev
        place = ((to // share) ^ heads_at) * share
        place = place + (((to % share) // rows_dev) ^ plane_at) * rows_dev + to % rows_dev
        row_order = (at == place).astype(jnp.bfloat16)
        cells = jnp.dot(patches, lane_order, preferred_element_type=jnp.float32)
        cells = jnp.dot(row_order, cells.astype(jnp.bfloat16), preferred_element_type=jnp.float32)
        cells = cells.astype(jnp.bfloat16)
        even_ref[...] = cells[:, :half]
        odd_ref[...] = cells[:, half:]


def final_layer(where, taken, partial, w_out, scale_mod, shift_mod, w_final, rows_dev, planes):
    depth = sum(o.shape[2] for _, _, o in taken)
    inner, features = w_out.shape
    steps, tokens, tile = partial.shape
    channels = w_final.shape[1]
    whole = lambda shape: pl.BlockSpec(shape, lambda i, *_: (0,) * len(shape))
    result = jax.ShapeDtypeStruct((tokens, channels // 2), jnp.bfloat16)
    return pl.pallas_call(
        functools.partial(final_kernel, count=len(taken), planes=planes, rows_dev=rows_dev),
        grid_spec=pltpu.PrefetchScalarGridSpec(
            num_scalar_prefetch=1,
            grid=(steps,),
            in_specs=projection_specs(taken, tile, inner // HEAD_DIM // HEAD_GROUPS)
            + [
                pl.BlockSpec((None, tokens, tile), lambda i, *_: (i, 0, 0)),
                whole((1, features)),
                whole((1, features)),
                whole((channels, features)),
            ],
            out_specs=[whole((tokens, channels // 2))] * 2,
            scratch_shapes=[
                pltpu.VMEM((tokens, depth), jnp.bfloat16),
                pltpu.VMEM((steps, tokens, tile), jnp.float32),
            ],
        ),
        out_shape=[result] * 2,
        compiler_params=pltpu.CompilerParams(vmem_limit_bytes=VMEM_LIMIT),
    )(
        where,
        *[o for _, _, o in taken],
        *[w_out] * len(row_blocks(taken, inner // HEAD_DIM // HEAD_GROUPS)),
        partial,
        scale_mod[None],
        shift_mod[None],
        w_final.T,
    )


def convolve_kernel(where_ref, even_ref, odd_ref, left_ref, right_ref, w_ref, bias_ref, out_ref, latent):
    frames, cols, _, ch = latent.shape
    rows = even_ref.shape[0] // frames
    height = 2 * rows
    even = even_ref[...].astype(jnp.float32)
    odd = odd_ref[...].astype(jnp.float32)
    left = jnp.where(where_ref[2] == 0, even, left_ref[...].astype(jnp.float32))
    right = jnp.where(where_ref[2] == where_ref[3] - 1, odd, right_ref[...].astype(jnp.float32))
    for x, cells in enumerate((left, even, odd, right)):
        for f in range(frames):
            own = cells[f * rows : (f + 1) * rows]
            for p in range(2):
                latent[f, x, pl.ds(8 + p, rows, stride=2), :] = own[:, p * ch : (p + 1) * ch]
            latent[f, x, 7:8, :] = own[:1, :ch]
            latent[f, x, 8 + height : 9 + height, :] = own[rows - 1 :, ch:]
    depth = 9 * ch
    for x in range(cols - 2):
        stacked = []
        for f in range(frames):
            taps = [latent[f, x + b, 7 + e : 7 + e + height, :] for b in range(3) for e in range(3)]
            stacked.append(jnp.concatenate(taps, axis=1).astype(jnp.bfloat16))
        stacked = [stacked[0]] * 2 + stacked
        acc = None
        for a in range(3):
            flat = jnp.concatenate(stacked[a : a + frames], axis=0)
            part = jnp.dot(
                flat, w_ref[a * depth : (a + 1) * depth, :], preferred_element_type=jnp.float32
            )
            acc = part if acc is None else acc + part
        acc = (acc + bias_ref[...]).astype(jnp.bfloat16)
        out_ref[:, x] = acc.reshape(frames, height, acc.shape[1])


def convolve(where, even, odd, left, right, conv_weight, conv_bias):
    rows = even.shape[0] // FRAMES
    channels = conv_weight.shape[1]
    smem = pl.BlockSpec(memory_space=pltpu.SMEM)
    vmem = pl.BlockSpec(memory_space=pltpu.VMEM)
    return pl.pallas_call(
        convolve_kernel,
        in_specs=[smem] + [vmem] * 6,
        out_specs=vmem,
        out_shape=jax.ShapeDtypeStruct((FRAMES, 2, 2 * rows, channels), jnp.bfloat16),
        scratch_shapes=[pltpu.VMEM((FRAMES, 4, 2 * rows + 16, LATENT_CH), jnp.float32)],
        compiler_params=pltpu.CompilerParams(vmem_limit_bytes=VMEM_LIMIT),
    )(where, even, odd, left, right, conv_weight, conv_bias[None])


def after(value, *others):
    return lax.optimization_barrier((value,) + others)[0] if others else value


def shards(queries, keys, values, w_out, shift_mod, scale_mod, w_final, conv_weight, conv_bias):
    groups = lax.axis_size("heads")
    planes = lax.axis_size("plane")
    heads_at = lax.axis_index("heads")
    plane_at = lax.axis_index("plane")
    devices = groups * planes
    tokens = queries.shape[0]
    rows_dev = tokens // devices
    where = jnp.stack(
        [heads_at, plane_at, heads_at * planes + plane_at, jnp.int32(devices)]
    ).astype(jnp.int32)

    made = bundles(where, queries, keys, values, groups, planes, range(groups))
    both_parts, share = 2 * tokens, tokens // planes
    chunks, done, arrived = [], [], []
    for chunk, (low, high) in enumerate(CHUNKS):
        mine_made = made[chunk * groups : (chunk + 1) * groups]
        got = {r: swap(mine_made[r], "heads", r) if r else mine_made[r] for r in range(groups)}

        held = {r: [got[r]] for r in range(groups)}
        for r in (0, 1, 2, 3):
            for d in range(2, planes, 2):
                asked = got[r][both_parts + d * share : both_parts + (d + 2) * share]
                sent = jnp.concatenate([got[r][:both_parts], asked], axis=0)
                held[r].append(swap(after(sent, *done) if r == 3 else sent, "plane", d))

        keys_values, asked = [], {}
        for distances in ((0, 1), (2,), (3,)):
            passed = [h[:both_parts] for r in distances for h in held[r]]
            passed += [h[both_parts + share : both_parts + 2 * share] for r in distances for h in held[r]]
            mine = jnp.concatenate(passed, axis=0)
            if distances == (3,):
                mine = after(mine, *arrived)
            other = swap(mine, "plane", 1)
            keys_values += [mine, other]
            half = planes // 2
            first = both_parts * half * len(distances)
            for n, r in enumerate(distances):
                start = first + n * half * share
                asked[r] = jnp.concatenate(
                    [h[both_parts : both_parts + share] for h in held[r]]
                    + [other[start : start + half * share]],
                    axis=0,
                )
        asked = [asked[r] for r in range(groups)]

        taken, done = {}, []
        for targets in ((3, 2), (1, 0)):
            for target, o in zip(targets, attend(asked, keys_values, targets, planes)):
                done.append(o)
                taken[target] = (target, low, swap(o, "heads", target) if target else o)
        chunks.append(taken)
        arrived = [taken[target][2] for target in range(1, groups)]

    near = [chunk[target] for chunk in chunks[:-1] for target in (0, 1, 2, 3)]
    near += [chunks[-1][target] for target in (0, 3)]
    far = [chunks[-1][target] for target in (2, 1)]
    partial = project(where, near, w_out, 512)
    even, odd = final_layer(
        where, far, partial, w_out, scale_mod, shift_mod, w_final, rows_dev, planes
    )
    both = ("heads", "plane")
    left = lax.ppermute(odd, both, [(i, i + 1) for i in range(devices - 1)])
    right = lax.ppermute(even, both, [(i + 1, i) for i in range(devices - 1)])
    return convolve(where, even, odd, left, right, conv_weight, conv_bias)


def solution(mesh):
    groups, seq = mesh.devices.shape
    split = Mesh(
        mesh.devices.reshape(groups, HEAD_GROUPS, seq // HEAD_GROUPS), ("groups", "heads", "plane")
    )
    by_token = P(("groups", "heads", "plane"), None)
    placed = (by_token, by_token, by_token, P(), P("groups"), P("groups"), P(), P(), P())
    return jax.shard_map(
        shards,
        mesh=split,
        in_specs=placed,
        out_specs=P("groups", ("heads", "plane"), None, None),
        check_vma=False,
    )
```

```python
import functools
import math

import jax
import jax.numpy as jnp
from jax import lax
from jax.experimental import pallas as pl
from jax.experimental.pallas import tpu as pltpu
from jax.sharding import Mesh
from jax.sharding import PartitionSpec as P

HEAD_DIM = 128
HEAD_GROUPS = 4
LATENT_CH = 16
FRAMES = 4
VMEM_LIMIT = 16 * 1024 * 1024
EXP2_SCALE = math.log2(math.e) / math.sqrt(HEAD_DIM)


def swap(source, axis, distance):
    count = lax.axis_size(axis)
    return lax.ppermute(source, axis, [(i, i ^ distance) for i in range(count)])


def bundle_kernel(where_ref, qkv_ref, *out_refs, groups, planes, distances):
    tokens, width = qkv_ref.shape[0] // 3, qkv_ref.shape[1]
    group_width = width // groups
    rows_dev = tokens // (groups * planes)
    to = lax.broadcasted_iota(jnp.int32, (tokens, tokens), 0)
    at = lax.broadcasted_iota(jnp.int32, (tokens, tokens), 1)
    j, t, row = to // (groups * rows_dev), (to // rows_dev) % groups, to % rows_dev
    for r, out_ref in zip(distances, out_refs):
        group = where_ref[0] ^ r
        lanes = pl.ds(pl.multiple_of(group * group_width, 128), group_width)
        place = row * (groups * planes) + (t ^ group) * planes + (j ^ where_ref[1])
        order = (at == place).astype(jnp.bfloat16)
        out_ref[: 2 * tokens] = qkv_ref[tokens:, lanes]
        mixed = jnp.dot(order, qkv_ref[:tokens, lanes], preferred_element_type=jnp.float32)
        out_ref[2 * tokens :] = mixed.astype(jnp.bfloat16)


def bundles(where, queries, keys, values, groups, planes, distances):
    tokens, width = queries.shape
    vmem = pl.BlockSpec(memory_space=pltpu.VMEM)
    result = jax.ShapeDtypeStruct((3 * tokens, width // groups), jnp.bfloat16)
    return pl.pallas_call(
        functools.partial(bundle_kernel, groups=groups, planes=planes, distances=distances),
        in_specs=[pl.BlockSpec(memory_space=pltpu.SMEM), vmem],
        out_specs=[vmem] * len(distances),
        out_shape=[result] * len(distances),
        compiler_params=pltpu.CompilerParams(vmem_limit_bytes=VMEM_LIMIT),
    )(where, jnp.concatenate([queries, keys, values], axis=0))


def after(value, *others):
    return lax.optimization_barrier((value,) + others)[0]


def attend_kernel(*refs, sources, planes, blocks, part, targets, rows_step):
    q_refs = refs[:sources]
    kv_refs = refs[sources : sources + len(blocks)]
    o_refs = refs[sources + len(blocks) :]
    tokens, width = q_refs[0].shape
    rows = tokens // sources
    rows_dev = rows // planes
    to = lax.broadcasted_iota(jnp.int32, (tokens, tokens), 0)
    at = lax.broadcasted_iota(jnp.int32, (tokens, tokens), 1)
    t, j, row = to // rows, (to // rows_dev) % planes, to % rows_dev
    place = ((j % 2) * (planes // 2) + j // 2) * rows + t * rows_dev + row
    order = (at == place).astype(jnp.bfloat16)
    asked = [
        jnp.dot(order, q[...], preferred_element_type=jnp.float32).astype(jnp.bfloat16) for q in q_refs
    ]
    works = [
        (h, range(first, min(first + rows_step, len(targets))))
        for h in range(width // HEAD_DIM)
        for first in range(0, len(targets), rows_step)
    ]

    def taken(ref, count, h, which):
        cut = ref[: count * 2 * part, h * HEAD_DIM : (h + 1) * HEAD_DIM]
        return cut.reshape(count, 2, part, HEAD_DIM)[:, which].reshape(count * part, HEAD_DIM)

    def scores_of(work):
        h, block = work
        lanes = slice(h * HEAD_DIM, (h + 1) * HEAD_DIM)
        query = jnp.concatenate(
            [q[targets[i] * rows : (targets[i] + 1) * rows, lanes] for i in block for q in asked], axis=0
        )
        return [
            lax.dot_general(
                query,
                taken(kv, count, h, 0),
                (((1,), (1,)), ((), ())),
                preferred_element_type=jnp.float32,
            )
            for kv, count in zip(kv_refs, blocks)
        ]

    def finish(work, scores):
        h, block = work
        peak = functools.reduce(jnp.maximum, [jnp.max(s, axis=1, keepdims=True) for s in scores])
        peak = peak * EXP2_SCALE
        summed = None
        for s, kv, count in zip(scores, kv_refs, blocks):
            weights = jnp.exp2(s * EXP2_SCALE - peak).astype(jnp.bfloat16)
            value = taken(kv, count, h, 1)
            value = jnp.concatenate([value, jnp.ones_like(value)], axis=1)
            product = jnp.dot(weights, value, preferred_element_type=jnp.float32)
            summed = product if summed is None else summed + product
        out = (summed[:, :HEAD_DIM] / summed[:, HEAD_DIM:]).astype(jnp.bfloat16)
        for n, i in enumerate(block):
            for r in range(sources):
                first = (n * sources + r) * rows
                o_refs[i][targets[i] ^ r, :, h * HEAD_DIM : (h + 1) * HEAD_DIM] = out[first : first + rows]

    scores = scores_of(works[0])
    for n, work in enumerate(works):
        following = scores_of(works[n + 1]) if n + 1 < len(works) else None
        finish(work, scores)
        scores = following


def attend(queries, keys_values, targets, planes):
    sources = len(queries)
    tokens, width = queries[0].shape
    rows = tokens // sources
    blocks = [kv.shape[0] // (2 * tokens) for kv in keys_values]
    key_count = sum(blocks) * tokens
    small = key_count <= 4096
    rows_step, step_width = (2, width) if small else (1, HEAD_DIM)
    score_bytes = rows_step * tokens * key_count * 4
    limit = 8 * key_count * step_width + 3 * score_bytes + 6 * 1024 * 1024
    return pl.pallas_call(
        functools.partial(
            attend_kernel,
            sources=sources,
            planes=planes,
            blocks=blocks,
            part=tokens,
            targets=targets,
            rows_step=rows_step,
        ),
        grid=(width // step_width,),
        in_specs=[pl.BlockSpec((tokens, step_width), lambda h: (0, h))] * sources
        + [pl.BlockSpec((kv.shape[0], step_width), lambda h: (0, h)) for kv in keys_values],
        out_specs=[pl.BlockSpec((sources, rows, step_width), lambda h: (0, 0, h))] * len(targets),
        out_shape=[jax.ShapeDtypeStruct((sources, rows, width), jnp.bfloat16)] * len(targets),
        compiler_params=pltpu.CompilerParams(vmem_limit_bytes=min(limit, 60 * 1024 * 1024)),
    )(*queries, *keys_values)


def projection_of(o_refs, w_refs, lined):
    tokens, width = lined.shape[0], o_refs[0].shape[2]
    for n, o_ref in enumerate(o_refs):
        lined[:, n * width : (n + 1) * width] = o_ref[...].reshape(tokens, width)
    weights = jnp.concatenate([w[...] for w in w_refs], axis=0)
    return jnp.dot(lined[...], weights, preferred_element_type=jnp.float32)


def projection_specs(attended, targets, tile):
    o_spec = pl.BlockSpec(attended[0].shape, lambda i, *_: (0, 0, 0))
    width = attended[0].shape[2]
    return [o_spec] * len(targets) + [
        pl.BlockSpec((width, tile), lambda i, where, t=t: (where[0] ^ t, i)) for t in targets
    ]


def project_kernel(where_ref, *refs, targets):
    count = len(targets)
    out_ref, lined = refs[2 * count :]
    out_ref[...] = projection_of(refs[:count], refs[count : 2 * count], lined)


def project(where, attended, targets, w_out, tile):
    sources, rows, width = attended[0].shape
    tokens = sources * rows
    features = w_out.shape[1]
    return pl.pallas_call(
        functools.partial(project_kernel, targets=targets),
        grid_spec=pltpu.PrefetchScalarGridSpec(
            num_scalar_prefetch=1,
            grid=(features // tile,),
            in_specs=projection_specs(attended, targets, tile),
            out_specs=pl.BlockSpec((None, tokens, tile), lambda i, *_: (i, 0, 0)),
            scratch_shapes=[pltpu.VMEM((tokens, len(targets) * width), jnp.bfloat16)],
        ),
        out_shape=jax.ShapeDtypeStruct((features // tile, tokens, tile), jnp.float32),
        compiler_params=pltpu.CompilerParams(vmem_limit_bytes=VMEM_LIMIT),
    )(where, *attended, *[w_out] * len(targets))


def final_kernel(where_ref, *refs, targets, planes, rows_dev):
    count = len(targets)
    partial_ref, scale_ref, shift_ref, w_final_ref, even_ref, odd_ref, lined, projected = refs[2 * count :]
    step = pl.program_id(0)
    heads_at, plane_at = where_ref[0], where_ref[1]
    tokens = lined.shape[0]
    tile = partial_ref.shape[1]
    projected[step] = partial_ref[...] + projection_of(refs[:count], refs[count : 2 * count], lined)

    @pl.when(step == pl.num_programs(0) - 1)
    def _():
        steps = projected.shape[0]
        features = steps * tile
        total = projected[0]
        for i in range(1, steps):
            total = total + projected[i]
        mean = jnp.sum(total, axis=1, keepdims=True) * (1.0 / features)
        squares = None
        for i in range(steps):
            centered = projected[i] - mean
            squares = centered * centered if squares is None else squares + centered * centered
        variance = jnp.sum(squares, axis=1, keepdims=True) * (1.0 / features)
        inverse = lax.rsqrt(variance + 1e-06)
        patches = None
        for i in range(steps):
            lanes = slice(i * tile, (i + 1) * tile)
            normed = (projected[i] - mean) * inverse * (1.0 + scale_ref[:, lanes]) + shift_ref[:, lanes]
            part = lax.dot_general(
                normed.astype(jnp.bfloat16),
                w_final_ref[:, lanes],
                (((1,), (1,)), ((), ())),
                preferred_element_type=jnp.float32,
            )
            patches = part if patches is None else patches + part
        patches = patches.astype(jnp.bfloat16)
        channels = patches.shape[1]
        half = channels // 2
        source = lax.broadcasted_iota(jnp.int32, (channels, channels), 0)
        target = lax.broadcasted_iota(jnp.int32, (channels, channels), 1)
        q, p, c = target // half, (target // LATENT_CH) % 2, target % LATENT_CH
        lane_order = (source == 4 * c + 2 * p + q).astype(jnp.bfloat16)
        to = lax.broadcasted_iota(jnp.int32, (tokens, tokens), 0)
        at = lax.broadcasted_iota(jnp.int32, (tokens, tokens), 1)
        share = planes * rows_dev
        place = ((to // share) ^ heads_at) * share
        place = place + (((to % share) // rows_dev) ^ plane_at) * rows_dev + to % rows_dev
        row_order = (at == place).astype(jnp.bfloat16)
        cells = jnp.dot(patches, lane_order, preferred_element_type=jnp.float32)
        cells = jnp.dot(row_order, cells.astype(jnp.bfloat16), preferred_element_type=jnp.float32)
        cells = cells.astype(jnp.bfloat16)
        even_ref[...] = cells[:, :half]
        odd_ref[...] = cells[:, half:]


def final_layer(where, attended, targets, partial, w_out, scale_mod, shift_mod, w_final, rows_dev, planes):
    sources, rows, width = attended[0].shape
    features = w_out.shape[1]
    steps, tokens, tile = partial.shape
    channels = w_final.shape[1]
    whole = lambda shape: pl.BlockSpec(shape, lambda i, *_: (0,) * len(shape))
    result = jax.ShapeDtypeStruct((tokens, channels // 2), jnp.bfloat16)
    return pl.pallas_call(
        functools.partial(final_kernel, targets=targets, planes=planes, rows_dev=rows_dev),
        grid_spec=pltpu.PrefetchScalarGridSpec(
            num_scalar_prefetch=1,
            grid=(steps,),
            in_specs=projection_specs(attended, targets, tile)
            + [
                pl.BlockSpec((None, tokens, tile), lambda i, *_: (i, 0, 0)),
                whole((1, features)),
                whole((1, features)),
                whole((channels, features)),
            ],
            out_specs=[whole((tokens, channels // 2))] * 2,
            scratch_shapes=[
                pltpu.VMEM((tokens, len(targets) * width), jnp.bfloat16),
                pltpu.VMEM((steps, tokens, tile), jnp.float32),
            ],
        ),
        out_shape=[result] * 2,
        compiler_params=pltpu.CompilerParams(vmem_limit_bytes=VMEM_LIMIT),
    )(where, *attended, *[w_out] * len(targets), partial, scale_mod[None], shift_mod[None], w_final.T)


def convolve_kernel(where_ref, even_ref, odd_ref, left_ref, right_ref, w_ref, bias_ref, out_ref, latent):
    frames, cols, _, ch = latent.shape
    rows = even_ref.shape[0] // frames
    height = 2 * rows
    even = even_ref[...].astype(jnp.float32)
    odd = odd_ref[...].astype(jnp.float32)
    left = jnp.where(where_ref[2] == 0, even, left_ref[...].astype(jnp.float32))
    right = jnp.where(where_ref[2] == where_ref[3] - 1, odd, right_ref[...].astype(jnp.float32))
    for x, cells in enumerate((left, even, odd, right)):
        for f in range(frames):
            own = cells[f * rows : (f + 1) * rows]
            for p in range(2):
                latent[f, x, pl.ds(8 + p, rows, stride=2), :] = own[:, p * ch : (p + 1) * ch]
            latent[f, x, 7:8, :] = own[:1, :ch]
            latent[f, x, 8 + height : 9 + height, :] = own[rows - 1 :, ch:]
    depth = 9 * ch
    for x in range(cols - 2):
        stacked = []
        for f in range(frames):
            taps = [latent[f, x + b, 7 + e : 7 + e + height, :] for b in range(3) for e in range(3)]
            stacked.append(jnp.concatenate(taps, axis=1).astype(jnp.bfloat16))
        stacked = [stacked[0]] * 2 + stacked
        acc = None
        for a in range(3):
            flat = jnp.concatenate(stacked[a : a + frames], axis=0)
            part = jnp.dot(
                flat, w_ref[a * depth : (a + 1) * depth, :], preferred_element_type=jnp.float32
            )
            acc = part if acc is None else acc + part
        acc = (acc + bias_ref[...]).astype(jnp.bfloat16)
        out_ref[:, x] = acc.reshape(frames, height, acc.shape[1])


def convolve(where, even, odd, left, right, conv_weight, conv_bias):
    rows = even.shape[0] // FRAMES
    channels = conv_weight.shape[1]
    smem = pl.BlockSpec(memory_space=pltpu.SMEM)
    vmem = pl.BlockSpec(memory_space=pltpu.VMEM)
    return pl.pallas_call(
        convolve_kernel,
        in_specs=[smem] + [vmem] * 6,
        out_specs=vmem,
        out_shape=jax.ShapeDtypeStruct((FRAMES, 2, 2 * rows, channels), jnp.bfloat16),
        scratch_shapes=[pltpu.VMEM((FRAMES, 4, 2 * rows + 16, LATENT_CH), jnp.float32)],
        compiler_params=pltpu.CompilerParams(vmem_limit_bytes=VMEM_LIMIT),
    )(where, even, odd, left, right, conv_weight, conv_bias[None])


def shards(queries, keys, values, w_out, shift_mod, scale_mod, w_final, conv_weight, conv_bias):
    groups = lax.axis_size("heads")
    planes = lax.axis_size("plane")
    heads_at = lax.axis_index("heads")
    plane_at = lax.axis_index("plane")
    devices = groups * planes
    tokens = queries.shape[0]
    rows_dev = tokens // devices
    where = jnp.stack(
        [heads_at, plane_at, heads_at * planes + plane_at, jnp.int32(devices)]
    ).astype(jnp.int32)

    made = bundles(where, queries, keys, values, groups, planes, range(groups))
    got = {r: swap(made[r], "heads", r) if r else made[r] for r in range(groups)}

    both_parts, share = 2 * tokens, tokens // planes
    held = {r: [got[r]] for r in range(groups)}
    for r in (0, 1, 2, 3):
        for d in range(2, planes, 2):
            asked = got[r][both_parts + d * share : both_parts + (d + 2) * share]
            held[r].append(swap(jnp.concatenate([got[r][:both_parts], asked], axis=0), "plane", d))

    keys_values, asked = [], {}
    for distances in ((0, 1), (2,), (3,)):
        passed = [h[:both_parts] for r in distances for h in held[r]]
        passed += [h[both_parts + share : both_parts + 2 * share] for r in distances for h in held[r]]
        mine = jnp.concatenate(passed, axis=0)
        other = swap(mine, "plane", 1)
        keys_values += [mine, other]
        half = planes // 2
        first = both_parts * half * len(distances)
        for n, r in enumerate(distances):
            start = first + n * half * share
            asked[r] = jnp.concatenate(
                [h[both_parts : both_parts + share] for h in held[r]]
                + [other[start : start + half * share]],
                axis=0,
            )
    asked = [asked[r] for r in range(groups)]

    near, far = (0, 3), (2, 1)
    results = {}
    for targets in ((3,), (2,), (1, 0)):
        for t, o in zip(targets, attend(asked, keys_values, targets, planes)):
            results[t] = o if t == 0 else swap(o, "heads", t)
    partial = project(where, [results[t] for t in near], near, w_out, 512)
    sent = [results[t] for t in far]
    even, odd = final_layer(
        where, sent, far, partial, w_out, scale_mod, shift_mod, w_final, rows_dev, planes
    )
    both = ("heads", "plane")
    left = lax.ppermute(odd, both, [(i, i + 1) for i in range(devices - 1)])
    right = lax.ppermute(even, both, [(i + 1, i) for i in range(devices - 1)])
    return convolve(where, even, odd, left, right, conv_weight, conv_bias)


def solution(mesh):
    groups, seq = mesh.devices.shape
    split = Mesh(
        mesh.devices.reshape(groups, HEAD_GROUPS, seq // HEAD_GROUPS), ("groups", "heads", "plane")
    )
    by_token = P(("groups", "heads", "plane"), None)
    placed = (by_token, by_token, by_token, P(), P("groups"), P("groups"), P(), P(), P())
    return jax.shard_map(
        shards,
        mesh=split,
        in_specs=placed,
        out_specs=P("groups", ("heads", "plane"), None, None),
        check_vma=False,
    )
```

```python
import functools
import math

import jax
import jax.numpy as jnp
from jax import lax
from jax.experimental import pallas as pl
from jax.experimental.pallas import tpu as pltpu
from jax.sharding import Mesh
from jax.sharding import PartitionSpec as P

HEAD_DIM = 128
HEAD_GROUPS = 4
LATENT_CH = 16
FRAMES = 4
VMEM_LIMIT = 16 * 1024 * 1024
EXP2_SCALE = math.log2(math.e) / math.sqrt(HEAD_DIM)


def swap(source, axis, distance):
    count = lax.axis_size(axis)
    return lax.ppermute(source, axis, [(i, i ^ distance) for i in range(count)])


def bundle_kernel(where_ref, qkv_ref, *out_refs, groups, planes, distances):
    tokens, width = qkv_ref.shape[0] // 3, qkv_ref.shape[1]
    group_width = width // groups
    rows_dev = tokens // (groups * planes)
    to = lax.broadcasted_iota(jnp.int32, (tokens, tokens), 0)
    at = lax.broadcasted_iota(jnp.int32, (tokens, tokens), 1)
    j, t, row = to // (groups * rows_dev), (to // rows_dev) % groups, to % rows_dev
    for r, out_ref in zip(distances, out_refs):
        group = where_ref[0] ^ r
        lanes = pl.ds(pl.multiple_of(group * group_width, 128), group_width)
        place = row * (groups * planes) + (t ^ group) * planes + (j ^ where_ref[1])
        order = (at == place).astype(jnp.bfloat16)
        out_ref[: 2 * tokens] = qkv_ref[tokens:, lanes]
        mixed = jnp.dot(order, qkv_ref[:tokens, lanes], preferred_element_type=jnp.float32)
        out_ref[2 * tokens :] = mixed.astype(jnp.bfloat16)


def bundles(where, queries, keys, values, groups, planes, distances):
    tokens, width = queries.shape
    vmem = pl.BlockSpec(memory_space=pltpu.VMEM)
    result = jax.ShapeDtypeStruct((3 * tokens, width // groups), jnp.bfloat16)
    return pl.pallas_call(
        functools.partial(bundle_kernel, groups=groups, planes=planes, distances=distances),
        in_specs=[pl.BlockSpec(memory_space=pltpu.SMEM), vmem],
        out_specs=[vmem] * len(distances),
        out_shape=[result] * len(distances),
        compiler_params=pltpu.CompilerParams(vmem_limit_bytes=VMEM_LIMIT),
    )(where, jnp.concatenate([queries, keys, values], axis=0))


def after(value, *others):
    return lax.optimization_barrier((value,) + others)[0]


def attend_kernel(*refs, sources, planes, blocks, part, targets, rows_step):
    q_refs = refs[:sources]
    kv_refs = refs[sources : sources + len(blocks)]
    o_refs = refs[sources + len(blocks) :]
    tokens, width = q_refs[0].shape
    rows = tokens // sources
    rows_dev = rows // planes
    to = lax.broadcasted_iota(jnp.int32, (tokens, tokens), 0)
    at = lax.broadcasted_iota(jnp.int32, (tokens, tokens), 1)
    t, j, row = to // rows, (to // rows_dev) % planes, to % rows_dev
    place = ((j % 2) * (planes // 2) + j // 2) * rows + t * rows_dev + row
    order = (at == place).astype(jnp.bfloat16)
    asked = [
        jnp.dot(order, q[...], preferred_element_type=jnp.float32).astype(jnp.bfloat16) for q in q_refs
    ]
    works = [
        (h, range(first, min(first + rows_step, len(targets))))
        for h in range(width // HEAD_DIM)
        for first in range(0, len(targets), rows_step)
    ]

    def taken(ref, count, h, which):
        cut = ref[: count * 2 * part, h * HEAD_DIM : (h + 1) * HEAD_DIM]
        return cut.reshape(count, 2, part, HEAD_DIM)[:, which].reshape(count * part, HEAD_DIM)

    def scores_of(work):
        h, block = work
        lanes = slice(h * HEAD_DIM, (h + 1) * HEAD_DIM)
        query = jnp.concatenate(
            [q[targets[i] * rows : (targets[i] + 1) * rows, lanes] for i in block for q in asked], axis=0
        )
        return [
            lax.dot_general(
                query,
                taken(kv, count, h, 0),
                (((1,), (1,)), ((), ())),
                preferred_element_type=jnp.float32,
            )
            for kv, count in zip(kv_refs, blocks)
        ]

    def finish(work, scores):
        h, block = work
        peak = functools.reduce(jnp.maximum, [jnp.max(s, axis=1, keepdims=True) for s in scores])
        peak = peak * EXP2_SCALE
        summed = None
        for s, kv, count in zip(scores, kv_refs, blocks):
            weights = jnp.exp2(s * EXP2_SCALE - peak).astype(jnp.bfloat16)
            value = taken(kv, count, h, 1)
            value = jnp.concatenate([value, jnp.ones_like(value)], axis=1)
            product = jnp.dot(weights, value, preferred_element_type=jnp.float32)
            summed = product if summed is None else summed + product
        out = (summed[:, :HEAD_DIM] / summed[:, HEAD_DIM:]).astype(jnp.bfloat16)
        for n, i in enumerate(block):
            for r in range(sources):
                first = (n * sources + r) * rows
                o_refs[i][targets[i] ^ r, :, h * HEAD_DIM : (h + 1) * HEAD_DIM] = out[first : first + rows]

    scores = scores_of(works[0])
    for n, work in enumerate(works):
        following = scores_of(works[n + 1]) if n + 1 < len(works) else None
        finish(work, scores)
        scores = following


def attend(queries, keys_values, targets, planes):
    sources = len(queries)
    tokens, width = queries[0].shape
    rows = tokens // sources
    blocks = [kv.shape[0] // (2 * tokens) for kv in keys_values]
    key_count = sum(blocks) * tokens
    small = key_count <= 4096
    rows_step, step_width = (2, width) if small else (1, HEAD_DIM)
    score_bytes = rows_step * tokens * key_count * 4
    limit = 8 * key_count * step_width + 3 * score_bytes + 6 * 1024 * 1024
    return pl.pallas_call(
        functools.partial(
            attend_kernel,
            sources=sources,
            planes=planes,
            blocks=blocks,
            part=tokens,
            targets=targets,
            rows_step=rows_step,
        ),
        grid=(width // step_width,),
        in_specs=[pl.BlockSpec((tokens, step_width), lambda h: (0, h))] * sources
        + [pl.BlockSpec((kv.shape[0], step_width), lambda h: (0, h)) for kv in keys_values],
        out_specs=[pl.BlockSpec((sources, rows, step_width), lambda h: (0, 0, h))] * len(targets),
        out_shape=[jax.ShapeDtypeStruct((sources, rows, width), jnp.bfloat16)] * len(targets),
        compiler_params=pltpu.CompilerParams(vmem_limit_bytes=min(limit, 60 * 1024 * 1024)),
    )(*queries, *keys_values)


def projection_of(o_refs, w_refs, lined):
    tokens, width = lined.shape[0], o_refs[0].shape[2]
    for n, o_ref in enumerate(o_refs):
        lined[:, n * width : (n + 1) * width] = o_ref[...].reshape(tokens, width)
    weights = jnp.concatenate([w[...] for w in w_refs], axis=0)
    return jnp.dot(lined[...], weights, preferred_element_type=jnp.float32)


def projection_specs(attended, targets, tile):
    o_spec = pl.BlockSpec(attended[0].shape, lambda i, *_: (0, 0, 0))
    width = attended[0].shape[2]
    return [o_spec] * len(targets) + [
        pl.BlockSpec((width, tile), lambda i, where, t=t: (where[0] ^ t, i)) for t in targets
    ]


def project_kernel(where_ref, *refs, targets):
    count = len(targets)
    out_ref, lined = refs[2 * count :]
    out_ref[...] = projection_of(refs[:count], refs[count : 2 * count], lined)


def project(where, attended, targets, w_out, tile):
    sources, rows, width = attended[0].shape
    tokens = sources * rows
    features = w_out.shape[1]
    return pl.pallas_call(
        functools.partial(project_kernel, targets=targets),
        grid_spec=pltpu.PrefetchScalarGridSpec(
            num_scalar_prefetch=1,
            grid=(features // tile,),
            in_specs=projection_specs(attended, targets, tile),
            out_specs=pl.BlockSpec((None, tokens, tile), lambda i, *_: (i, 0, 0)),
            scratch_shapes=[pltpu.VMEM((tokens, len(targets) * width), jnp.bfloat16)],
        ),
        out_shape=jax.ShapeDtypeStruct((features // tile, tokens, tile), jnp.float32),
        compiler_params=pltpu.CompilerParams(vmem_limit_bytes=VMEM_LIMIT),
    )(where, *attended, *[w_out] * len(targets))


def final_kernel(where_ref, *refs, targets, planes, rows_dev):
    count = len(targets)
    partial_ref, scale_ref, shift_ref, w_final_ref, inner_ref, outer_ref, lined, projected = refs[2 * count :]
    step = pl.program_id(0)
    heads_at, plane_at = where_ref[0], where_ref[1]
    tokens = lined.shape[0]
    tile = partial_ref.shape[1]
    projected[step] = partial_ref[...] + projection_of(refs[:count], refs[count : 2 * count], lined)

    @pl.when(step == pl.num_programs(0) - 1)
    def _():
        steps = projected.shape[0]
        features = steps * tile
        total = projected[0]
        for i in range(1, steps):
            total = total + projected[i]
        mean = jnp.sum(total, axis=1, keepdims=True) * (1.0 / features)
        squares = None
        for i in range(steps):
            centered = projected[i] - mean
            squares = centered * centered if squares is None else squares + centered * centered
        variance = jnp.sum(squares, axis=1, keepdims=True) * (1.0 / features)
        inverse = lax.rsqrt(variance + 1e-06)
        patches = None
        for i in range(steps):
            lanes = slice(i * tile, (i + 1) * tile)
            normed = (projected[i] - mean) * inverse * (1.0 + scale_ref[:, lanes]) + shift_ref[:, lanes]
            part = lax.dot_general(
                normed.astype(jnp.bfloat16),
                w_final_ref[:, lanes],
                (((1,), (1,)), ((), ())),
                preferred_element_type=jnp.float32,
            )
            patches = part if patches is None else patches + part
        patches = patches.astype(jnp.bfloat16)
        channels = patches.shape[1]
        half = channels // 2
        source = lax.broadcasted_iota(jnp.int32, (channels, channels), 0)
        target = lax.broadcasted_iota(jnp.int32, (channels, channels), 1)
        q, p, c = target // half, (target // LATENT_CH) % 2, target % LATENT_CH
        lane_order = (source == 4 * c + 2 * p + q).astype(jnp.bfloat16)
        to = lax.broadcasted_iota(jnp.int32, (tokens, tokens), 0)
        at = lax.broadcasted_iota(jnp.int32, (tokens, tokens), 1)
        share = planes * rows_dev
        place = ((to // share) ^ heads_at) * share
        place = place + (((to % share) // rows_dev) ^ plane_at) * rows_dev + to % rows_dev
        row_order = (at == place).astype(jnp.bfloat16)
        cells = jnp.dot(patches, lane_order, preferred_element_type=jnp.float32)
        cells = jnp.dot(row_order, cells.astype(jnp.bfloat16), preferred_element_type=jnp.float32)
        first = plane_at % 2 == 0
        inner_ref[...] = jnp.where(first, cells[:, half:], cells[:, :half]).astype(jnp.bfloat16)
        outer_ref[...] = jnp.where(first, cells[:, :half], cells[:, half:]).astype(jnp.bfloat16)


def final_layer(where, attended, targets, partial, w_out, scale_mod, shift_mod, w_final, rows_dev, planes):
    sources, rows, width = attended[0].shape
    features = w_out.shape[1]
    steps, tokens, tile = partial.shape
    channels = w_final.shape[1]
    whole = lambda shape: pl.BlockSpec(shape, lambda i, *_: (0,) * len(shape))
    result = jax.ShapeDtypeStruct((tokens, channels // 2), jnp.bfloat16)
    return pl.pallas_call(
        functools.partial(final_kernel, targets=targets, planes=planes, rows_dev=rows_dev),
        grid_spec=pltpu.PrefetchScalarGridSpec(
            num_scalar_prefetch=1,
            grid=(steps,),
            in_specs=projection_specs(attended, targets, tile)
            + [
                pl.BlockSpec((None, tokens, tile), lambda i, *_: (i, 0, 0)),
                whole((1, features)),
                whole((1, features)),
                whole((channels, features)),
            ],
            out_specs=[whole((tokens, channels // 2))] * 2,
            scratch_shapes=[
                pltpu.VMEM((tokens, len(targets) * width), jnp.bfloat16),
                pltpu.VMEM((steps, tokens, tile), jnp.float32),
            ],
        ),
        out_shape=[result] * 2,
        compiler_params=pltpu.CompilerParams(vmem_limit_bytes=VMEM_LIMIT),
    )(where, *attended, *[w_out] * len(targets), partial, scale_mod[None], shift_mod[None], w_final.T)


def convolve_kernel(
    where_ref, inner_ref, outer_ref, inner_got_ref, outer_got_ref, w_ref, bias_ref, out_ref, latent
):
    frames, cols, _, ch = latent.shape
    rows = inner_ref.shape[0] // frames
    height = 2 * rows
    inner, outer, inner_got, outer_got = [
        ref[...].astype(jnp.float32) for ref in (inner_ref, outer_ref, inner_got_ref, outer_got_ref)
    ]
    first = where_ref[2] % 2 == 0
    even, odd = jnp.where(first, outer, inner), jnp.where(first, inner, outer)
    left = jnp.where(where_ref[2] == 0, even, jnp.where(first, outer_got, inner_got))
    right = jnp.where(where_ref[2] == where_ref[3] - 1, odd, jnp.where(first, inner_got, outer_got))
    for x, cells in enumerate((left, even, odd, right)):
        for f in range(frames):
            own = cells[f * rows : (f + 1) * rows]
            for p in range(2):
                latent[f, x, pl.ds(8 + p, rows, stride=2), :] = own[:, p * ch : (p + 1) * ch]
            latent[f, x, 7:8, :] = own[:1, :ch]
            latent[f, x, 8 + height : 9 + height, :] = own[rows - 1 :, ch:]
    depth = 9 * ch
    for x in range(cols - 2):
        stacked = []
        for f in range(frames):
            taps = [latent[f, x + b, 7 + e : 7 + e + height, :] for b in range(3) for e in range(3)]
            stacked.append(jnp.concatenate(taps, axis=1).astype(jnp.bfloat16))
        stacked = [stacked[0]] * 2 + stacked
        acc = None
        for a in range(3):
            flat = jnp.concatenate(stacked[a : a + frames], axis=0)
            part = jnp.dot(
                flat, w_ref[a * depth : (a + 1) * depth, :], preferred_element_type=jnp.float32
            )
            acc = part if acc is None else acc + part
        acc = (acc + bias_ref[...]).astype(jnp.bfloat16)
        out_ref[:, x] = acc.reshape(frames, height, acc.shape[1])


def convolve(where, inner, outer, inner_got, outer_got, conv_weight, conv_bias):
    rows = inner.shape[0] // FRAMES
    channels = conv_weight.shape[1]
    smem = pl.BlockSpec(memory_space=pltpu.SMEM)
    vmem = pl.BlockSpec(memory_space=pltpu.VMEM)
    return pl.pallas_call(
        convolve_kernel,
        in_specs=[smem] + [vmem] * 6,
        out_specs=vmem,
        out_shape=jax.ShapeDtypeStruct((FRAMES, 2, 2 * rows, channels), jnp.bfloat16),
        scratch_shapes=[pltpu.VMEM((FRAMES, 4, 2 * rows + 16, LATENT_CH), jnp.float32)],
        compiler_params=pltpu.CompilerParams(vmem_limit_bytes=VMEM_LIMIT),
    )(where, inner, outer, inner_got, outer_got, conv_weight, conv_bias[None])


def shards(queries, keys, values, w_out, shift_mod, scale_mod, w_final, conv_weight, conv_bias):
    groups = lax.axis_size("heads")
    planes = lax.axis_size("plane")
    heads_at = lax.axis_index("heads")
    plane_at = lax.axis_index("plane")
    devices = groups * planes
    tokens = queries.shape[0]
    rows_dev = tokens // devices
    where = jnp.stack(
        [heads_at, plane_at, heads_at * planes + plane_at, jnp.int32(devices)]
    ).astype(jnp.int32)

    made = bundles(where, queries, keys, values, groups, planes, range(groups))
    got = {r: swap(made[r], "heads", r) if r else made[r] for r in range(groups)}

    both_parts, share = 2 * tokens, tokens // planes
    held = {r: [got[r]] for r in range(groups)}
    for r in (0, 1, 2, 3):
        for d in range(2, planes, 2):
            asked = got[r][both_parts + d * share : both_parts + (d + 2) * share]
            held[r].append(swap(jnp.concatenate([got[r][:both_parts], asked], axis=0), "plane", d))

    keys_values, asked = [], {}
    for distances in ((0, 1), (2,), (3,)):
        passed = [h[:both_parts] for r in distances for h in held[r]]
        passed += [h[both_parts + share : both_parts + 2 * share] for r in distances for h in held[r]]
        mine = jnp.concatenate(passed, axis=0)
        other = swap(mine, "plane", 1)
        keys_values += [mine, other]
        half = planes // 2
        first = both_parts * half * len(distances)
        for n, r in enumerate(distances):
            start = first + n * half * share
            asked[r] = jnp.concatenate(
                [h[both_parts : both_parts + share] for h in held[r]]
                + [other[start : start + half * share]],
                axis=0,
            )
    asked = [asked[r] for r in range(groups)]

    near, far = (0, 3), (2, 1)
    results = {}
    for targets in ((3,), (2,), (1,), (0,)):
        for t, o in zip(targets, attend(asked, keys_values, targets, planes)):
            results[t] = o if t == 0 else swap(o, "heads", t)
    partial = project(where, [results[t] for t in near], near, w_out, 1024)
    sent = [results[t] for t in far]
    inner, outer = final_layer(
        where, sent, far, partial, w_out, scale_mod, shift_mod, w_final, rows_dev, planes
    )
    pairs = [(i, i + 1) for i in range(1, devices - 1, 2)]
    inner_got = swap(inner, "plane", 1)
    outer_got = lax.ppermute(outer, ("heads", "plane"), pairs + [(j, i) for i, j in pairs])
    return convolve(where, inner, outer, inner_got, outer_got, conv_weight, conv_bias)


def solution(mesh):
    groups, seq = mesh.devices.shape
    split = Mesh(
        mesh.devices.reshape(groups, HEAD_GROUPS, seq // HEAD_GROUPS), ("groups", "heads", "plane")
    )
    by_token = P(("groups", "heads", "plane"), None)
    placed = (by_token, by_token, by_token, P(), P("groups"), P("groups"), P(), P(), P())
    return jax.shard_map(
        shards,
        mesh=split,
        in_specs=placed,
        out_specs=P("groups", ("heads", "plane"), None, None),
        check_vma=False,
    )
```

```python
import functools
import math

import jax
import jax.numpy as jnp
from jax import lax
from jax.experimental import pallas as pl
from jax.experimental.pallas import tpu as pltpu
from jax.sharding import Mesh
from jax.sharding import PartitionSpec as P

HEAD_DIM = 128
HEAD_GROUPS = 4
LATENT_CH = 16
FRAMES = 4
VMEM_LIMIT = 16 * 1024 * 1024
EXP2_SCALE = math.log2(math.e) / math.sqrt(HEAD_DIM)


def swap(source, axis, distance):
    count = lax.axis_size(axis)
    return lax.ppermute(source, axis, [(i, i ^ distance) for i in range(count)])


def bundle_kernel(where_ref, qkv_ref, *out_refs, groups, planes, distances):
    tokens, width = qkv_ref.shape[0] // 3, qkv_ref.shape[1]
    group_width = width // groups
    rows_dev = tokens // (groups * planes)
    to = lax.broadcasted_iota(jnp.int32, (tokens, tokens), 0)
    at = lax.broadcasted_iota(jnp.int32, (tokens, tokens), 1)
    j, t, row = to // (groups * rows_dev), (to // rows_dev) % groups, to % rows_dev
    for r, out_ref in zip(distances, out_refs):
        group = where_ref[0] ^ r
        lanes = pl.ds(pl.multiple_of(group * group_width, 128), group_width)
        place = row * (groups * planes) + (t ^ group) * planes + (j ^ where_ref[1])
        order = (at == place).astype(jnp.bfloat16)
        out_ref[: 2 * tokens] = qkv_ref[tokens:, lanes]
        mixed = jnp.dot(order, qkv_ref[:tokens, lanes], preferred_element_type=jnp.float32)
        out_ref[2 * tokens :] = mixed.astype(jnp.bfloat16)


def bundles(where, queries, keys, values, groups, planes, distances):
    tokens, width = queries.shape
    vmem = pl.BlockSpec(memory_space=pltpu.VMEM)
    result = jax.ShapeDtypeStruct((3 * tokens, width // groups), jnp.bfloat16)
    return pl.pallas_call(
        functools.partial(bundle_kernel, groups=groups, planes=planes, distances=distances),
        in_specs=[pl.BlockSpec(memory_space=pltpu.SMEM), vmem],
        out_specs=[vmem] * len(distances),
        out_shape=[result] * len(distances),
        compiler_params=pltpu.CompilerParams(vmem_limit_bytes=VMEM_LIMIT),
    )(where, jnp.concatenate([queries, keys, values], axis=0))


def after(value, *others):
    return lax.optimization_barrier((value,) + others)[0]


def attend_kernel(*refs, sources, planes, blocks, part, targets, rows_step):
    q_refs = refs[:sources]
    kv_refs = refs[sources : sources + len(blocks)]
    o_refs = refs[sources + len(blocks) :]
    tokens, width = q_refs[0].shape
    rows = tokens // sources
    rows_dev = rows // planes
    to = lax.broadcasted_iota(jnp.int32, (tokens, tokens), 0)
    at = lax.broadcasted_iota(jnp.int32, (tokens, tokens), 1)
    t, j, row = to // rows, (to // rows_dev) % planes, to % rows_dev
    place = ((j % 2) * (planes // 2) + j // 2) * rows + t * rows_dev + row
    order = (at == place).astype(jnp.bfloat16)
    asked = [
        jnp.dot(order, q[...], preferred_element_type=jnp.float32).astype(jnp.bfloat16) for q in q_refs
    ]
    works = [
        (h, range(first, min(first + rows_step, len(targets))))
        for h in range(width // HEAD_DIM)
        for first in range(0, len(targets), rows_step)
    ]

    def taken(ref, count, h, which):
        cut = ref[: count * 2 * part, h * HEAD_DIM : (h + 1) * HEAD_DIM]
        return cut.reshape(count, 2, part, HEAD_DIM)[:, which].reshape(count * part, HEAD_DIM)

    def scores_of(work):
        h, block = work
        lanes = slice(h * HEAD_DIM, (h + 1) * HEAD_DIM)
        query = jnp.concatenate(
            [q[targets[i] * rows : (targets[i] + 1) * rows, lanes] for i in block for q in asked], axis=0
        )
        return [
            lax.dot_general(
                query,
                taken(kv, count, h, 0),
                (((1,), (1,)), ((), ())),
                preferred_element_type=jnp.float32,
            )
            for kv, count in zip(kv_refs, blocks)
        ]

    def finish(work, scores):
        h, block = work
        peak = functools.reduce(jnp.maximum, [jnp.max(s, axis=1, keepdims=True) for s in scores])
        peak = peak * EXP2_SCALE
        summed = None
        for s, kv, count in zip(scores, kv_refs, blocks):
            weights = jnp.exp2(s * EXP2_SCALE - peak).astype(jnp.bfloat16)
            value = taken(kv, count, h, 1)
            value = jnp.concatenate([value, jnp.ones_like(value)], axis=1)
            product = jnp.dot(weights, value, preferred_element_type=jnp.float32)
            summed = product if summed is None else summed + product
        out = (summed[:, :HEAD_DIM] / summed[:, HEAD_DIM:]).astype(jnp.bfloat16)
        for n, i in enumerate(block):
            for r in range(sources):
                first = (n * sources + r) * rows
                o_refs[i][targets[i] ^ r, :, h * HEAD_DIM : (h + 1) * HEAD_DIM] = out[first : first + rows]

    scores = scores_of(works[0])
    for n, work in enumerate(works):
        following = scores_of(works[n + 1]) if n + 1 < len(works) else None
        finish(work, scores)
        scores = following


def attend(queries, keys_values, targets, planes):
    sources = len(queries)
    tokens, width = queries[0].shape
    rows = tokens // sources
    blocks = [kv.shape[0] // (2 * tokens) for kv in keys_values]
    key_count = sum(blocks) * tokens
    small = key_count <= 4096
    rows_step, step_width = (2, width) if small else (1, HEAD_DIM)
    score_bytes = rows_step * tokens * key_count * 4
    limit = 8 * key_count * step_width + 3 * score_bytes + 6 * 1024 * 1024
    return pl.pallas_call(
        functools.partial(
            attend_kernel,
            sources=sources,
            planes=planes,
            blocks=blocks,
            part=tokens,
            targets=targets,
            rows_step=rows_step,
        ),
        grid=(width // step_width,),
        in_specs=[pl.BlockSpec((tokens, step_width), lambda h: (0, h))] * sources
        + [pl.BlockSpec((kv.shape[0], step_width), lambda h: (0, h)) for kv in keys_values],
        out_specs=[pl.BlockSpec((sources, rows, step_width), lambda h: (0, 0, h))] * len(targets),
        out_shape=[jax.ShapeDtypeStruct((sources, rows, width), jnp.bfloat16)] * len(targets),
        compiler_params=pltpu.CompilerParams(vmem_limit_bytes=min(limit, 60 * 1024 * 1024)),
    )(*queries, *keys_values)


def projection_of(o_refs, w_refs, lined):
    tokens, width = lined.shape[0], o_refs[0].shape[2]
    for n, o_ref in enumerate(o_refs):
        lined[:, n * width : (n + 1) * width] = o_ref[...].reshape(tokens, width)
    weights = jnp.concatenate([w[...] for w in w_refs], axis=0)
    return jnp.dot(lined[...], weights, preferred_element_type=jnp.float32)


def projection_specs(attended, targets, tile):
    o_spec = pl.BlockSpec(attended[0].shape, lambda i, *_: (0, 0, 0))
    width = attended[0].shape[2]
    return [o_spec] * len(targets) + [
        pl.BlockSpec((width, tile), lambda i, where, t=t: (where[0] ^ t, i)) for t in targets
    ]


def project_kernel(where_ref, *refs, targets):
    count = len(targets)
    out_ref, lined = refs[2 * count :]
    out_ref[...] = projection_of(refs[:count], refs[count : 2 * count], lined)


def project(where, attended, targets, w_out, tile):
    sources, rows, width = attended[0].shape
    tokens = sources * rows
    features = w_out.shape[1]
    return pl.pallas_call(
        functools.partial(project_kernel, targets=targets),
        grid_spec=pltpu.PrefetchScalarGridSpec(
            num_scalar_prefetch=1,
            grid=(features // tile,),
            in_specs=projection_specs(attended, targets, tile),
            out_specs=pl.BlockSpec((None, tokens, tile), lambda i, *_: (i, 0, 0)),
            scratch_shapes=[pltpu.VMEM((tokens, len(targets) * width), jnp.bfloat16)],
        ),
        out_shape=jax.ShapeDtypeStruct((features // tile, tokens, tile), jnp.float32),
        compiler_params=pltpu.CompilerParams(vmem_limit_bytes=VMEM_LIMIT),
    )(where, *attended, *[w_out] * len(targets))


def final_kernel(where_ref, *refs, targets, planes, rows_dev):
    count = len(targets)
    partial_ref, scale_ref, shift_ref, w_final_ref, inner_ref, outer_ref, lined, projected = refs[2 * count :]
    step = pl.program_id(0)
    heads_at, plane_at = where_ref[0], where_ref[1]
    tokens = lined.shape[0]
    tile = partial_ref.shape[1]
    projected[step] = partial_ref[...] + projection_of(refs[:count], refs[count : 2 * count], lined)

    @pl.when(step == pl.num_programs(0) - 1)
    def _():
        steps = projected.shape[0]
        features = steps * tile
        total = projected[0]
        for i in range(1, steps):
            total = total + projected[i]
        mean = jnp.sum(total, axis=1, keepdims=True) * (1.0 / features)
        squares = None
        for i in range(steps):
            centered = projected[i] - mean
            squares = centered * centered if squares is None else squares + centered * centered
        variance = jnp.sum(squares, axis=1, keepdims=True) * (1.0 / features)
        inverse = lax.rsqrt(variance + 1e-06)
        patches = None
        for i in range(steps):
            lanes = slice(i * tile, (i + 1) * tile)
            normed = (projected[i] - mean) * inverse * (1.0 + scale_ref[:, lanes]) + shift_ref[:, lanes]
            part = lax.dot_general(
                normed.astype(jnp.bfloat16),
                w_final_ref[:, lanes],
                (((1,), (1,)), ((), ())),
                preferred_element_type=jnp.float32,
            )
            patches = part if patches is None else patches + part
        patches = patches.astype(jnp.bfloat16)
        channels = patches.shape[1]
        half = channels // 2
        source = lax.broadcasted_iota(jnp.int32, (channels, channels), 0)
        target = lax.broadcasted_iota(jnp.int32, (channels, channels), 1)
        q, p, c = target // half, (target // LATENT_CH) % 2, target % LATENT_CH
        lane_order = (source == 4 * c + 2 * p + q).astype(jnp.bfloat16)
        to = lax.broadcasted_iota(jnp.int32, (tokens, tokens), 0)
        at = lax.broadcasted_iota(jnp.int32, (tokens, tokens), 1)
        share = planes * rows_dev
        place = ((to // share) ^ heads_at) * share
        place = place + (((to % share) // rows_dev) ^ plane_at) * rows_dev + to % rows_dev
        row_order = (at == place).astype(jnp.bfloat16)
        cells = jnp.dot(patches, lane_order, preferred_element_type=jnp.float32)
        cells = jnp.dot(row_order, cells.astype(jnp.bfloat16), preferred_element_type=jnp.float32)
        first = plane_at % 2 == 0
        inner_ref[...] = jnp.where(first, cells[:, half:], cells[:, :half]).astype(jnp.bfloat16)
        outer_ref[...] = jnp.where(first, cells[:, :half], cells[:, half:]).astype(jnp.bfloat16)


def final_layer(where, attended, targets, partial, w_out, scale_mod, shift_mod, w_final, rows_dev, planes):
    sources, rows, width = attended[0].shape
    features = w_out.shape[1]
    steps, tokens, tile = partial.shape
    channels = w_final.shape[1]
    whole = lambda shape: pl.BlockSpec(shape, lambda i, *_: (0,) * len(shape))
    result = jax.ShapeDtypeStruct((tokens, channels // 2), jnp.bfloat16)
    return pl.pallas_call(
        functools.partial(final_kernel, targets=targets, planes=planes, rows_dev=rows_dev),
        grid_spec=pltpu.PrefetchScalarGridSpec(
            num_scalar_prefetch=1,
            grid=(steps,),
            in_specs=projection_specs(attended, targets, tile)
            + [
                pl.BlockSpec((None, tokens, tile), lambda i, *_: (i, 0, 0)),
                whole((1, features)),
                whole((1, features)),
                whole((channels, features)),
            ],
            out_specs=[whole((tokens, channels // 2))] * 2,
            scratch_shapes=[
                pltpu.VMEM((tokens, len(targets) * width), jnp.bfloat16),
                pltpu.VMEM((steps, tokens, tile), jnp.float32),
            ],
        ),
        out_shape=[result] * 2,
        compiler_params=pltpu.CompilerParams(vmem_limit_bytes=VMEM_LIMIT),
    )(where, *attended, *[w_out] * len(targets), partial, scale_mod[None], shift_mod[None], w_final.T)


def lay_out(latent, columns):
    frames, _, extent, ch = latent.shape
    height = extent - 16
    rows = height // 2
    for x, cells in enumerate(columns):
        for f in range(frames):
            own = cells[f * rows : (f + 1) * rows]
            for p in range(2):
                latent[f, x, pl.ds(8 + p, rows, stride=2), :] = own[:, p * ch : (p + 1) * ch]
            latent[f, x, 7:8, :] = own[:1, :ch]
            latent[f, x, 8 + height : 9 + height, :] = own[rows - 1 :, ch:]


def tap_sum(latent, w_ref, columns, shift):
    frames, _, extent, ch = latent.shape
    height = extent - 16
    stacked = []
    for f in range(frames):
        taps = [latent[f, x, 7 + e : 7 + e + height, :] for x in columns for e in range(3)]
        stacked.append(jnp.concatenate(taps, axis=1).astype(jnp.bfloat16))
    stacked = [stacked[0]] * 2 + stacked
    depth = 3 * len(columns) * ch
    total = None
    for a in range(3):
        flat = jnp.concatenate(stacked[a : a + frames], axis=0)
        first = (9 * a + 3 * shift) * ch
        part = jnp.dot(flat, w_ref[first : first + depth, :], preferred_element_type=jnp.float32)
        total = part if total is None else total + part
    return total


def own_columns(where_ref, inner_ref, outer_ref):
    inner, outer = inner_ref[...].astype(jnp.float32), outer_ref[...].astype(jnp.float32)
    first = where_ref[2] % 2 == 0
    return jnp.where(first, outer, inner), jnp.where(first, inner, outer)


def own_taps_kernel(where_ref, inner_ref, outer_ref, w_ref, out_ref, latent):
    lay_out(latent, own_columns(where_ref, inner_ref, outer_ref))
    out_ref[0] = tap_sum(latent, w_ref, (0, 1), 1)
    out_ref[1] = tap_sum(latent, w_ref, (0, 1), 0)


def halo_taps_kernel(
    where_ref, inner_ref, outer_ref, inner_got_ref, outer_got_ref, own_ref, w_ref, bias_ref, out_ref, latent
):
    even, odd = own_columns(where_ref, inner_ref, outer_ref)
    right, left = own_columns(where_ref, outer_got_ref, inner_got_ref)
    left = jnp.where(where_ref[2] == 0, even, left)
    right = jnp.where(where_ref[2] == where_ref[3] - 1, odd, right)
    lay_out(latent, (left, right))
    frames, _, height, channels = out_ref.shape
    for x in range(2):
        total = own_ref[x] + tap_sum(latent, w_ref, (x,), 2 * x) + bias_ref[...]
        out_ref[:, x] = total.astype(jnp.bfloat16).reshape(frames, height, channels)


def latent_scratch(rows):
    return [pltpu.VMEM((FRAMES, 2, 2 * rows + 16, LATENT_CH), jnp.float32)]


def convolve_own(where, inner, outer, conv_weight):
    rows = inner.shape[0] // FRAMES
    channels = conv_weight.shape[1]
    smem = pl.BlockSpec(memory_space=pltpu.SMEM)
    vmem = pl.BlockSpec(memory_space=pltpu.VMEM)
    return pl.pallas_call(
        own_taps_kernel,
        in_specs=[smem] + [vmem] * 3,
        out_specs=vmem,
        out_shape=jax.ShapeDtypeStruct((2, FRAMES * 2 * rows, channels), jnp.float32),
        scratch_shapes=latent_scratch(rows),
        compiler_params=pltpu.CompilerParams(vmem_limit_bytes=VMEM_LIMIT),
    )(where, inner, outer, conv_weight)


def convolve_halo(where, inner, outer, inner_got, outer_got, own, conv_weight, conv_bias):
    rows = inner.shape[0] // FRAMES
    channels = conv_weight.shape[1]
    smem = pl.BlockSpec(memory_space=pltpu.SMEM)
    vmem = pl.BlockSpec(memory_space=pltpu.VMEM)
    return pl.pallas_call(
        halo_taps_kernel,
        in_specs=[smem] + [vmem] * 7,
        out_specs=vmem,
        out_shape=jax.ShapeDtypeStruct((FRAMES, 2, 2 * rows, channels), jnp.bfloat16),
        scratch_shapes=latent_scratch(rows),
        compiler_params=pltpu.CompilerParams(vmem_limit_bytes=VMEM_LIMIT),
    )(where, inner, outer, inner_got, outer_got, own, conv_weight, conv_bias[None])


def shards(queries, keys, values, w_out, shift_mod, scale_mod, w_final, conv_weight, conv_bias):
    groups = lax.axis_size("heads")
    planes = lax.axis_size("plane")
    heads_at = lax.axis_index("heads")
    plane_at = lax.axis_index("plane")
    devices = groups * planes
    tokens = queries.shape[0]
    rows_dev = tokens // devices
    where = jnp.stack(
        [heads_at, plane_at, heads_at * planes + plane_at, jnp.int32(devices)]
    ).astype(jnp.int32)

    made = bundles(where, queries, keys, values, groups, planes, range(groups))
    got = {r: swap(made[r], "heads", r) if r else made[r] for r in range(groups)}

    both_parts, share = 2 * tokens, tokens // planes
    held = {r: [got[r]] for r in range(groups)}
    for r in (0, 1, 2, 3):
        for d in range(2, planes, 2):
            asked = got[r][both_parts + d * share : both_parts + (d + 2) * share]
            held[r].append(swap(jnp.concatenate([got[r][:both_parts], asked], axis=0), "plane", d))

    keys_values, asked = [], {}
    for distances in ((0, 1), (2,), (3,)):
        passed = [h[:both_parts] for r in distances for h in held[r]]
        passed += [h[both_parts + share : both_parts + 2 * share] for r in distances for h in held[r]]
        mine = jnp.concatenate(passed, axis=0)
        other = swap(mine, "plane", 1)
        keys_values += [mine, other]
        half = planes // 2
        first = both_parts * half * len(distances)
        for n, r in enumerate(distances):
            start = first + n * half * share
            asked[r] = jnp.concatenate(
                [h[both_parts : both_parts + share] for h in held[r]]
                + [other[start : start + half * share]],
                axis=0,
            )
    asked = [asked[r] for r in range(groups)]

    near, far = (0, 3), (2, 1)
    results = {}
    for targets in ((3,), (2,), (1,), (0,)):
        for t, o in zip(targets, attend(asked, keys_values, targets, planes)):
            results[t] = o if t == 0 else swap(o, "heads", t)
    partial = project(where, [results[t] for t in near], near, w_out, 1536)
    sent = [results[t] for t in far]
    inner, outer = final_layer(
        where, sent, far, partial, w_out, scale_mod, shift_mod, w_final, rows_dev, planes
    )
    pairs = [(i, i + 1) for i in range(1, devices - 1, 2)]
    inner_got = swap(inner, "plane", 1)
    outer_got = lax.ppermute(outer, ("heads", "plane"), pairs + [(j, i) for i, j in pairs])
    own = convolve_own(where, inner, outer, conv_weight)
    return convolve_halo(where, inner, outer, inner_got, outer_got, own, conv_weight, conv_bias)


def solution(mesh):
    groups, seq = mesh.devices.shape
    split = Mesh(
        mesh.devices.reshape(groups, HEAD_GROUPS, seq // HEAD_GROUPS), ("groups", "heads", "plane")
    )
    by_token = P(("groups", "heads", "plane"), None)
    placed = (by_token, by_token, by_token, P(), P("groups"), P("groups"), P(), P(), P())
    return jax.shard_map(
        shards,
        mesh=split,
        in_specs=placed,
        out_specs=P("groups", ("heads", "plane"), None, None),
        check_vma=False,
    )
```

```python
import functools
import math

import jax
import jax.numpy as jnp
from jax import lax
from jax.experimental import pallas as pl
from jax.experimental.pallas import tpu as pltpu
from jax.sharding import Mesh
from jax.sharding import PartitionSpec as P

HEAD_DIM = 128
HEAD_GROUPS = 4
LATENT_CH = 16
FRAMES = 4
VMEM_LIMIT = 16 * 1024 * 1024
EXP2_SCALE = math.log2(math.e) / math.sqrt(HEAD_DIM)


def swap(source, axis, distance):
    count = lax.axis_size(axis)
    return lax.ppermute(source, axis, [(i, i ^ distance) for i in range(count)])


def bundle_kernel(where_ref, qkv_ref, *out_refs, groups, planes, distances):
    tokens, width = qkv_ref.shape[0] // 3, qkv_ref.shape[1]
    group_width = width // groups
    rows_dev = tokens // (groups * planes)
    to = lax.broadcasted_iota(jnp.int32, (tokens, tokens), 0)
    at = lax.broadcasted_iota(jnp.int32, (tokens, tokens), 1)
    j, t, row = to // (groups * rows_dev), (to // rows_dev) % groups, to % rows_dev
    for r, out_ref in zip(distances, out_refs):
        group = where_ref[0] ^ r
        lanes = pl.ds(pl.multiple_of(group * group_width, 128), group_width)
        place = row * (groups * planes) + (t ^ group) * planes + (j ^ where_ref[1])
        order = (at == place).astype(jnp.bfloat16)
        out_ref[: 2 * tokens] = qkv_ref[tokens:, lanes]
        mixed = jnp.dot(order, qkv_ref[:tokens, lanes], preferred_element_type=jnp.float32)
        out_ref[2 * tokens :] = mixed.astype(jnp.bfloat16)


def bundles(where, queries, keys, values, groups, planes, distances):
    tokens, width = queries.shape
    vmem = pl.BlockSpec(memory_space=pltpu.VMEM)
    result = jax.ShapeDtypeStruct((3 * tokens, width // groups), jnp.bfloat16)
    return pl.pallas_call(
        functools.partial(bundle_kernel, groups=groups, planes=planes, distances=distances),
        in_specs=[pl.BlockSpec(memory_space=pltpu.SMEM), vmem],
        out_specs=[vmem] * len(distances),
        out_shape=[result] * len(distances),
        compiler_params=pltpu.CompilerParams(vmem_limit_bytes=VMEM_LIMIT),
    )(where, jnp.concatenate([queries, keys, values], axis=0))


def after(value, *others):
    return lax.optimization_barrier((value,) + others)[0]


def attend_kernel(*refs, sources, planes, blocks, part, targets, rows_step):
    q_refs = refs[:sources]
    kv_refs = refs[sources : sources + len(blocks)]
    o_refs = refs[sources + len(blocks) :]
    tokens, width = q_refs[0].shape
    rows = tokens // sources
    rows_dev = rows // planes
    to = lax.broadcasted_iota(jnp.int32, (tokens, tokens), 0)
    at = lax.broadcasted_iota(jnp.int32, (tokens, tokens), 1)
    t, j, row = to // rows, (to // rows_dev) % planes, to % rows_dev
    place = ((j % 2) * (planes // 2) + j // 2) * rows + t * rows_dev + row
    order = (at == place).astype(jnp.bfloat16)
    asked = [
        jnp.dot(order, q[...], preferred_element_type=jnp.float32).astype(jnp.bfloat16) for q in q_refs
    ]
    works = [
        (h, range(first, min(first + rows_step, len(targets))))
        for h in range(width // HEAD_DIM)
        for first in range(0, len(targets), rows_step)
    ]

    def taken(ref, count, h, which):
        cut = ref[: count * 2 * part, h * HEAD_DIM : (h + 1) * HEAD_DIM]
        return cut.reshape(count, 2, part, HEAD_DIM)[:, which].reshape(count * part, HEAD_DIM)

    def scores_of(work):
        h, block = work
        lanes = slice(h * HEAD_DIM, (h + 1) * HEAD_DIM)
        query = jnp.concatenate(
            [q[targets[i] * rows : (targets[i] + 1) * rows, lanes] for i in block for q in asked], axis=0
        )
        return [
            lax.dot_general(
                query,
                taken(kv, count, h, 0),
                (((1,), (1,)), ((), ())),
                preferred_element_type=jnp.float32,
            )
            for kv, count in zip(kv_refs, blocks)
        ]

    def finish(work, scores):
        h, block = work
        peak = functools.reduce(jnp.maximum, [jnp.max(s, axis=1, keepdims=True) for s in scores])
        peak = peak * EXP2_SCALE
        summed = None
        for s, kv, count in zip(scores, kv_refs, blocks):
            weights = jnp.exp2(s * EXP2_SCALE - peak).astype(jnp.bfloat16)
            value = taken(kv, count, h, 1)
            value = jnp.concatenate([value, jnp.ones_like(value)], axis=1)
            product = jnp.dot(weights, value, preferred_element_type=jnp.float32)
            summed = product if summed is None else summed + product
        out = (summed[:, :HEAD_DIM] / summed[:, HEAD_DIM:]).astype(jnp.bfloat16)
        for n, i in enumerate(block):
            for r in range(sources):
                first = (n * sources + r) * rows
                o_refs[i][targets[i] ^ r, :, h * HEAD_DIM : (h + 1) * HEAD_DIM] = out[first : first + rows]

    scores = scores_of(works[0])
    for n, work in enumerate(works):
        following = scores_of(works[n + 1]) if n + 1 < len(works) else None
        finish(work, scores)
        scores = following


def attend(queries, keys_values, targets, planes):
    sources = len(queries)
    tokens, width = queries[0].shape
    rows = tokens // sources
    blocks = [kv.shape[0] // (2 * tokens) for kv in keys_values]
    key_count = sum(blocks) * tokens
    small = key_count <= 4096
    rows_step, step_width = (2, width) if small else (1, HEAD_DIM)
    score_bytes = rows_step * tokens * key_count * 4
    limit = 8 * key_count * step_width + 3 * score_bytes + 6 * 1024 * 1024
    return pl.pallas_call(
        functools.partial(
            attend_kernel,
            sources=sources,
            planes=planes,
            blocks=blocks,
            part=tokens,
            targets=targets,
            rows_step=rows_step,
        ),
        grid=(width // step_width,),
        in_specs=[pl.BlockSpec((tokens, step_width), lambda h: (0, h))] * sources
        + [pl.BlockSpec((kv.shape[0], step_width), lambda h: (0, h)) for kv in keys_values],
        out_specs=[pl.BlockSpec((sources, rows, step_width), lambda h: (0, 0, h))] * len(targets),
        out_shape=[jax.ShapeDtypeStruct((sources, rows, width), jnp.bfloat16)] * len(targets),
        compiler_params=pltpu.CompilerParams(vmem_limit_bytes=min(limit, 60 * 1024 * 1024)),
    )(*queries, *keys_values)


def projection_of(o_refs, w_refs, lined):
    tokens, width = lined.shape[0], o_refs[0].shape[2]
    for n, o_ref in enumerate(o_refs):
        lined[:, n * width : (n + 1) * width] = o_ref[...].reshape(tokens, width)
    weights = jnp.concatenate([w[...] for w in w_refs], axis=0)
    return jnp.dot(lined[...], weights, preferred_element_type=jnp.float32)


def projection_specs(attended, targets, tile):
    o_spec = pl.BlockSpec(attended[0].shape, lambda i, *_: (0, 0, 0))
    width = attended[0].shape[2]
    return [o_spec] * len(targets) + [
        pl.BlockSpec((width, tile), lambda i, where, t=t: (where[0] ^ t, i)) for t in targets
    ]


def project_kernel(where_ref, *refs, targets):
    count = len(targets)
    out_ref, lined = refs[2 * count :]
    out_ref[...] = projection_of(refs[:count], refs[count : 2 * count], lined)


def project(where, attended, targets, w_out, tile):
    sources, rows, width = attended[0].shape
    tokens = sources * rows
    features = w_out.shape[1]
    return pl.pallas_call(
        functools.partial(project_kernel, targets=targets),
        grid_spec=pltpu.PrefetchScalarGridSpec(
            num_scalar_prefetch=1,
            grid=(features // tile,),
            in_specs=projection_specs(attended, targets, tile),
            out_specs=pl.BlockSpec((None, tokens, tile), lambda i, *_: (i, 0, 0)),
            scratch_shapes=[pltpu.VMEM((tokens, len(targets) * width), jnp.bfloat16)],
        ),
        out_shape=jax.ShapeDtypeStruct((features // tile, tokens, tile), jnp.float32),
        compiler_params=pltpu.CompilerParams(vmem_limit_bytes=VMEM_LIMIT),
    )(where, *attended, *[w_out] * len(targets))


def final_kernel(where_ref, *refs, targets, planes, rows_dev):
    count = len(targets)
    partial_ref, scale_ref, shift_ref, w_final_ref, inner_ref, outer_ref, lined, projected = refs[2 * count :]
    step = pl.program_id(0)
    heads_at, plane_at = where_ref[0], where_ref[1]
    tokens = lined.shape[0]
    tile = partial_ref.shape[1]
    projected[step] = partial_ref[...] + projection_of(refs[:count], refs[count : 2 * count], lined)

    @pl.when(step == pl.num_programs(0) - 1)
    def _():
        steps = projected.shape[0]
        features = steps * tile
        total = projected[0]
        for i in range(1, steps):
            total = total + projected[i]
        mean = jnp.sum(total, axis=1, keepdims=True) * (1.0 / features)
        squares = None
        for i in range(steps):
            centered = projected[i] - mean
            squares = centered * centered if squares is None else squares + centered * centered
        variance = jnp.sum(squares, axis=1, keepdims=True) * (1.0 / features)
        inverse = lax.rsqrt(variance + 1e-06)
        patches = None
        for i in range(steps):
            lanes = slice(i * tile, (i + 1) * tile)
            normed = (projected[i] - mean) * inverse * (1.0 + scale_ref[:, lanes]) + shift_ref[:, lanes]
            part = lax.dot_general(
                normed.astype(jnp.bfloat16),
                w_final_ref[:, lanes],
                (((1,), (1,)), ((), ())),
                preferred_element_type=jnp.float32,
            )
            patches = part if patches is None else patches + part
        patches = patches.astype(jnp.bfloat16)
        channels = patches.shape[1]
        half = channels // 2
        source = lax.broadcasted_iota(jnp.int32, (channels, channels), 0)
        target = lax.broadcasted_iota(jnp.int32, (channels, channels), 1)
        q, p, c = target // half, (target // LATENT_CH) % 2, target % LATENT_CH
        lane_order = (source == 4 * c + 2 * p + q).astype(jnp.bfloat16)
        to = lax.broadcasted_iota(jnp.int32, (tokens, tokens), 0)
        at = lax.broadcasted_iota(jnp.int32, (tokens, tokens), 1)
        share = planes * rows_dev
        place = ((to // share) ^ heads_at) * share
        place = place + (((to % share) // rows_dev) ^ plane_at) * rows_dev + to % rows_dev
        row_order = (at == place).astype(jnp.bfloat16)
        cells = jnp.dot(patches, lane_order, preferred_element_type=jnp.float32)
        cells = jnp.dot(row_order, cells.astype(jnp.bfloat16), preferred_element_type=jnp.float32)
        first = plane_at % 2 == 0
        inner_ref[...] = jnp.where(first, cells[:, half:], cells[:, :half]).astype(jnp.bfloat16)
        outer_ref[...] = jnp.where(first, cells[:, :half], cells[:, half:]).astype(jnp.bfloat16)


def final_layer(where, attended, targets, partial, w_out, scale_mod, shift_mod, w_final, rows_dev, planes):
    sources, rows, width = attended[0].shape
    features = w_out.shape[1]
    steps, tokens, tile = partial.shape
    channels = w_final.shape[1]
    whole = lambda shape: pl.BlockSpec(shape, lambda i, *_: (0,) * len(shape))
    result = jax.ShapeDtypeStruct((tokens, channels // 2), jnp.bfloat16)
    return pl.pallas_call(
        functools.partial(final_kernel, targets=targets, planes=planes, rows_dev=rows_dev),
        grid_spec=pltpu.PrefetchScalarGridSpec(
            num_scalar_prefetch=1,
            grid=(steps,),
            in_specs=projection_specs(attended, targets, tile)
            + [
                pl.BlockSpec((None, tokens, tile), lambda i, *_: (i, 0, 0)),
                whole((1, features)),
                whole((1, features)),
                whole((channels, features)),
            ],
            out_specs=[whole((tokens, channels // 2))] * 2,
            scratch_shapes=[
                pltpu.VMEM((tokens, len(targets) * width), jnp.bfloat16),
                pltpu.VMEM((steps, tokens, tile), jnp.float32),
            ],
        ),
        out_shape=[result] * 2,
        compiler_params=pltpu.CompilerParams(vmem_limit_bytes=VMEM_LIMIT),
    )(where, *attended, *[w_out] * len(targets), partial, scale_mod[None], shift_mod[None], w_final.T)


def convolve_kernel(
    where_ref, inner_ref, outer_ref, inner_got_ref, outer_got_ref, w_ref, bias_ref, out_ref, latent
):
    frames, cols, _, ch = latent.shape
    rows = inner_ref.shape[0] // frames
    height = 2 * rows
    inner, outer, inner_got, outer_got = [
        ref[...].astype(jnp.float32) for ref in (inner_ref, outer_ref, inner_got_ref, outer_got_ref)
    ]
    first = where_ref[2] % 2 == 0
    even, odd = jnp.where(first, outer, inner), jnp.where(first, inner, outer)
    left = jnp.where(where_ref[2] == 0, even, jnp.where(first, outer_got, inner_got))
    right = jnp.where(where_ref[2] == where_ref[3] - 1, odd, jnp.where(first, inner_got, outer_got))
    for x, cells in enumerate((left, even, odd, right)):
        for f in range(frames):
            own = cells[f * rows : (f + 1) * rows]
            for p in range(2):
                latent[f, x, pl.ds(8 + p, rows, stride=2), :] = own[:, p * ch : (p + 1) * ch]
            latent[f, x, 7:8, :] = own[:1, :ch]
            latent[f, x, 8 + height : 9 + height, :] = own[rows - 1 :, ch:]
    depth = 9 * ch
    for x in range(cols - 2):
        stacked = []
        for f in range(frames):
            taps = [latent[f, x + b, 7 + e : 7 + e + height, :] for b in range(3) for e in range(3)]
            stacked.append(jnp.concatenate(taps, axis=1).astype(jnp.bfloat16))
        stacked = [stacked[0]] * 2 + stacked
        acc = None
        for a in range(3):
            flat = jnp.concatenate(stacked[a : a + frames], axis=0)
            part = jnp.dot(
                flat, w_ref[a * depth : (a + 1) * depth, :], preferred_element_type=jnp.float32
            )
            acc = part if acc is None else acc + part
        acc = (acc + bias_ref[...]).astype(jnp.bfloat16)
        out_ref[:, x] = acc.reshape(frames, height, acc.shape[1])


def convolve(where, inner, outer, inner_got, outer_got, conv_weight, conv_bias):
    rows = inner.shape[0] // FRAMES
    channels = conv_weight.shape[1]
    smem = pl.BlockSpec(memory_space=pltpu.SMEM)
    vmem = pl.BlockSpec(memory_space=pltpu.VMEM)
    return pl.pallas_call(
        convolve_kernel,
        in_specs=[smem] + [vmem] * 6,
        out_specs=vmem,
        out_shape=jax.ShapeDtypeStruct((FRAMES, 2, 2 * rows, channels), jnp.bfloat16),
        scratch_shapes=[pltpu.VMEM((FRAMES, 4, 2 * rows + 16, LATENT_CH), jnp.float32)],
        compiler_params=pltpu.CompilerParams(vmem_limit_bytes=VMEM_LIMIT),
    )(where, inner, outer, inner_got, outer_got, conv_weight, conv_bias[None])


def shards(queries, keys, values, w_out, shift_mod, scale_mod, w_final, conv_weight, conv_bias):
    groups = lax.axis_size("heads")
    planes = lax.axis_size("plane")
    heads_at = lax.axis_index("heads")
    plane_at = lax.axis_index("plane")
    devices = groups * planes
    tokens = queries.shape[0]
    rows_dev = tokens // devices
    where = jnp.stack(
        [heads_at, plane_at, heads_at * planes + plane_at, jnp.int32(devices)]
    ).astype(jnp.int32)

    made = bundles(where, queries, keys, values, groups, planes, range(groups))
    got = {r: swap(made[r], "heads", r) if r else made[r] for r in range(groups)}

    both_parts, share = 2 * tokens, tokens // planes
    held = {r: [got[r]] for r in range(groups)}
    for batch in ((0, 1), (2,), (3,)):
        for d in range(2, planes, 2):
            sent = []
            for r in batch:
                sent += [got[r][:both_parts], got[r][both_parts + d * share : both_parts + (d + 2) * share]]
            crossed = swap(jnp.concatenate(sent, axis=0), "plane", d)
            extent = both_parts + 2 * share
            for n, r in enumerate(batch):
                held[r].append(crossed[n * extent : (n + 1) * extent])

    keys_values, asked = [], {}
    for distances in ((0, 1), (2,), (3,)):
        passed = [h[:both_parts] for r in distances for h in held[r]]
        passed += [h[both_parts + share : both_parts + 2 * share] for r in distances for h in held[r]]
        mine = jnp.concatenate(passed, axis=0)
        other = swap(mine, "plane", 1)
        keys_values += [mine, other]
        half = planes // 2
        first = both_parts * half * len(distances)
        for n, r in enumerate(distances):
            start = first + n * half * share
            asked[r] = jnp.concatenate(
                [h[both_parts : both_parts + share] for h in held[r]]
                + [other[start : start + half * share]],
                axis=0,
            )
    asked = [asked[r] for r in range(groups)]

    near, far = (0, 3), (2, 1)
    results = {}
    for targets in ((3,), (2,), (1,), (0,)):
        for t, o in zip(targets, attend(asked, keys_values, targets, planes)):
            results[t] = o if t == 0 else swap(o, "heads", t)
    partial = project(where, [results[t] for t in near], near, w_out, 1536)
    sent = [results[t] for t in far]
    inner, outer = final_layer(
        where, sent, far, partial, w_out, scale_mod, shift_mod, w_final, rows_dev, planes
    )
    pairs = [(i, i + 1) for i in range(1, devices - 1, 2)]
    inner_got = swap(inner, "plane", 1)
    outer_got = lax.ppermute(outer, ("heads", "plane"), pairs + [(j, i) for i, j in pairs])
    return convolve(where, inner, outer, inner_got, outer_got, conv_weight, conv_bias)


def solution(mesh):
    groups, seq = mesh.devices.shape
    split = Mesh(
        mesh.devices.reshape(groups, HEAD_GROUPS, seq // HEAD_GROUPS), ("groups", "heads", "plane")
    )
    by_token = P(("groups", "heads", "plane"), None)
    placed = (by_token, by_token, by_token, P(), P("groups"), P("groups"), P(), P(), P())
    return jax.shard_map(
        shards,
        mesh=split,
        in_specs=placed,
        out_specs=P("groups", ("heads", "plane"), None, None),
        check_vma=False,
    )
```

```python
import functools
import math

import jax
import jax.numpy as jnp
from jax import lax
from jax.experimental import pallas as pl
from jax.experimental.pallas import tpu as pltpu
from jax.sharding import Mesh
from jax.sharding import PartitionSpec as P

HEAD_DIM = 128
HEAD_GROUPS = 4
LATENT_CH = 16
FRAMES = 4
VMEM_LIMIT = 16 * 1024 * 1024
EXP2_SCALE = math.log2(math.e) / math.sqrt(HEAD_DIM)


def swap(source, axis, distance):
    count = lax.axis_size(axis)
    return lax.ppermute(source, axis, [(i, i ^ distance) for i in range(count)])


def bundle_kernel(where_ref, qkv_ref, *out_refs, groups, planes, distances):
    tokens, width = qkv_ref.shape[0] // 3, qkv_ref.shape[1]
    group_width = width // groups
    rows_dev = tokens // (groups * planes)
    to = lax.broadcasted_iota(jnp.int32, (tokens, tokens), 0)
    at = lax.broadcasted_iota(jnp.int32, (tokens, tokens), 1)
    j, t, row = to // (groups * rows_dev), (to // rows_dev) % groups, to % rows_dev
    for r, out_ref in zip(distances, out_refs):
        group = where_ref[0] ^ r
        lanes = pl.ds(pl.multiple_of(group * group_width, 128), group_width)
        place = row * (groups * planes) + (t ^ group) * planes + (j ^ where_ref[1])
        order = (at == place).astype(jnp.bfloat16)
        out_ref[: 2 * tokens] = qkv_ref[tokens:, lanes]
        mixed = jnp.dot(order, qkv_ref[:tokens, lanes], preferred_element_type=jnp.float32)
        out_ref[2 * tokens :] = mixed.astype(jnp.bfloat16)


def bundles(where, queries, keys, values, groups, planes, distances):
    tokens, width = queries.shape
    vmem = pl.BlockSpec(memory_space=pltpu.VMEM)
    result = jax.ShapeDtypeStruct((3 * tokens, width // groups), jnp.bfloat16)
    return pl.pallas_call(
        functools.partial(bundle_kernel, groups=groups, planes=planes, distances=distances),
        in_specs=[pl.BlockSpec(memory_space=pltpu.SMEM), vmem],
        out_specs=[vmem] * len(distances),
        out_shape=[result] * len(distances),
        compiler_params=pltpu.CompilerParams(vmem_limit_bytes=VMEM_LIMIT),
    )(where, jnp.concatenate([queries, keys, values], axis=0))


def after(value, *others):
    return lax.optimization_barrier((value,) + others)[0]


def attend_kernel(*refs, sources, planes, blocks, part, targets, rows_step):
    q_refs = refs[:sources]
    kv_refs = refs[sources : sources + len(blocks)]
    o_refs = refs[sources + len(blocks) :]
    tokens, width = q_refs[0].shape
    rows = tokens // sources
    rows_dev = rows // planes
    to = lax.broadcasted_iota(jnp.int32, (tokens, tokens), 0)
    at = lax.broadcasted_iota(jnp.int32, (tokens, tokens), 1)
    t, j, row = to // rows, (to // rows_dev) % planes, to % rows_dev
    place = ((j % 2) * (planes // 2) + j // 2) * rows + t * rows_dev + row
    order = (at == place).astype(jnp.bfloat16)
    asked = [
        jnp.dot(order, q[...], preferred_element_type=jnp.float32).astype(jnp.bfloat16) for q in q_refs
    ]
    works = [
        (h, range(first, min(first + rows_step, len(targets))))
        for h in range(width // HEAD_DIM)
        for first in range(0, len(targets), rows_step)
    ]

    def taken(ref, count, h, which):
        cut = ref[: count * 2 * part, h * HEAD_DIM : (h + 1) * HEAD_DIM]
        return cut.reshape(count, 2, part, HEAD_DIM)[:, which].reshape(count * part, HEAD_DIM)

    def scores_of(work):
        h, block = work
        lanes = slice(h * HEAD_DIM, (h + 1) * HEAD_DIM)
        query = jnp.concatenate(
            [q[targets[i] * rows : (targets[i] + 1) * rows, lanes] for i in block for q in asked], axis=0
        )
        return [
            lax.dot_general(
                query,
                taken(kv, count, h, 0),
                (((1,), (1,)), ((), ())),
                preferred_element_type=jnp.float32,
            )
            for kv, count in zip(kv_refs, blocks)
        ]

    def finish(work, scores):
        h, block = work
        peak = functools.reduce(jnp.maximum, [jnp.max(s, axis=1, keepdims=True) for s in scores])
        peak = peak * EXP2_SCALE
        summed = None
        for s, kv, count in zip(scores, kv_refs, blocks):
            weights = jnp.exp2(s * EXP2_SCALE - peak).astype(jnp.bfloat16)
            value = taken(kv, count, h, 1)
            value = jnp.concatenate([value, jnp.ones_like(value)], axis=1)
            product = jnp.dot(weights, value, preferred_element_type=jnp.float32)
            summed = product if summed is None else summed + product
        out = (summed[:, :HEAD_DIM] / summed[:, HEAD_DIM:]).astype(jnp.bfloat16)
        for n, i in enumerate(block):
            for r in range(sources):
                first = (n * sources + r) * rows
                o_refs[i][targets[i] ^ r, :, h * HEAD_DIM : (h + 1) * HEAD_DIM] = out[first : first + rows]

    scores = scores_of(works[0])
    for n, work in enumerate(works):
        following = scores_of(works[n + 1]) if n + 1 < len(works) else None
        finish(work, scores)
        scores = following


def attend(queries, keys_values, targets, planes):
    sources = len(queries)
    tokens, width = queries[0].shape
    rows = tokens // sources
    blocks = [kv.shape[0] // (2 * tokens) for kv in keys_values]
    key_count = sum(blocks) * tokens
    small = key_count <= 4096
    rows_step, step_width = (2, width) if small else (1, HEAD_DIM)
    score_bytes = rows_step * tokens * key_count * 4
    limit = 8 * key_count * step_width + 3 * score_bytes + 6 * 1024 * 1024
    return pl.pallas_call(
        functools.partial(
            attend_kernel,
            sources=sources,
            planes=planes,
            blocks=blocks,
            part=tokens,
            targets=targets,
            rows_step=rows_step,
        ),
        grid=(width // step_width,),
        in_specs=[pl.BlockSpec((tokens, step_width), lambda h: (0, h))] * sources
        + [pl.BlockSpec((kv.shape[0], step_width), lambda h: (0, h)) for kv in keys_values],
        out_specs=[pl.BlockSpec((sources, rows, step_width), lambda h: (0, 0, h))] * len(targets),
        out_shape=[jax.ShapeDtypeStruct((sources, rows, width), jnp.bfloat16)] * len(targets),
        compiler_params=pltpu.CompilerParams(vmem_limit_bytes=min(limit, 60 * 1024 * 1024)),
    )(*queries, *keys_values)


def projection_of(o_refs, w_refs, lined):
    tokens, width = lined.shape[0], o_refs[0].shape[2]
    for n, o_ref in enumerate(o_refs):
        lined[:, n * width : (n + 1) * width] = o_ref[...].reshape(tokens, width)
    weights = jnp.concatenate([w[...] for w in w_refs], axis=0)
    return jnp.dot(lined[...], weights, preferred_element_type=jnp.float32)


def projection_specs(attended, targets, tile):
    o_spec = pl.BlockSpec(attended[0].shape, lambda i, *_: (0, 0, 0))
    width = attended[0].shape[2]
    return [o_spec] * len(targets) + [
        pl.BlockSpec((width, tile), lambda i, where, t=t: (where[0] ^ t, i)) for t in targets
    ]


def project_kernel(where_ref, *refs, targets):
    count = len(targets)
    out_ref, lined = refs[2 * count :]
    out_ref[...] = projection_of(refs[:count], refs[count : 2 * count], lined)


def project(where, attended, targets, w_out, tile):
    sources, rows, width = attended[0].shape
    tokens = sources * rows
    features = w_out.shape[1]
    return pl.pallas_call(
        functools.partial(project_kernel, targets=targets),
        grid_spec=pltpu.PrefetchScalarGridSpec(
            num_scalar_prefetch=1,
            grid=(features // tile,),
            in_specs=projection_specs(attended, targets, tile),
            out_specs=pl.BlockSpec((None, tokens, tile), lambda i, *_: (i, 0, 0)),
            scratch_shapes=[pltpu.VMEM((tokens, len(targets) * width), jnp.bfloat16)],
        ),
        out_shape=jax.ShapeDtypeStruct((features // tile, tokens, tile), jnp.float32),
        compiler_params=pltpu.CompilerParams(vmem_limit_bytes=VMEM_LIMIT),
    )(where, *attended, *[w_out] * len(targets))


def final_kernel(where_ref, *refs, targets, planes, rows_dev):
    count = len(targets)
    partial_ref, scale_ref, shift_ref, w_final_ref, inner_ref, outer_ref, lined, projected = refs[2 * count :]
    step = pl.program_id(0)
    heads_at, plane_at = where_ref[0], where_ref[1]
    tokens = lined.shape[0]
    tile = partial_ref.shape[1]
    projected[step] = partial_ref[...] + projection_of(refs[:count], refs[count : 2 * count], lined)

    @pl.when(step == pl.num_programs(0) - 1)
    def _():
        steps = projected.shape[0]
        features = steps * tile
        total = projected[0]
        for i in range(1, steps):
            total = total + projected[i]
        mean = jnp.sum(total, axis=1, keepdims=True) * (1.0 / features)
        squares = None
        for i in range(steps):
            centered = projected[i] - mean
            squares = centered * centered if squares is None else squares + centered * centered
        variance = jnp.sum(squares, axis=1, keepdims=True) * (1.0 / features)
        inverse = lax.rsqrt(variance + 1e-06)
        patches = None
        for i in range(steps):
            lanes = slice(i * tile, (i + 1) * tile)
            normed = (projected[i] - mean) * inverse * (1.0 + scale_ref[:, lanes]) + shift_ref[:, lanes]
            part = lax.dot_general(
                normed.astype(jnp.bfloat16),
                w_final_ref[:, lanes],
                (((1,), (1,)), ((), ())),
                preferred_element_type=jnp.float32,
            )
            patches = part if patches is None else patches + part
        patches = patches.astype(jnp.bfloat16)
        channels = patches.shape[1]
        half = channels // 2
        source = lax.broadcasted_iota(jnp.int32, (channels, channels), 0)
        target = lax.broadcasted_iota(jnp.int32, (channels, channels), 1)
        q, p, c = target // half, (target // LATENT_CH) % 2, target % LATENT_CH
        lane_order = (source == 4 * c + 2 * p + q).astype(jnp.bfloat16)
        to = lax.broadcasted_iota(jnp.int32, (tokens, tokens), 0)
        at = lax.broadcasted_iota(jnp.int32, (tokens, tokens), 1)
        share = planes * rows_dev
        place = ((to // share) ^ heads_at) * share
        place = place + (((to % share) // rows_dev) ^ plane_at) * rows_dev + to % rows_dev
        row_order = (at == place).astype(jnp.bfloat16)
        cells = jnp.dot(patches, lane_order, preferred_element_type=jnp.float32)
        cells = jnp.dot(row_order, cells.astype(jnp.bfloat16), preferred_element_type=jnp.float32)
        first = plane_at % 2 == 0
        inner_ref[...] = jnp.where(first, cells[:, half:], cells[:, :half]).astype(jnp.bfloat16)
        outer_ref[...] = jnp.where(first, cells[:, :half], cells[:, half:]).astype(jnp.bfloat16)


def final_layer(where, attended, targets, partial, w_out, scale_mod, shift_mod, w_final, rows_dev, planes):
    sources, rows, width = attended[0].shape
    features = w_out.shape[1]
    steps, tokens, tile = partial.shape
    channels = w_final.shape[1]
    whole = lambda shape: pl.BlockSpec(shape, lambda i, *_: (0,) * len(shape))
    result = jax.ShapeDtypeStruct((tokens, channels // 2), jnp.bfloat16)
    return pl.pallas_call(
        functools.partial(final_kernel, targets=targets, planes=planes, rows_dev=rows_dev),
        grid_spec=pltpu.PrefetchScalarGridSpec(
            num_scalar_prefetch=1,
            grid=(steps,),
            in_specs=projection_specs(attended, targets, tile)
            + [
                pl.BlockSpec((None, tokens, tile), lambda i, *_: (i, 0, 0)),
                whole((1, features)),
                whole((1, features)),
                whole((channels, features)),
            ],
            out_specs=[whole((tokens, channels // 2))] * 2,
            scratch_shapes=[
                pltpu.VMEM((tokens, len(targets) * width), jnp.bfloat16),
                pltpu.VMEM((steps, tokens, tile), jnp.float32),
            ],
        ),
        out_shape=[result] * 2,
        compiler_params=pltpu.CompilerParams(vmem_limit_bytes=VMEM_LIMIT),
    )(where, *attended, *[w_out] * len(targets), partial, scale_mod[None], shift_mod[None], w_final.T)


def convolve_kernel(
    where_ref, inner_ref, outer_ref, inner_got_ref, outer_got_ref, w_ref, bias_ref, out_ref, latent
):
    frames, cols, _, ch = latent.shape
    rows = inner_ref.shape[0] // frames
    height = 2 * rows
    inner, outer, inner_got, outer_got = [
        ref[...].astype(jnp.float32) for ref in (inner_ref, outer_ref, inner_got_ref, outer_got_ref)
    ]
    first = where_ref[2] % 2 == 0
    even, odd = jnp.where(first, outer, inner), jnp.where(first, inner, outer)
    left = jnp.where(where_ref[2] == 0, even, jnp.where(first, outer_got, inner_got))
    right = jnp.where(where_ref[2] == where_ref[3] - 1, odd, jnp.where(first, inner_got, outer_got))
    for x, cells in enumerate((left, even, odd, right)):
        for f in range(frames):
            own = cells[f * rows : (f + 1) * rows]
            for p in range(2):
                latent[f, x, pl.ds(8 + p, rows, stride=2), :] = own[:, p * ch : (p + 1) * ch]
            latent[f, x, 7:8, :] = own[:1, :ch]
            latent[f, x, 8 + height : 9 + height, :] = own[rows - 1 :, ch:]
    depth = 9 * ch
    row_taps = [
        [
            jnp.concatenate([latent[f, x, 7 + e : 7 + e + height, :] for e in range(3)], axis=1).astype(
                jnp.bfloat16
            )
            for x in range(cols)
        ]
        for f in range(frames)
    ]
    for x in range(cols - 2):
        stacked = [jnp.concatenate(row_taps[f][x : x + 3], axis=1) for f in range(frames)]
        stacked = [stacked[0]] * 2 + stacked
        acc = None
        for a in range(3):
            flat = jnp.concatenate(stacked[a : a + frames], axis=0)
            part = jnp.dot(
                flat, w_ref[a * depth : (a + 1) * depth, :], preferred_element_type=jnp.float32
            )
            acc = part if acc is None else acc + part
        acc = (acc + bias_ref[...]).astype(jnp.bfloat16)
        out_ref[:, x] = acc.reshape(frames, height, acc.shape[1])


def convolve(where, inner, outer, inner_got, outer_got, conv_weight, conv_bias):
    rows = inner.shape[0] // FRAMES
    channels = conv_weight.shape[1]
    smem = pl.BlockSpec(memory_space=pltpu.SMEM)
    vmem = pl.BlockSpec(memory_space=pltpu.VMEM)
    return pl.pallas_call(
        convolve_kernel,
        in_specs=[smem] + [vmem] * 6,
        out_specs=vmem,
        out_shape=jax.ShapeDtypeStruct((FRAMES, 2, 2 * rows, channels), jnp.bfloat16),
        scratch_shapes=[pltpu.VMEM((FRAMES, 4, 2 * rows + 16, LATENT_CH), jnp.float32)],
        compiler_params=pltpu.CompilerParams(vmem_limit_bytes=VMEM_LIMIT),
    )(where, inner, outer, inner_got, outer_got, conv_weight, conv_bias[None])


def shards(queries, keys, values, w_out, shift_mod, scale_mod, w_final, conv_weight, conv_bias):
    groups = lax.axis_size("heads")
    planes = lax.axis_size("plane")
    heads_at = lax.axis_index("heads")
    plane_at = lax.axis_index("plane")
    devices = groups * planes
    tokens = queries.shape[0]
    rows_dev = tokens // devices
    where = jnp.stack(
        [heads_at, plane_at, heads_at * planes + plane_at, jnp.int32(devices)]
    ).astype(jnp.int32)

    made = bundles(where, queries, keys, values, groups, planes, range(groups))
    got = {r: swap(made[r], "heads", r) if r else made[r] for r in range(groups)}

    both_parts, share = 2 * tokens, tokens // planes
    held = {r: [got[r]] for r in range(groups)}
    for r in (0, 1, 2, 3):
        for d in range(2, planes, 2):
            asked = got[r][both_parts + d * share : both_parts + (d + 2) * share]
            held[r].append(swap(jnp.concatenate([got[r][:both_parts], asked], axis=0), "plane", d))

    keys_values, asked = [], {}
    for distances in ((0, 1), (2,), (3,)):
        passed = [h[:both_parts] for r in distances for h in held[r]]
        passed += [h[both_parts + share : both_parts + 2 * share] for r in distances for h in held[r]]
        mine = jnp.concatenate(passed, axis=0)
        other = swap(mine, "plane", 1)
        keys_values += [mine, other]
        half = planes // 2
        first = both_parts * half * len(distances)
        for n, r in enumerate(distances):
            start = first + n * half * share
            asked[r] = jnp.concatenate(
                [h[both_parts : both_parts + share] for h in held[r]]
                + [other[start : start + half * share]],
                axis=0,
            )
    asked = [asked[r] for r in range(groups)]

    near, far = (0, 3), (2, 1)
    results = {}
    for targets in ((3,), (2,), (1,), (0,)):
        for t, o in zip(targets, attend(asked, keys_values, targets, planes)):
            results[t] = o if t == 0 else swap(o, "heads", t)
    partial = project(where, [results[t] for t in near], near, w_out, 1536)
    sent = [results[t] for t in far]
    inner, outer = final_layer(
        where, sent, far, partial, w_out, scale_mod, shift_mod, w_final, rows_dev, planes
    )
    pairs = [(i, i + 1) for i in range(1, devices - 1, 2)]
    inner_got = swap(inner, "plane", 1)
    outer_got = lax.ppermute(outer, ("heads", "plane"), pairs + [(j, i) for i, j in pairs])
    return convolve(where, inner, outer, inner_got, outer_got, conv_weight, conv_bias)


def solution(mesh):
    groups, seq = mesh.devices.shape
    split = Mesh(
        mesh.devices.reshape(groups, HEAD_GROUPS, seq // HEAD_GROUPS), ("groups", "heads", "plane")
    )
    by_token = P(("groups", "heads", "plane"), None)
    placed = (by_token, by_token, by_token, P(), P("groups"), P("groups"), P(), P(), P())
    return jax.shard_map(
        shards,
        mesh=split,
        in_specs=placed,
        out_specs=P("groups", ("heads", "plane"), None, None),
        check_vma=False,
    )
```

```python
import functools
import math

import jax
import jax.numpy as jnp
from jax import lax
from jax.experimental import pallas as pl
from jax.experimental.pallas import tpu as pltpu
from jax.sharding import Mesh
from jax.sharding import PartitionSpec as P

HEAD_DIM = 128
HEAD_GROUPS = 4
LATENT_CH = 16
FRAMES = 4
VMEM_LIMIT = 16 * 1024 * 1024
EXP2_SCALE = math.log2(math.e) / math.sqrt(HEAD_DIM)


def swap(source, axis, distance):
    count = lax.axis_size(axis)
    return lax.ppermute(source, axis, [(i, i ^ distance) for i in range(count)])


def bundle_kernel(where_ref, qkv_ref, *out_refs, groups, planes, distances):
    tokens, width = qkv_ref.shape[0] // 3, qkv_ref.shape[1]
    group_width = width // groups
    rows_dev = tokens // (groups * planes)
    to = lax.broadcasted_iota(jnp.int32, (tokens, tokens), 0)
    at = lax.broadcasted_iota(jnp.int32, (tokens, tokens), 1)
    j, t, row = to // (groups * rows_dev), (to // rows_dev) % groups, to % rows_dev
    for r, out_ref in zip(distances, out_refs):
        group = where_ref[0] ^ r
        lanes = pl.ds(pl.multiple_of(group * group_width, 128), group_width)
        place = row * (groups * planes) + (t ^ group) * planes + (j ^ where_ref[1])
        order = (at == place).astype(jnp.bfloat16)
        out_ref[: 2 * tokens] = qkv_ref[tokens:, lanes]
        mixed = jnp.dot(order, qkv_ref[:tokens, lanes], preferred_element_type=jnp.float32)
        out_ref[2 * tokens :] = mixed.astype(jnp.bfloat16)


def bundles(where, queries, keys, values, groups, planes, distances):
    tokens, width = queries.shape
    vmem = pl.BlockSpec(memory_space=pltpu.VMEM)
    result = jax.ShapeDtypeStruct((3 * tokens, width // groups), jnp.bfloat16)
    return pl.pallas_call(
        functools.partial(bundle_kernel, groups=groups, planes=planes, distances=distances),
        in_specs=[pl.BlockSpec(memory_space=pltpu.SMEM), vmem],
        out_specs=[vmem] * len(distances),
        out_shape=[result] * len(distances),
        compiler_params=pltpu.CompilerParams(vmem_limit_bytes=VMEM_LIMIT),
    )(where, jnp.concatenate([queries, keys, values], axis=0))


def after(value, *others):
    return lax.optimization_barrier((value,) + others)[0]


def attend_kernel(*refs, sources, planes, blocks, part, targets, rows_step):
    q_refs = refs[:sources]
    kv_refs = refs[sources : sources + len(blocks)]
    o_refs = refs[sources + len(blocks) :]
    tokens, width = q_refs[0].shape
    rows = tokens // sources
    rows_dev = rows // planes
    to = lax.broadcasted_iota(jnp.int32, (tokens, tokens), 0)
    at = lax.broadcasted_iota(jnp.int32, (tokens, tokens), 1)
    t, j, row = to // rows, (to // rows_dev) % planes, to % rows_dev
    place = ((j % 2) * (planes // 2) + j // 2) * rows + t * rows_dev + row
    order = (at == place).astype(jnp.bfloat16)
    asked = [
        jnp.dot(order, q[...], preferred_element_type=jnp.float32).astype(jnp.bfloat16) for q in q_refs
    ]
    works = [
        (h, range(first, min(first + rows_step, len(targets))))
        for h in range(width // HEAD_DIM)
        for first in range(0, len(targets), rows_step)
    ]

    def taken(ref, count, h, which):
        cut = ref[: count * 2 * part, h * HEAD_DIM : (h + 1) * HEAD_DIM]
        return cut.reshape(count, 2, part, HEAD_DIM)[:, which].reshape(count * part, HEAD_DIM)

    def scores_of(work):
        h, block = work
        lanes = slice(h * HEAD_DIM, (h + 1) * HEAD_DIM)
        query = jnp.concatenate(
            [q[targets[i] * rows : (targets[i] + 1) * rows, lanes] for i in block for q in asked], axis=0
        )
        return [
            lax.dot_general(
                query,
                taken(kv, count, h, 0),
                (((1,), (1,)), ((), ())),
                preferred_element_type=jnp.float32,
            )
            for kv, count in zip(kv_refs, blocks)
        ]

    def finish(work, scores):
        h, block = work
        peak = functools.reduce(jnp.maximum, [jnp.max(s, axis=1, keepdims=True) for s in scores])
        peak = peak * EXP2_SCALE
        summed = None
        for s, kv, count in zip(scores, kv_refs, blocks):
            weights = jnp.exp2(s * EXP2_SCALE - peak).astype(jnp.bfloat16)
            value = taken(kv, count, h, 1)
            value = jnp.concatenate([value, jnp.ones_like(value)], axis=1)
            product = jnp.dot(weights, value, preferred_element_type=jnp.float32)
            summed = product if summed is None else summed + product
        out = (summed[:, :HEAD_DIM] / summed[:, HEAD_DIM:]).astype(jnp.bfloat16)
        for n, i in enumerate(block):
            for r in range(sources):
                first = (n * sources + r) * rows
                o_refs[i][targets[i] ^ r, :, h * HEAD_DIM : (h + 1) * HEAD_DIM] = out[first : first + rows]

    scores = scores_of(works[0])
    for n, work in enumerate(works):
        following = scores_of(works[n + 1]) if n + 1 < len(works) else None
        finish(work, scores)
        scores = following


def attend(queries, keys_values, targets, planes):
    sources = len(queries)
    tokens, width = queries[0].shape
    rows = tokens // sources
    blocks = [kv.shape[0] // (2 * tokens) for kv in keys_values]
    key_count = sum(blocks) * tokens
    small = key_count <= 4096
    rows_step, step_width = (2, width) if small else (1, HEAD_DIM)
    score_bytes = rows_step * tokens * key_count * 4
    limit = 8 * key_count * step_width + 3 * score_bytes + 6 * 1024 * 1024
    return pl.pallas_call(
        functools.partial(
            attend_kernel,
            sources=sources,
            planes=planes,
            blocks=blocks,
            part=tokens,
            targets=targets,
            rows_step=rows_step,
        ),
        grid=(width // step_width,),
        in_specs=[pl.BlockSpec((tokens, step_width), lambda h: (0, h))] * sources
        + [pl.BlockSpec((kv.shape[0], step_width), lambda h: (0, h)) for kv in keys_values],
        out_specs=[pl.BlockSpec((sources, rows, step_width), lambda h: (0, 0, h))] * len(targets),
        out_shape=[jax.ShapeDtypeStruct((sources, rows, width), jnp.bfloat16)] * len(targets),
        compiler_params=pltpu.CompilerParams(vmem_limit_bytes=min(limit, 60 * 1024 * 1024)),
    )(*queries, *keys_values)


def projection_of(o_refs, w_refs, lined):
    tokens, width = lined.shape[0], o_refs[0].shape[2]
    for n, o_ref in enumerate(o_refs):
        lined[:, n * width : (n + 1) * width] = o_ref[...].reshape(tokens, width)
    weights = jnp.concatenate([w[...] for w in w_refs], axis=0)
    return jnp.dot(lined[...], weights, preferred_element_type=jnp.float32)


def projection_specs(attended, targets, tile):
    o_spec = pl.BlockSpec(attended[0].shape, lambda i, *_: (0, 0, 0))
    width = attended[0].shape[2]
    return [o_spec] * len(targets) + [
        pl.BlockSpec((width, tile), lambda i, where, t=t: (where[0] ^ t, i)) for t in targets
    ]


def project_kernel(where_ref, *refs, targets):
    count = len(targets)
    out_ref, lined = refs[2 * count :]
    out_ref[...] = projection_of(refs[:count], refs[count : 2 * count], lined)


def project(where, attended, targets, w_out, tile):
    sources, rows, width = attended[0].shape
    tokens = sources * rows
    features = w_out.shape[1]
    return pl.pallas_call(
        functools.partial(project_kernel, targets=targets),
        grid_spec=pltpu.PrefetchScalarGridSpec(
            num_scalar_prefetch=1,
            grid=(features // tile,),
            in_specs=projection_specs(attended, targets, tile),
            out_specs=pl.BlockSpec((None, tokens, tile), lambda i, *_: (i, 0, 0)),
            scratch_shapes=[pltpu.VMEM((tokens, len(targets) * width), jnp.bfloat16)],
        ),
        out_shape=jax.ShapeDtypeStruct((features // tile, tokens, tile), jnp.float32),
        compiler_params=pltpu.CompilerParams(vmem_limit_bytes=VMEM_LIMIT),
    )(where, *attended, *[w_out] * len(targets))


def final_kernel(where_ref, *refs, targets, planes, rows_dev):
    count = len(targets)
    partial_ref, scale_ref, shift_ref, w_final_ref, inner_ref, outer_ref, lined, projected = refs[2 * count :]
    step = pl.program_id(0)
    heads_at, plane_at = where_ref[0], where_ref[1]
    tokens = lined.shape[0]
    tile = partial_ref.shape[1]
    projected[step] = partial_ref[...] + projection_of(refs[:count], refs[count : 2 * count], lined)

    @pl.when(step == pl.num_programs(0) - 1)
    def _():
        steps = projected.shape[0]
        features = steps * tile
        total = projected[0]
        for i in range(1, steps):
            total = total + projected[i]
        mean = jnp.sum(total, axis=1, keepdims=True) * (1.0 / features)
        squares = None
        for i in range(steps):
            centered = projected[i] - mean
            squares = centered * centered if squares is None else squares + centered * centered
        variance = jnp.sum(squares, axis=1, keepdims=True) * (1.0 / features)
        inverse = lax.rsqrt(variance + 1e-06)
        patches = None
        for i in range(steps):
            lanes = slice(i * tile, (i + 1) * tile)
            normed = (projected[i] - mean) * inverse * (1.0 + scale_ref[:, lanes]) + shift_ref[:, lanes]
            part = lax.dot_general(
                normed.astype(jnp.bfloat16),
                w_final_ref[:, lanes],
                (((1,), (1,)), ((), ())),
                preferred_element_type=jnp.float32,
            )
            patches = part if patches is None else patches + part
        patches = patches.astype(jnp.bfloat16)
        channels = patches.shape[1]
        half = channels // 2
        source = lax.broadcasted_iota(jnp.int32, (channels, channels), 0)
        target = lax.broadcasted_iota(jnp.int32, (channels, channels), 1)
        q, p, c = target // half, (target // LATENT_CH) % 2, target % LATENT_CH
        lane_order = (source == 4 * c + 2 * p + q).astype(jnp.bfloat16)
        to = lax.broadcasted_iota(jnp.int32, (tokens, tokens), 0)
        at = lax.broadcasted_iota(jnp.int32, (tokens, tokens), 1)
        share = planes * rows_dev
        place = ((to // share) ^ heads_at) * share
        place = place + (((to % share) // rows_dev) ^ plane_at) * rows_dev + to % rows_dev
        row_order = (at == place).astype(jnp.bfloat16)
        cells = jnp.dot(patches, lane_order, preferred_element_type=jnp.float32)
        cells = jnp.dot(row_order, cells.astype(jnp.bfloat16), preferred_element_type=jnp.float32)
        first = plane_at % 2 == 0
        inner_ref[...] = jnp.where(first, cells[:, half:], cells[:, :half]).astype(jnp.bfloat16)
        outer_ref[...] = jnp.where(first, cells[:, :half], cells[:, half:]).astype(jnp.bfloat16)


def final_layer(where, attended, targets, partial, w_out, scale_mod, shift_mod, w_final, rows_dev, planes):
    sources, rows, width = attended[0].shape
    features = w_out.shape[1]
    steps, tokens, tile = partial.shape
    channels = w_final.shape[1]
    whole = lambda shape: pl.BlockSpec(shape, lambda i, *_: (0,) * len(shape))
    result = jax.ShapeDtypeStruct((tokens, channels // 2), jnp.bfloat16)
    return pl.pallas_call(
        functools.partial(final_kernel, targets=targets, planes=planes, rows_dev=rows_dev),
        grid_spec=pltpu.PrefetchScalarGridSpec(
            num_scalar_prefetch=1,
            grid=(steps,),
            in_specs=projection_specs(attended, targets, tile)
            + [
                pl.BlockSpec((None, tokens, tile), lambda i, *_: (i, 0, 0)),
                whole((1, features)),
                whole((1, features)),
                whole((channels, features)),
            ],
            out_specs=[whole((tokens, channels // 2))] * 2,
            scratch_shapes=[
                pltpu.VMEM((tokens, len(targets) * width), jnp.bfloat16),
                pltpu.VMEM((steps, tokens, tile), jnp.float32),
            ],
        ),
        out_shape=[result] * 2,
        compiler_params=pltpu.CompilerParams(vmem_limit_bytes=VMEM_LIMIT),
    )(where, *attended, *[w_out] * len(targets), partial, scale_mod[None], shift_mod[None], w_final.T)


def convolve_kernel(
    where_ref, inner_ref, outer_ref, outer_got_ref, inner_got_ref, w_ref, bias_ref, out_ref, latent
):
    frames, cols, _, ch = latent.shape
    rows = inner_ref.shape[0] // frames
    height = 2 * rows
    inner, outer, inner_got, outer_got = [
        ref[...].astype(jnp.float32) for ref in (inner_ref, outer_ref, inner_got_ref, outer_got_ref)
    ]
    first = where_ref[2] % 2 == 0
    even, odd = jnp.where(first, outer, inner), jnp.where(first, inner, outer)
    left = jnp.where(where_ref[2] == 0, even, jnp.where(first, outer_got, inner_got))
    right = jnp.where(where_ref[2] == where_ref[3] - 1, odd, jnp.where(first, inner_got, outer_got))
    for x, cells in enumerate((left, even, odd, right)):
        for f in range(frames):
            own = cells[f * rows : (f + 1) * rows]
            for p in range(2):
                latent[f, x, pl.ds(8 + p, rows, stride=2), :] = own[:, p * ch : (p + 1) * ch]
            latent[f, x, 7:8, :] = own[:1, :ch]
            latent[f, x, 8 + height : 9 + height, :] = own[rows - 1 :, ch:]
    depth = 9 * ch
    for x in range(cols - 2):
        stacked = []
        for f in range(frames):
            taps = [latent[f, x + b, 7 + e : 7 + e + height, :] for b in range(3) for e in range(3)]
            stacked.append(jnp.concatenate(taps, axis=1).astype(jnp.bfloat16))
        stacked = [stacked[0]] * 2 + stacked
        acc = None
        for a in range(3):
            flat = jnp.concatenate(stacked[a : a + frames], axis=0)
            part = jnp.dot(
                flat, w_ref[a * depth : (a + 1) * depth, :], preferred_element_type=jnp.float32
            )
            acc = part if acc is None else acc + part
        acc = (acc + bias_ref[...]).astype(jnp.bfloat16)
        out_ref[:, x] = acc.reshape(frames, height, acc.shape[1])


def convolve(where, inner, outer, inner_got, outer_got, conv_weight, conv_bias):
    rows = inner.shape[0] // FRAMES
    channels = conv_weight.shape[1]
    smem = pl.BlockSpec(memory_space=pltpu.SMEM)
    vmem = pl.BlockSpec(memory_space=pltpu.VMEM)
    return pl.pallas_call(
        convolve_kernel,
        in_specs=[smem] + [vmem] * 6,
        out_specs=vmem,
        out_shape=jax.ShapeDtypeStruct((FRAMES, 2, 2 * rows, channels), jnp.bfloat16),
        scratch_shapes=[pltpu.VMEM((FRAMES, 4, 2 * rows + 16, LATENT_CH), jnp.float32)],
        compiler_params=pltpu.CompilerParams(vmem_limit_bytes=VMEM_LIMIT),
    )(where, inner, outer, outer_got, inner_got, conv_weight, conv_bias[None])


def shards(queries, keys, values, w_out, shift_mod, scale_mod, w_final, conv_weight, conv_bias):
    groups = lax.axis_size("heads")
    planes = lax.axis_size("plane")
    heads_at = lax.axis_index("heads")
    plane_at = lax.axis_index("plane")
    devices = groups * planes
    tokens = queries.shape[0]
    rows_dev = tokens // devices
    where = jnp.stack(
        [heads_at, plane_at, heads_at * planes + plane_at, jnp.int32(devices)]
    ).astype(jnp.int32)

    made = bundles(where, queries, keys, values, groups, planes, range(groups))
    got = {r: swap(made[r], "heads", r) if r else made[r] for r in range(groups)}

    both_parts, share = 2 * tokens, tokens // planes
    held = {r: [got[r]] for r in range(groups)}
    for r in (0, 1, 2, 3):
        for d in range(2, planes, 2):
            asked = got[r][both_parts + d * share : both_parts + (d + 2) * share]
            held[r].append(swap(jnp.concatenate([got[r][:both_parts], asked], axis=0), "plane", d))

    keys_values, asked = [], {}
    for distances in ((0, 1), (2,), (3,)):
        passed = [h[:both_parts] for r in distances for h in held[r]]
        passed += [h[both_parts + share : both_parts + 2 * share] for r in distances for h in held[r]]
        mine = jnp.concatenate(passed, axis=0)
        other = swap(mine, "plane", 1)
        keys_values += [mine, other]
        half = planes // 2
        first = both_parts * half * len(distances)
        for n, r in enumerate(distances):
            start = first + n * half * share
            asked[r] = jnp.concatenate(
                [h[both_parts : both_parts + share] for h in held[r]]
                + [other[start : start + half * share]],
                axis=0,
            )
    asked = [asked[r] for r in range(groups)]

    near, far = (0, 3), (2, 1)
    results = {}
    for targets in ((3,), (2,), (1,), (0,)):
        for t, o in zip(targets, attend(asked, keys_values, targets, planes)):
            results[t] = o if t == 0 else swap(o, "heads", t)
    partial = project(where, [results[t] for t in near], near, w_out, 1536)
    sent = [results[t] for t in far]
    inner, outer = final_layer(
        where, sent, far, partial, w_out, scale_mod, shift_mod, w_final, rows_dev, planes
    )
    pairs = [(i, i + 1) for i in range(1, devices - 1, 2)]
    inner_got = swap(inner, "plane", 1)
    outer_got = lax.ppermute(outer, ("heads", "plane"), pairs + [(j, i) for i, j in pairs])
    return convolve(where, inner, outer, inner_got, outer_got, conv_weight, conv_bias)


def solution(mesh):
    groups, seq = mesh.devices.shape
    split = Mesh(
        mesh.devices.reshape(groups, HEAD_GROUPS, seq // HEAD_GROUPS), ("groups", "heads", "plane")
    )
    by_token = P(("groups", "heads", "plane"), None)
    placed = (by_token, by_token, by_token, P(), P("groups"), P("groups"), P(), P(), P())
    return jax.shard_map(
        shards,
        mesh=split,
        in_specs=placed,
        out_specs=P("groups", ("heads", "plane"), None, None),
        check_vma=False,
    )
```
